32 devices in a mesh: dp: 4 (over z), member: 8 (over y, x, core).
Axes of the slice: x: 2, y: 2, z: 4, core: 2. Of those that a mesh axis runs over, the one named last changes fastest.
Arguments:
- objects: bfloat16 [16384, 512], P(('dp', 'member'))
- counts: int32 [32], P(('dp', 'member')), may hold values from 1 to 512, as said below
- cotangent: float32 [16384], P(('dp', 'member')), may hold values from -6 to 6
- matrix: float32 [512, 512], P(('dp', 'member'))
- matrix_first: float32 [512, 512], P(('dp', 'member'))
- matrix_second: float32 [512, 512], P(('dp', 'member')), may hold values from 16 to 64
- adapters: float32 [3, 32, 512], P(None, None, ('dp', 'member'))
- adapter_first: float32 [3, 32, 512], P(None, None, ('dp', 'member'))
- adapter_second: float32 [3, 32, 512], P(None, None, ('dp', 'member')), may hold values from 0.125 to 0.5
- head_weights: float32 [32, 512], P('member')
- head_first: float32 [32, 512], P('member')
- head_second: float32 [32, 512], P('member'), may hold values from 4 to 16
Outputs:
- predictions: float32 [16384], P(('dp', 'member'))
- input_grad: float32 [16384, 512], P(('dp', 'member'))
- new_matrix: float32 [512, 512], P(('dp', 'member'))
- new_matrix_first: float32 [512, 512], P(('dp', 'member'))
- new_matrix_second: float32 [512, 512], P(('dp', 'member'))
- new_adapters: float32 [3, 32, 512], P(None, None, ('dp', 'member'))
- new_adapter_first: float32 [3, 32, 512], P(None, None, ('dp', 'member'))
- new_adapter_second: float32 [3, 32, 512], P(None, None, ('dp', 'member'))
- new_heads: float32 [32, 512], P('member')
- new_head_first: float32 [32, 512], P('member')
- new_head_second: float32 [32, 512], P('member')
- norm_pairs: float32 [5, 2], replicated
The draws below stay inside these ranges and needn't reach their ends.
Inputs may be any that keep to these rules, and one draw needn't show every extreme that they name: `counts`: the last device's count is always the full 512.
All inputs are finite; a program needn't handle non-finite values.
Results may differ from the reference program's by a relative error of at most 0.0095.
Values may be sent and summed in bfloat16 or wider, within the bound.
No kernel may reach another device: no remote copies, remote signals or barrier semaphores. Data moves between devices by JAX's collectives and lax.ppermute only.
A program may use at most 192 MiB of HBM per device.

```python
import math
import jax
import jax.numpy as jnp
from jax import lax

D = 512
K = 32
OBJ_DEV = 512
STEP = 10
TOTAL = 16384
N_DP = 4
N_MEMBER = 8


def rising(count, top):
    return 1.0 + (top - 1.0) * jnp.arange(count, dtype=jnp.float32) / max(count - 1, 1)


def draw_objects(key, part):
    key = jax.random.fold_in(key, 11)
    base_draw = jax.random.normal(key, (TOTAL, D), jnp.float32)
    return (base_draw * rising(D, 3.0)[None, :]).astype(jnp.bfloat16)


def draw_counts(key, part):
    key = jax.random.fold_in(key, 12)
    places = N_DP * N_MEMBER
    device_index = jnp.arange(places, dtype=jnp.int32)
    floor_count = OBJ_DEV // 3
    base_count = floor_count + (OBJ_DEV - floor_count) * device_index // (places - 1)
    jitter = jax.random.randint(key, (places,), 0, OBJ_DEV // 4 + 1, dtype=jnp.int32)
    drawn = jnp.maximum(base_count - jitter, 1)
    return drawn.at[places - 1].set(OBJ_DEV)


def draw_matrix(key, part):
    key = jax.random.fold_in(key, 13)
    base_draw = jax.random.normal(key, (D, D), jnp.float32)
    return base_draw * rising(D, 3.0)[:, None] * (0.2 / D ** 0.5)


def draw_adapters(key, part):
    key = jax.random.fold_in(key, 14)
    key_list = jax.random.split(key, 5)
    sign_in = jax.random.rademacher(key_list[0], (K, D)).astype(jnp.float32)
    sign_out = jax.random.rademacher(key_list[1], (K, D)).astype(jnp.float32)
    size_in = jnp.exp(jax.random.uniform(key_list[2], (K, D), jnp.float32, -0.35, 0.35))
    size_out = jnp.exp(jax.random.uniform(key_list[3], (K, D), jnp.float32, -0.35, 0.35))
    shift_draw = 0.5 * jax.random.normal(key_list[4], (K, D), jnp.float32)
    member_rise = 0.6 * rising(K, 3.0)[:, None]
    return jnp.stack([sign_in * size_in, sign_out * size_out * member_rise, shift_draw])


def draw_head_weights(key, part):
    key = jax.random.fold_in(key, 15)
    base_draw = jax.random.normal(key, (K, D), jnp.float32)
    return base_draw * rising(K, 3.0)[:, None] * (2.0 / D ** 0.5)


def moment_draw(key, shape, rise):
    return jax.random.normal(key, shape, jnp.float32) * rise * 0.5


def draw_matrix_first(key, part):
    key = jax.random.fold_in(key, 16)
    top = 3.0
    scale = 4.0 * (TOTAL * K) ** 0.5 / (K * D ** 0.5)
    return moment_draw(key, (D, D), rising(D, top)[:, None]) * scale


def draw_adapter_first(key, part):
    key = jax.random.fold_in(key, 17)
    top = 3.0
    scale = 2.0 * TOTAL ** 0.5 / (K * D ** 0.5)
    return moment_draw(key, (3, K, D), rising(D, top)[None, None, :]) * scale


def draw_head_first(key, part):
    key = jax.random.fold_in(key, 18)
    top = 3.0
    scale = 0.5 * TOTAL ** 0.5 / K
    return moment_draw(key, (K, D), rising(K, top)[:, None]) * scale


def block_scale(own_key, extent, cuts, low, high):
    level, own = 1.0, jax.random.fold_in(own_key, 6)
    for position, shards_of in cuts:
        draws = jnp.exp(jax.random.uniform(jax.random.fold_in(own, position), (shards_of,), jnp.float32, low / len(cuts), high / len(cuts)))
        level = level * jnp.repeat(draws, extent[position] // shards_of).reshape([-1 if axis == position else 1 for axis in range(len(extent))])
    return level


def bell_draw(own_key, shape, deviation, limit, pieces=(), kind=jnp.bfloat16):
    entries = deviation * jax.random.normal(own_key, shape, jnp.float32)
    if pieces:
        entries = entries * block_scale(own_key, shape, pieces, -0.22, 0.18)
    return jnp.clip(entries, -limit, limit).astype(kind)


def setup_inputs(seed: int = 0) -> dict:
    streams_of = jax.random.split(jax.random.key(seed), 13)
    return {
        "objects": draw_objects(jax.random.fold_in(streams_of[12], 71), 0),
        "counts": draw_counts(jax.random.fold_in(streams_of[12], 71), 0),
        "cotangent": bell_draw(streams_of[2], (TOTAL,), 1.0, 6.0, ((0, 32),), jnp.float32),
        "matrix": draw_matrix(jax.random.fold_in(streams_of[12], 71), 0),
        "matrix_first": draw_matrix_first(jax.random.fold_in(streams_of[12], 71), 0),
        "matrix_second": jnp.clip(jnp.exp(math.log(64.0) - 1.3862944 * jax.random.uniform(streams_of[5], (D, D), jnp.float32) ** block_scale(streams_of[5], (D, D), ((0, 32),), -0.2, 0.2)), 16.0, 64.0),
        "adapters": draw_adapters(jax.random.fold_in(streams_of[12], 71), 0),
        "adapter_first": draw_adapter_first(jax.random.fold_in(streams_of[12], 71), 0),
        "adapter_second": jnp.clip(jnp.exp(math.log(0.5) - 1.3862944 * jax.random.uniform(streams_of[8], (3, K, D), jnp.float32) ** block_scale(streams_of[8], (3, K, D), ((2, 32),), -0.2, 0.2)), 0.125, 0.5),
        "head_weights": draw_head_weights(jax.random.fold_in(streams_of[12], 71), 0),
        "head_first": draw_head_first(jax.random.fold_in(streams_of[12], 71), 0),
        "head_second": jnp.clip(jnp.exp(math.log(16.0) - 1.3862944 * jax.random.uniform(streams_of[11], (K, D), jnp.float32) ** block_scale(streams_of[11], (K, D), ((0, 8),), -0.2, 0.2)), 4.0, 16.0),
    }


beta_one = 0.5
beta_two = 0.5
epsilon = 1e-06
weight_decay = 0.01
learn_rate = 0.25

@jax.custom_vjp
def low(v):
    return lax.optimization_barrier(v.astype(jnp.bfloat16)).astype(jnp.float32)

@jax.custom_vjp
def low_back(v):
    return v

def low_keep(v):
    return (low(v), None)

def low_pass(kept, grad):
    return (grad,)

def back_keep(v):
    return (v, None)

def back_low(kept, grad):
    return (low(grad),)
low.defvjp(low_keep, low_pass)
low_back.defvjp(back_keep, back_low)

def forward(inputs, matrix, adapters, head_weights, valid_rows):
    matrix_low = low(matrix)
    adapt_low = low(adapters)
    heads_low = low(head_weights)
    scale_in = adapt_low[0]
    scale_out = adapt_low[1]
    shift_vec = adapt_low[2]
    block_count = inputs.shape[0] // OBJ_DEV

    def one_block(block_pair):
        rows_in, keep_rows = block_pair
        mixed_rows = low(rows_in[:, None, :] * scale_in[None])
        inner_sum = low_back(jnp.einsum('ckd,de->cke', mixed_rows, matrix_low, precision=lax.Precision.HIGHEST))
        active = low(low_back(jax.nn.silu(inner_sum * scale_out[None] + shift_vec[None])))
        return keep_rows * jnp.einsum('ckd,kd->c', active, heads_low, precision=lax.Precision.HIGHEST) / K
    block_preds = lax.map(jax.checkpoint(one_block), (inputs.reshape(block_count, OBJ_DEV, D), valid_rows.reshape(block_count, OBJ_DEV)))
    return block_preds.reshape(-1)

def direction(weight, first_old, second_old, gradient):
    first_new = beta_one * first_old + (1.0 - beta_one) * gradient
    second_new = beta_two * second_old + (1.0 - beta_two) * gradient * gradient
    fix_one = 1.0 - beta_one ** STEP
    fix_two = 1.0 - beta_two ** STEP
    update = first_new / fix_one / (jnp.sqrt(second_new / fix_two) + epsilon) + weight_decay * weight
    return (first_new, second_new, update)

def reference(objects, counts, cotangent, matrix, matrix_first, matrix_second, adapters, adapter_first, adapter_second, head_weights, head_first, head_second):
    slot_index = jnp.arange(OBJ_DEV, dtype=jnp.int32)
    valid_rows = (slot_index[None, :] < counts[:, None]).astype(jnp.float32).reshape(-1)
    inputs = objects.astype(jnp.float32)
    predictions, pullback = jax.vjp(lambda a, b, c, d: forward(a, b, c, d, valid_rows), inputs, matrix, adapters, head_weights)
    input_grad, grad_matrix, grad_adapt, grad_heads = pullback(cotangent)
    m_first, m_second, m_update = direction(matrix, matrix_first, matrix_second, grad_matrix)
    a_first, a_second, a_update = direction(adapters, adapter_first, adapter_second, grad_adapt)
    h_first, h_second, h_update = direction(head_weights, head_first, head_second, grad_heads)
    weight_sq = jnp.concatenate([jnp.sum(matrix * matrix)[None], lax.optimization_barrier(jnp.sum(adapters * adapters, axis=(1, 2))), jnp.sum(head_weights * head_weights)[None]])
    update_sq = jnp.concatenate([jnp.sum(m_update * m_update)[None], lax.optimization_barrier(jnp.sum(a_update * a_update, axis=(1, 2))), jnp.sum(h_update * h_update)[None]])
    weight_norm = jnp.sqrt(weight_sq)
    update_norm = jnp.sqrt(update_sq)
    trust_ratio = weight_norm / update_norm
    new_matrix = matrix - learn_rate * trust_ratio[0] * m_update
    new_adapters = adapters - learn_rate * trust_ratio[1:4][:, None, None] * a_update
    new_heads = head_weights - learn_rate * trust_ratio[4] * h_update
    norm_pairs = jnp.stack([weight_norm, update_norm], axis=1)
    return (predictions, input_grad, new_matrix, m_first, m_second, new_adapters, a_first, a_second, new_heads, h_first, h_second, norm_pairs)
```

```python
import functools
import jax
import jax.numpy as jnp
from jax import lax
from jax.experimental import pallas as pl
from jax.experimental.pallas import tpu as pltpu
from jax.sharding import PartitionSpec as P

LANES = 128
F32, BF16 = jnp.float32, jnp.bfloat16


def grad_kernel(
    count_ref, x_ref, cot_ref, packed_ref,
    grads_ref, heads_grad_ref, pred_ref, back_ref,
    rows_ref, cols_ref, heads_ref, weight_ref, xq_ref, q_ref, z0_ref, z1_ref, gp0_ref, gp1_ref, post_ref, pred_acc, sums_ref, gr_ref, sems,
):
    R, D = x_ref.shape
    K = heads_grad_ref.shape[0]
    z_refs, gp_refs = (z0_ref, z1_ref), (gp0_ref, gp1_ref)

    weight_ref[...] = packed_ref[:, :D].astype(F32)
    cols = packed_ref[:, D:D + LANES].astype(F32)
    cols_ref[...] = cols
    rows_ref[...] = cols.T
    L = packed_ref.shape[1] - D - LANES
    per_head = D // L
    for c in range(0, L, LANES):
        gr_ref[:K * per_head, :] = packed_ref[:K * per_head, D + LANES + c:D + 2 * LANES + c].astype(F32)
        for k in range(per_head):
            heads_ref[:, k * L + c:k * L + c + LANES] = gr_ref[pl.ds(k, K, stride=per_head), :]
    lane_rows = lax.broadcasted_iota(jnp.int32, (1, R), 1)
    q_row = jnp.where(lane_rows < count_ref[0], cot_ref[...], 0.0) * (1.0 / K)
    q_wide = jnp.broadcast_to(q_row, (LANES, R)).T
    q_ref[...] = q_wide
    half_q = 0.5 * q_row
    q_hi = half_q.astype(BF16)
    q_lo = (half_q - q_hi.astype(F32)).astype(BF16)
    xq_ref[:D, :] = (x_ref[...].astype(F32).T * half_q).astype(BF16)
    sub = lax.broadcasted_iota(jnp.int32, (16, R), 0)
    extra = jnp.where(sub == 0, q_hi.astype(F32), jnp.where(sub == 1, q_lo.astype(F32), 0.0))
    xq_ref[D:, :] = extra.astype(BF16)
    pred_acc[...] = jnp.zeros_like(pred_acc)
    gr_ref[...] = jnp.zeros_like(gr_ref)
    sums_ref[...] = jnp.zeros_like(sums_ref)
    grads_ref[...] = jnp.zeros_like(grads_ref)

    def forward(i, z_ref):
        r = rows_ref[pl.ds(i, 1), :].astype(BF16)
        step = 128
        for c in range(0, R, step):
            u = x_ref[c:c + step, :] * r
            z_ref[c:c + step, :] = jnp.dot(u, packed_ref[:, :D], preferred_element_type=F32)

    def middle(i, z_ref, gp_ref):
        s = 0.5 * rows_ref[pl.ds(K + i, 1), :]
        b = 0.5 * rows_ref[pl.ds(2 * K + i, 1), :]
        hb = heads_ref[pl.ds(i, 1), :]
        total = None
        step = 16
        for c in range(0, R, step):
            y = z_ref[c:c + step, :] * s + b
            t = jnp.tanh(y)
            a = 1.0 + t
            h = y * a
            d = a + h * (1.0 - t)
            gp_ref[c:c + step, :] = (hb * d).astype(BF16)
            hh = h * hb
            pred_acc[c:c + step, :] += sum(hh[:, l:l + LANES] for l in range(0, D, LANES))
            q = q_ref[c:c + step, :]
            qh = jnp.concatenate([h[:, l:l + LANES] * q for l in range(0, D, LANES)], axis=1)
            part = sum(qh[k:k + 8] for k in range(0, step, 8))
            total = part if total is None else total + part
        heads_grad_ref[pl.ds(i, 1), :] = jnp.sum(total, axis=0, keepdims=True)

    def after(i, gp_ref):
        s = rows_ref[pl.ds(K + i, 1), :]
        post_ref[...] = jnp.dot(xq_ref[...], gp_ref[...], preferred_element_type=F32)
        sums_ref[pl.ds(2 * K + i, 1), :] = post_ref[D:D + 1, :] + post_ref[D + 1:D + 2, :]
        total = None
        step = 16
        lane = lax.broadcasted_iota(jnp.int32, (step, LANES), 1)
        for c in range(0, D, step):
            g = post_ref[c:c + step, :]
            r = jnp.sum(jnp.where(lane == i, cols_ref[c:c + step, :], 0.0), axis=1, keepdims=True)
            t = g * weight_ref[c:c + step, :]
            rt = t * r
            part = sum(rt[k:k + 8] for k in range(0, step, 8))
            total = part if total is None else total + part
            st = t * s
            fold = sum(st[:, l:l + LANES] for l in range(0, D, LANES))
            gr_ref[c:c + step, :] += jnp.where(lane == i, jnp.sum(fold, axis=1, keepdims=True), 0.0)
            grads_ref[c:c + step, :D] += (g * s) * r
        sums_ref[pl.ds(K + i, 1), :] = jnp.sum(total, axis=0, keepdims=True)

    def send(i, which):
        return pltpu.make_async_copy(gp_refs[which], back_ref.at[i], sems.at[which])

    forward(0, z_refs[0])
    forward(1, z_refs[1])
    middle(0, z_refs[0], gp_refs[0])
    send(0, 0).start()
    forward(2, z_refs[0])
    middle(1, z_refs[1], gp_refs[1])
    after(0, gp_refs[0])
    send(1, 1).start()

    def pair(p, carry):
        i = 2 * p
        send(i - 2, 0).wait()
        forward(i + 1, z_refs[1])
        middle(i, z_refs[0], gp_refs[0])
        after(i - 1, gp_refs[1])
        send(i, 0).start()
        send(i - 1, 1).wait()
        forward(jnp.minimum(i + 2, K - 1), z_refs[0])
        middle(i + 1, z_refs[1], gp_refs[1])
        after(i, gp_refs[0])
        send(i + 1, 1).start()
        return carry

    lax.fori_loop(1, K // 2, pair, 0)
    after(K - 1, gp_refs[1])
    send(K - 2, 0).wait()
    send(K - 1, 1).wait()

    pred = jnp.sum(pred_acc[...].T, axis=0, keepdims=True)
    pred_ref[...] = jnp.where(lane_rows < count_ref[0], pred, 0.0) * (1.0 / K)
    grads_ref[:, D:] = sums_ref[...].T + gr_ref[...]


def grad_call(count, x, cot, packed, K):
    R, D = x.shape
    vm = pl.BlockSpec(memory_space=pltpu.VMEM)
    return pl.pallas_call(
        grad_kernel,
        out_shape=(
            jax.ShapeDtypeStruct((D, D + LANES), F32),
            jax.ShapeDtypeStruct((K, D), F32),
            jax.ShapeDtypeStruct((1, R), F32),
            jax.ShapeDtypeStruct((K, R, D), BF16),
        ),
        in_specs=[pl.BlockSpec(memory_space=pltpu.SMEM), vm, vm, vm],
        out_specs=(vm, vm, vm, pl.BlockSpec(memory_space=pl.ANY)),
        scratch_shapes=[
            pltpu.VMEM((LANES, D), F32), pltpu.VMEM((D, LANES), F32), pltpu.VMEM((K, D), F32), pltpu.VMEM((D, D), F32),
            pltpu.VMEM((D + 16, R), BF16), pltpu.VMEM((R, LANES), F32),
            pltpu.VMEM((R, D), F32), pltpu.VMEM((R, D), F32), pltpu.VMEM((R, D), BF16), pltpu.VMEM((R, D), BF16),
            pltpu.VMEM((D + 16, D), F32), pltpu.VMEM((R, LANES), F32), pltpu.VMEM((LANES, D), F32), pltpu.VMEM((D, LANES), F32),
            pltpu.SemaphoreType.DMA((2,)),
        ],
        compiler_params=pltpu.CompilerParams(vmem_limit_bytes=48 * 1024 * 1024),
        name="member_grads",
    )(count, x, cot, packed)


def back_kernel(G, count_ref, cot_ref, packed_ref, gp_ref, out_ref, rows_ref, cols_ref, wt_ref, ws_ref, acc_ref):
    n, R, D = gp_ref.shape
    step = pl.program_id(0)
    K = pl.num_programs(0) * n

    @pl.when(step == 0)
    def _():
        cols = packed_ref[:, D:D + LANES].astype(F32)
        cols_ref[...] = cols
        rows_ref[...] = cols.T
        wt_ref[...] = packed_ref[:, :D].astype(F32).T
        acc_ref[...] = jnp.zeros_like(acc_ref)

    lane = lax.broadcasted_iota(jnp.int32, (16, LANES), 1)
    for k in range(n):
        i = step * n + k
        r = rows_ref[pl.ds(i, 1), :]
        for c in range(0, D, 16):
            s = jnp.sum(jnp.where(lane == i + G, cols_ref[c:c + 16, :], 0.0), axis=1, keepdims=True)
            ws_ref[k * D + c:k * D + c + 16, :] = (wt_ref[c:c + 16, :] * s * r).astype(BF16)
    left = jnp.concatenate([gp_ref[k] for k in range(n)], axis=1)
    acc_ref[...] += jnp.dot(left, ws_ref[...], preferred_element_type=F32)

    @pl.when(step == pl.num_programs(0) - 1)
    def _():
        lane_rows = lax.broadcasted_iota(jnp.int32, (1, R), 1)
        q_row = jnp.where(lane_rows < count_ref[0], cot_ref[...], 0.0) * (0.5 / G)
        q_wide = jnp.broadcast_to(q_row, (LANES, R)).T
        for l in range(0, D, LANES):
            out_ref[:, l:l + LANES] = acc_ref[:, l:l + LANES] * q_wide


def back_call(count, cot, packed, back, n=4):
    K, R, D = back.shape
    vm = pl.BlockSpec(memory_space=pltpu.VMEM)
    return pl.pallas_call(
        functools.partial(back_kernel, K),
        grid=(K // n,),
        out_shape=jax.ShapeDtypeStruct((R, D), F32),
        in_specs=[pl.BlockSpec(memory_space=pltpu.SMEM), vm, vm, pl.BlockSpec((n, R, D), lambda i: (i, 0, 0))],
        out_specs=pl.BlockSpec((R, D), lambda i: (0, 0)),
        scratch_shapes=[
            pltpu.VMEM((LANES, D), F32), pltpu.VMEM((D, LANES), F32), pltpu.VMEM((D, D), F32),
            pltpu.VMEM((n * D, D), BF16), pltpu.VMEM((R, D), F32),
        ],
        compiler_params=pltpu.CompilerParams(vmem_limit_bytes=48 * 1024 * 1024),
        name="input_grads",
    )(count, cot, packed, back)


STEP = 10
beta_one = 0.5
beta_two = 0.5
epsilon = 1e-06
weight_decay = 0.01
learn_rate = 0.25
AXES = ("dp", "member")


def direction(weight, first_old, second_old, gradient):
    first_new = beta_one * first_old + (1.0 - beta_one) * gradient
    second_new = beta_two * second_old + (1.0 - beta_two) * gradient * gradient
    fix_one = 1.0 - beta_one**STEP
    fix_two = 1.0 - beta_two**STEP
    update = (
        first_new / fix_one / (jnp.sqrt(second_new / fix_two) + epsilon) + weight_decay * weight
    )
    return (first_new, second_new, update)


def bit_groups(n_dp, n_member):
    def split(low, count):
        bits = count.bit_length() - 1
        groups = []
        while bits > 0:
            take = 2 if bits >= 2 else 1
            bits -= take
            groups.append((low << bits, 1 << take))
        return groups

    return split(n_member, n_dp), split(2, n_member // 2) + [(1, 2)]


def swap(value, total, mask):
    return lax.ppermute(value, AXES, [(i, i ^ mask) for i in range(total)])


def gather_groups(value, groups, total, index):
    for axis, (low, size) in enumerate(groups):
        place = (index // low) % size
        held = [value] + [swap(value, total, low * m) for m in range(1, size)]
        value = jnp.stack([lax.select_n(place ^ p, *held) for p in range(size)], axis=axis)
    return value


def shards(n_dp, n_member, objects, counts, cotangent, matrix, matrix_first, matrix_second,
           adapters, adapter_first, adapter_second, head_weights, head_first, head_second):
    R, D = objects.shape
    K = adapters.shape[1]
    own, own_heads = matrix.shape[0], head_weights.shape[0]
    total = n_dp * n_member
    index = lax.axis_index("dp") * n_member + lax.axis_index("member")
    dp_groups, member_groups = bit_groups(n_dp, n_member)
    groups = dp_groups + member_groups

    columns = adapters.reshape(3 * K, own).T
    packed = jnp.concatenate(
        [matrix, columns, jnp.zeros((own, LANES - 3 * K), F32), head_weights.reshape(own, -1)], axis=1
    ).astype(BF16)
    full = gather_groups(packed, groups, total, index).reshape(D, -1)
    cot = cotangent.reshape(1, R)
    grads, head_grads, preds, back = grad_call(counts, objects, cot, full, K)
    input_grad = back_call(counts, cot, full, back)
    predictions = preds.reshape(R)

    grads = grads.reshape([n_dp] + [size for _, size in member_groups] + [own, D + LANES])
    head_grads = head_grads.reshape([size for _, size in member_groups] + [own_heads, D])
    head_grads = jnp.pad(head_grads, [(0, 0)] * len(member_groups) + [(0, 0), (0, LANES)])
    wide = jnp.concatenate(
        [grads.reshape((n_dp,) + grads.shape[1:]).transpose(list(range(1, 1 + len(member_groups))) + [0] + list(range(1 + len(member_groups), grads.ndim))).reshape(
            [size for _, size in member_groups] + [n_dp * own, D + LANES]), head_grads], axis=len(member_groups))
    for axis in reversed(range(len(member_groups))):
        low, size = member_groups[axis]
        place = (index // low) % size
        part = [lax.dynamic_index_in_dim(wide, place ^ m, axis, keepdims=False) for m in range(size)]
        wide = part[0]
        for m in range(1, size):
            wide = wide + swap(part[m].astype(BF16), total, low * m).astype(F32)
    mine = wide[: n_dp * own].reshape([size for _, size in dp_groups] + [own, D + LANES])
    heads = wide[n_dp * own:]
    for axis in reversed(range(len(dp_groups))):
        low, size = dp_groups[axis]
        place = (index // low) % size
        part = [lax.dynamic_index_in_dim(mine, place ^ m, axis, keepdims=False) for m in range(size)]
        mine = part[0]
        lead = part[0].shape[:-2]
        own_sum = heads
        for m in range(1, size):
            both = jnp.concatenate([part[m].reshape(-1, D + LANES), own_sum], axis=0)
            came = swap(both.astype(BF16), total, low * m).astype(F32)
            mine = mine + came[:-own_heads].reshape(lead + (own, D + LANES))
            heads = heads + came[-own_heads:]
    grad_matrix = mine[:, :D]
    grad_adapt = mine[:, D:D + 3 * K].T.reshape(3, K, own)
    head_grad = heads[:, :D]

    m_first, m_second, m_update = direction(matrix, matrix_first, matrix_second, grad_matrix)
    a_first, a_second, a_update = direction(adapters, adapter_first, adapter_second, grad_adapt)
    h_first, h_second, h_update = direction(head_weights, head_first, head_second, head_grad)

    def squares(m, a, h):
        return [jnp.sum(m * m)] + [jnp.sum(a[j] * a[j]) for j in range(3)] + [jnp.sum(h * h) / n_dp]

    sums = jnp.stack(squares(matrix, adapters, head_weights) + squares(m_update, a_update, h_update))
    for low, size in reversed(groups):
        came = [swap(sums, total, low * m) for m in range(1, size)]
        for c in came:
            sums = sums + c
    norms = jnp.sqrt(sums)
    weight_norm, update_norm = norms[:5], norms[5:]
    trust_ratio = weight_norm / update_norm
    new_matrix = matrix - learn_rate * trust_ratio[0] * m_update
    new_adapters = adapters - learn_rate * trust_ratio[1:4][:, None, None] * a_update
    new_heads = head_weights - learn_rate * trust_ratio[4] * h_update
    norm_pairs = jnp.stack([weight_norm, update_norm], axis=1)
    return (predictions, input_grad, new_matrix, m_first, m_second, new_adapters, a_first, a_second,
            new_heads, h_first, h_second, norm_pairs)


def solution(mesh):
    n_dp, n_member = mesh.shape["dp"], mesh.shape["member"]
    rows, cols = P(AXES, None), P(None, None, AXES)
    heads = P("member", None)
    return jax.shard_map(
        functools.partial(shards, n_dp, n_member),
        mesh=mesh,
        in_specs=(rows, P(AXES), P(AXES), rows, rows, rows, cols, cols, cols, heads, heads, heads),
        out_specs=(P(AXES), rows, rows, rows, rows, cols, cols, cols, heads, heads, heads, P()),
        check_vma=False,
    )
```

```python
import functools

import jax
import jax.numpy as jnp
from jax import lax
from jax.experimental import pallas as pl
from jax.experimental.pallas import tpu as pltpu
from jax.sharding import PartitionSpec as P

LANES = 128
F32, BF16 = jnp.float32, jnp.bfloat16
STEP = 10
beta_one = 0.5
beta_two = 0.5
epsilon = 1e-06
weight_decay = 0.01
learn_rate = 0.25
AXES = ("dp", "member")
VMEM = pl.BlockSpec(memory_space=pltpu.VMEM)
SMEM = pl.BlockSpec(memory_space=pltpu.SMEM)
LIMIT = 48 * 1024 * 1024


def shape(dims, dtype=F32):
    return jax.ShapeDtypeStruct(dims, dtype)


def this_core():
    return lax.rem(lax.axis_index("member"), 2)


def pack_kernel(count_ref, matrix_ref, adapters_ref, heads_ref, cot_ref, packed_ref, q_ref):
    own, D = matrix_ref.shape
    K = adapters_ref.shape[2]
    packed_ref[:, :D] = matrix_ref[...].astype(BF16)
    parts = [adapters_ref[k] for k in range(3)] + [jnp.zeros((own, LANES - 3 * K), F32)]
    packed_ref[:, D:D + LANES] = jnp.concatenate(parts, axis=1).astype(BF16)
    L = packed_ref.shape[1] - D - LANES
    rows = []
    for t in range(own):
        h, c = divmod(t * L, D)
        rows.append(heads_ref[h:h + 1, c:c + L])
    packed_ref[:, D + LANES:] = jnp.concatenate(rows, axis=0).astype(BF16)
    lane = lax.broadcasted_iota(jnp.int32, cot_ref.shape, 1)
    q_ref[...] = jnp.where(lane < count_ref[0], cot_ref[...], 0.0) * (1.0 / K)


def pack_call(counts, matrix, adapters_t, heads, cot):
    own, D = matrix.shape
    L = heads.shape[0] * D // own
    return pl.pallas_call(
        pack_kernel,
        out_shape=(shape((own, D + LANES + L), BF16), shape(cot.shape)),
        in_specs=[SMEM, VMEM, VMEM, VMEM, VMEM],
        out_specs=(VMEM, VMEM),
        name="pack_weights",
    )(counts, matrix, adapters_t, heads, cot)


def grad_kernel(
    x0_ref, x1_ref, q0_ref, q1_ref, packed_ref,
    keep_ref, sent_ref, heads_grad_ref, pred_ref, back_ref,
    rows_ref, cols_ref, heads_ref, weight_ref, x_ref, xq_ref, q_ref, z0_ref, z1_ref, gp0_ref, gp1_ref,
    post_ref, pred_acc, sums_ref, gr_ref, grads_ref, *, own,
):
    half, D = x0_ref.shape
    R = 2 * half
    K = heads_grad_ref.shape[0]
    members = K // 2
    n = back_ref.shape[0]
    step_id, steps = pl.program_id(0), pl.num_programs(0)
    core = this_core()
    base = core * members
    z_refs, gp_refs = (z0_ref, z1_ref), (gp0_ref, gp1_ref)

    def set_up():
        weight_ref[...] = packed_ref[:, :D].astype(F32)
        cols = packed_ref[:, D:D + LANES].astype(F32)
        cols_ref[...] = cols
        rows_ref[...] = cols.T
        L = packed_ref.shape[1] - D - LANES
        per_head = D // L
        for c in range(0, L, LANES):
            gr_ref[:K * per_head, :] = packed_ref[:K * per_head, D + LANES + c:D + 2 * LANES + c].astype(F32)
            for k in range(per_head):
                heads_ref[:, k * L + c:k * L + c + LANES] = gr_ref[pl.ds(k, K, stride=per_head), :]
        x_ref[:half, :] = x0_ref[...]
        x_ref[half:, :] = x1_ref[...]
        for side, (x_side, q_side) in enumerate(((x0_ref, q0_ref), (x1_ref, q1_ref))):
            at = slice(side * half, (side + 1) * half)
            q_row = q_side[...]
            q_ref[at, :] = jnp.broadcast_to(q_row, (LANES, half)).T
            half_q = 0.5 * q_row
            q_hi = half_q.astype(BF16)
            q_lo = (half_q - q_hi.astype(F32)).astype(BF16)
            xq_ref[:D, at] = (x_side[...].astype(F32).T * half_q).astype(BF16)
            sub = lax.broadcasted_iota(jnp.int32, (16, half), 0)
            extra = jnp.where(sub == 0, q_hi.astype(F32), jnp.where(sub == 1, q_lo.astype(F32), 0.0))
            xq_ref[D:, at] = extra.astype(BF16)
        for ref in (pred_acc, gr_ref, sums_ref, grads_ref, gp1_ref, heads_grad_ref):
            ref[...] = jnp.zeros_like(ref)

    def forward(i, z_ref):
        r = rows_ref[pl.ds(base + i, 1), :].astype(BF16)
        z_ref[...] = jnp.dot(x_ref[...] * r, packed_ref[:, :D], preferred_element_type=F32)

    def middle(i, k, z_ref, gp_ref):
        s = 0.5 * rows_ref[pl.ds(K + base + i, 1), :]
        b = 0.5 * rows_ref[pl.ds(2 * K + base + i, 1), :]
        hb = heads_ref[pl.ds(base + i, 1), :]
        total = None
        step = 16
        for c in range(0, R, step):
            y = z_ref[c:c + step, :] * s + b
            t = jnp.tanh(y)
            a = 1.0 + t
            h = y * a
            d = a + h * (1.0 - t)
            gp = (hb * d).astype(BF16)
            gp_ref[c:c + step, :] = gp
            back_ref[k, c:c + step, :] = gp
            hh = h * hb
            pred_acc[c:c + step, :] += sum(hh[:, l:l + LANES] for l in range(0, D, LANES))
            q = q_ref[c:c + step, :]
            qh = jnp.concatenate([h[:, l:l + LANES] * q for l in range(0, D, LANES)], axis=1)
            part = sum(qh[j:j + 8] for j in range(0, step, 8))
            total = part if total is None else total + part
        heads_grad_ref[pl.ds(base + i, 1), :] = jnp.sum(total, axis=0, keepdims=True)

    def after(i, gp_ref):
        s = rows_ref[pl.ds(K + base + i, 1), :]
        post_ref[...] = jnp.dot(xq_ref[...], gp_ref[...], preferred_element_type=F32)
        sums_ref[pl.ds(2 * K + base + i, 1), :] = post_ref[D:D + 1, :] + post_ref[D + 1:D + 2, :]
        total = None
        step = 16
        lane = lax.broadcasted_iota(jnp.int32, (step, LANES), 1)
        for c in range(0, D, step):
            g = post_ref[c:c + step, :]
            r = jnp.sum(jnp.where(lane == base + i, cols_ref[c:c + step, :], 0.0), axis=1, keepdims=True)
            t = g * weight_ref[c:c + step, :]
            rt = t * r
            part = sum(rt[j:j + 8] for j in range(0, step, 8))
            total = part if total is None else total + part
            st = t * s
            fold = sum(st[:, l:l + LANES] for l in range(0, D, LANES))
            gr_ref[c:c + step, :] += jnp.where(lane == base + i, jnp.sum(fold, axis=1, keepdims=True), 0.0)
            grads_ref[c:c + step, :D] += (g * s) * r
        sums_ref[pl.ds(K + base + i, 1), :] = jnp.sum(total, axis=0, keepdims=True)

    @pl.when(step_id == 0)
    def _():
        set_up()
        forward(0, z_refs[0])
        middle(0, 0, z_refs[0], gp_refs[0])
        forward(1, z_refs[1])

    @pl.when(step_id > 0)
    def _():
        i = step_id * n
        middle(i, 0, z_refs[0], gp_refs[0])
        after(i - 1, gp_refs[1])
        forward(i + 1, z_refs[1])

    for k in range(1, n):
        i, now, other = step_id * n + k, k % 2, (k + 1) % 2
        middle(i, k, z_refs[now], gp_refs[now])
        after(i - 1, gp_refs[other])
        forward(jnp.minimum(i + 1, members - 1), z_refs[other])

    @pl.when(step_id == steps - 1)
    def _():
        after(members - 1, gp_refs[1])
        for side in range(2):
            at = slice(side * half, (side + 1) * half)
            pred_ref[side:side + 1, :] = jnp.sum(pred_acc[at, :].T, axis=0, keepdims=True)
        grads_ref[:, D:] = sums_ref[...].T + gr_ref[...]
        for j in range(D // (2 * own)):
            low = grads_ref[2 * j * own:(2 * j + 1) * own, :]
            high = grads_ref[(2 * j + 1) * own:(2 * j + 2) * own, :]
            keep_ref[j * own:(j + 1) * own, :] = jnp.where(core == 0, low, high)
            sent_ref[j * own:(j + 1) * own, :] = jnp.where(core == 0, high, low).astype(BF16)


def grad_call(x0, x1, q0, q1, packed, K, own, n=2):
    half, D = x0.shape
    R = 2 * half
    members = K // 2
    flops = 4 * members * R * D * D
    return pl.pallas_call(
        functools.partial(grad_kernel, own=own),
        grid=(members // n,),
        out_shape=(
            shape((D // 2, D + LANES)), shape((D // 2, D + LANES), BF16), shape((K, D)), shape((2, half)),
            shape((members, R, D), BF16),
        ),
        in_specs=[VMEM] * 5,
        out_specs=(VMEM, VMEM, VMEM, VMEM, pl.BlockSpec((n, R, D), lambda i: (i, 0, 0))),
        scratch_shapes=[
            pltpu.VMEM((LANES, D), F32), pltpu.VMEM((D, LANES), F32), pltpu.VMEM((K, D), F32), pltpu.VMEM((D, D), F32),
            pltpu.VMEM((R, D), BF16), pltpu.VMEM((D + 16, R), BF16), pltpu.VMEM((R, LANES), F32),
            pltpu.VMEM((R, D), F32), pltpu.VMEM((R, D), F32), pltpu.VMEM((R, D), BF16), pltpu.VMEM((R, D), BF16),
            pltpu.VMEM((D + 16, D), F32), pltpu.VMEM((R, LANES), F32), pltpu.VMEM((LANES, D), F32),
            pltpu.VMEM((D, LANES), F32), pltpu.VMEM((D, D + LANES), F32),
        ],
        compiler_params=pltpu.CompilerParams(vmem_limit_bytes=LIMIT),
        cost_estimate=pl.CostEstimate(flops=2 * flops, bytes_accessed=members * R * D * 2, transcendentals=members * R * D),
        name="member_grads",
    )(x0, x1, q0, q1, packed)


def back_kernel(q_ref, packed_ref, gp_ref, *refs, members, other):
    if other:
        out_ref, rows_ref, cols_ref, wt_ref, ws_ref, acc_ref = refs
    else:
        came_ref, pred_ref, pred_came_ref, out_ref, pred_out_ref, rows_ref, cols_ref, wt_ref, ws_ref, acc_ref = refs
    n, R, D = gp_ref.shape
    step = pl.program_id(0)
    K = 2 * members
    base = this_core() * members

    @pl.when(step == 0)
    def _():
        cols = packed_ref[:, D:D + LANES].astype(F32)
        cols_ref[...] = cols
        rows_ref[...] = cols.T
        wt_ref[...] = packed_ref[:, :D].astype(F32).T
        acc_ref[...] = jnp.zeros_like(acc_ref)

    lane = lax.broadcasted_iota(jnp.int32, (16, LANES), 1)
    for k in range(n):
        i = base + step * n + k
        r = rows_ref[pl.ds(i, 1), :]
        for c in range(0, D, 16):
            s = jnp.sum(jnp.where(lane == i + K, cols_ref[c:c + 16, :], 0.0), axis=1, keepdims=True)
            ws_ref[k * D + c:k * D + c + 16, :] = (wt_ref[c:c + 16, :] * s * r).astype(BF16)
    left = jnp.concatenate([gp_ref[k] for k in range(n)], axis=1)
    acc_ref[...] += jnp.dot(left, ws_ref[...], preferred_element_type=F32)

    @pl.when(step == pl.num_programs(0) - 1)
    def _():
        q_wide = jnp.broadcast_to(0.5 * q_ref[...], (LANES, R)).T
        for l in range(0, D, LANES):
            value = acc_ref[:, l:l + LANES] * q_wide
            out_ref[:, l:l + LANES] = value if other else value + came_ref[:, l:l + LANES]
        if not other:
            pred_out_ref[...] = (pred_ref[0:1, :] + pred_came_ref[...]) * (1.0 / K)


def back_call(q, packed, back, came=None, n=4):
    members, R2, D = back.shape
    R = R2 // 2
    other = came is None
    where = 1 if other else 0
    more = [] if other else list(came)
    return pl.pallas_call(
        functools.partial(back_kernel, members=members, other=other),
        grid=(members // n,),
        out_shape=shape((R, D)) if other else (shape((R, D)), shape((1, R))),
        in_specs=[VMEM, VMEM, pl.BlockSpec((n, R, D), lambda i: (i, where, 0))] + [VMEM] * len(more),
        out_specs=VMEM if other else (VMEM, VMEM),
        scratch_shapes=[
            pltpu.VMEM((LANES, D), F32), pltpu.VMEM((D, LANES), F32), pltpu.VMEM((D, D), F32),
            pltpu.VMEM((n * D, D), BF16), pltpu.VMEM((R, D), F32),
        ],
        compiler_params=pltpu.CompilerParams(vmem_limit_bytes=LIMIT),
        cost_estimate=pl.CostEstimate(flops=2 * members * R * D * D, bytes_accessed=members * R * D * 2, transcendentals=0),
        name="input_grads_other" if other else "input_grads",
    )(q, packed, back, *more)


def direction(weight, first_old, second_old, gradient):
    first_new = beta_one * first_old + (1.0 - beta_one) * gradient
    second_new = beta_two * second_old + (1.0 - beta_two) * gradient * gradient
    fix_one = 1.0 - beta_one**STEP
    fix_two = 1.0 - beta_two**STEP
    update = (
        first_new / fix_one / (jnp.sqrt(second_new / fix_two) + epsilon) + weight_decay * weight
    )
    return (first_new, second_new, update)


def lane_sums(value):
    total = jnp.sum(value, axis=0, keepdims=True)
    width = total.shape[1]
    if width < LANES:
        return jnp.concatenate([total, jnp.zeros((1, LANES - width), F32)], axis=1)
    return sum(total[:, l:l + LANES] for l in range(0, width, LANES))


def direction_kernel(count, *refs):
    mine_ref, heads_ref = refs[:2]
    came = refs[2:2 + count]
    (m_ref, m1_ref, m2_ref, a_ref, a1_ref, a2_ref, h_ref, h1_ref, h2_ref,
     m1_out, m2_out, mu_out, a1_out, a2_out, au_out, h1_out, h2_out, hu_out, sums_out) = refs[2 + count:]
    own, D = m_ref.shape
    K = a_ref.shape[2]
    n_heads = h_ref.shape[0]
    grad = mine_ref[...]
    heads = heads_ref[:, :D]
    for c in came:
        grad = grad + c[:own, :].astype(F32)
        heads = heads + c[own:own + n_heads, :D].astype(F32)
    weight_rows, update_rows = [], []
    first, second, update = direction(m_ref[...], m1_ref[...], m2_ref[...], grad[:, :D])
    m1_out[...], m2_out[...], mu_out[...] = first, second, update
    weight_rows.append(lane_sums(m_ref[...] * m_ref[...]))
    update_rows.append(lane_sums(update * update))
    for k in range(3):
        first, second, update = direction(a_ref[k], a1_ref[k], a2_ref[k], grad[:, D + k * K:D + (k + 1) * K])
        a1_out[k], a2_out[k], au_out[k] = first, second, update
        weight_rows.append(lane_sums(a_ref[k] * a_ref[k]))
        update_rows.append(lane_sums(update * update))
    first, second, update = direction(h_ref[...], h1_ref[...], h2_ref[...], heads)
    h1_out[...], h2_out[...], hu_out[...] = first, second, update
    share = 1.0 / lax.axis_size("dp")
    weight_rows.append(lane_sums(h_ref[...] * h_ref[...]) * share)
    update_rows.append(lane_sums(update * update) * share)
    sums_out[...] = jnp.concatenate(weight_rows + update_rows + [jnp.zeros((6, LANES), F32)], axis=0)


def direction_call(mine, heads, came, states):
    m, a, h = states[0], states[3], states[6]
    outs = [shape(v.shape) for v in (m, m, m, a, a, a, h, h, h)] + [shape((16, LANES))]
    return pl.pallas_call(
        functools.partial(direction_kernel, len(came)),
        out_shape=tuple(outs),
        in_specs=[VMEM] * (2 + len(came) + 9),
        out_specs=tuple([VMEM] * 10),
        name="directions",
    )(mine, heads, *came, *states)


def update_kernel(count, *refs):
    sums_refs = refs[:count]
    m_ref, a_ref, h_ref, mu_ref, au_ref, hu_ref, m_out, a_out, h_out, norms_out = refs[count:]
    total = sums_refs[0][...]
    for ref in sums_refs[1:]:
        total = total + ref[...]
    norms = jnp.sqrt(jnp.sum(total, axis=1, keepdims=True))
    weight_norm, update_norm = norms[0:5], norms[5:10]
    rate = learn_rate * (weight_norm / update_norm)
    m_out[...] = m_ref[...] - rate[0:1] * mu_ref[...]
    for k in range(3):
        a_out[k] = a_ref[k] - rate[1 + k:2 + k] * au_ref[k]
    h_out[...] = h_ref[...] - rate[4:5] * hu_ref[...]
    norms_out[...] = jnp.concatenate([weight_norm, update_norm], axis=1)


def update_call(sums, m, a, h, mu, au, hu):
    return pl.pallas_call(
        functools.partial(update_kernel, len(sums)),
        out_shape=(shape(m.shape), shape(a.shape), shape(h.shape), shape((5, 2))),
        in_specs=[VMEM] * (len(sums) + 6),
        out_specs=(VMEM,) * 4,
        name="updates",
    )(*sums, m, a, h, mu, au, hu)


def bit_groups(n_dp, n_member):
    def split(low, count):
        bits = count.bit_length() - 1
        groups = []
        while bits > 0:
            take = 2 if bits >= 2 else 1
            bits -= take
            groups.append((low << bits, 1 << take))
        return groups

    return split(n_member, n_dp), split(2, n_member // 2) + [(1, 2)]


def swap(value, total, mask):
    return lax.ppermute(value, AXES, [(i, i ^ mask) for i in range(total)])


def gather_groups(value, groups, total, index):
    for axis, (low, size) in enumerate(groups):
        place = (index // low) % size
        held = [value] + [swap(value, total, low * m) for m in range(1, size)]
        value = jnp.stack([lax.select_n(place ^ p, *held) for p in range(size)], axis=axis)
    return value


def shards(n_dp, n_member, objects, counts, cotangent, matrix, matrix_first, matrix_second,
           adapters, adapter_first, adapter_second, head_weights, head_first, head_second):
    R, D = objects.shape
    K = adapters.shape[1]
    own, own_heads = matrix.shape[0], head_weights.shape[0]
    total = n_dp * n_member
    index = lax.axis_index("dp") * n_member + lax.axis_index("member")
    dp_groups, member_groups = bit_groups(n_dp, n_member)
    chip_groups = member_groups[:-1]
    turned = [v.transpose(0, 2, 1) for v in (adapters, adapter_first, adapter_second)]

    packed, q_own = pack_call(counts, matrix, turned[0], head_weights, cotangent.reshape(1, R))
    x_other = swap(objects, total, 1)
    q_other = swap(q_own, total, 1)
    full = gather_groups(packed, dp_groups + member_groups, total, index).reshape(D, -1)
    keep, sent, head_grads, preds, back = grad_call(objects, x_other, q_own, q_other, full, K, own)
    pred_came = swap(preds[1:2], total, 1)

    chips = [size for _, size in chip_groups]
    head_grads = head_grads.reshape(chips + [2, own_heads, D])
    core = index % 2
    axis = len(chips)

    def arrange(main, heads):
        main = main.reshape([n_dp] + chips + [own, D + LANES])
        main = jnp.moveaxis(main, 0, len(chips)).reshape(chips + [n_dp * own, D + LANES])
        return jnp.concatenate([main, jnp.pad(heads, [(0, 0)] * (len(chips) + 1) + [(0, LANES)])], axis=len(chips))

    other_heads = lax.dynamic_index_in_dim(head_grads, 1 - core, axis, keepdims=False)
    own_heads_grad = lax.dynamic_index_in_dim(head_grads, core, axis, keepdims=False)
    came = swap(arrange(sent, other_heads.astype(BF16)), total, 1)
    wide = arrange(keep, own_heads_grad) + came.astype(F32)
    for axis in reversed(range(len(chips))):
        low, size = chip_groups[axis]
        place = (index // low) % size
        part = [lax.dynamic_index_in_dim(wide, place ^ m, axis, keepdims=False) for m in range(size)]
        wide = part[0]
        for m in range(1, size):
            wide = wide + swap(part[m].astype(BF16), total, low * m).astype(F32)
    mine = wide[: n_dp * own].reshape([size for _, size in dp_groups] + [own, D + LANES])
    heads = wide[n_dp * own:]
    for axis in reversed(range(len(dp_groups))):
        low, size = dp_groups[axis]
        place = (index // low) % size
        part = [lax.dynamic_index_in_dim(mine, place ^ m, axis, keepdims=False) for m in range(size)]
        lead = part[0].shape[:-2]
        both = [jnp.concatenate([p.reshape(-1, D + LANES), heads], axis=0).astype(BF16) for p in part[1:]]
        last = [swap(b, total, low * (m + 1)) for m, b in enumerate(both)]
        mine = part[0]
        if axis:
            for c in last:
                mine = mine + c[:-own_heads].astype(F32).reshape(lead + (own, D + LANES))
                heads = heads + c[-own_heads:].astype(F32)

    ig_came = swap(back_call(q_other, full, back), total, 1)
    input_grad, predictions = back_call(q_own, full, back, (ig_came, preds, pred_came))
    lane = lax.broadcasted_iota(jnp.int32, (1, R), 1)
    predictions = jnp.where(lane < counts[0], predictions, 0.0)

    states = [matrix, matrix_first, matrix_second, *turned, head_weights, head_first, head_second]
    (m_first, m_second, m_update, a_first, a_second, a_update, h_first, h_second, h_update, sums) = direction_call(
        mine, heads, last, states)
    pending = [sums]
    for low, size in [(1, 2)] + chip_groups[::-1] + dp_groups[::-1]:
        sums = pending[0]
        for p in pending[1:]:
            sums = sums + p
        pending = [sums] + [swap(sums, total, low * m) for m in range(1, size)]
    new_matrix, new_adapters, new_heads, norm_pairs = update_call(
        pending, matrix, turned[0], head_weights, m_update, a_update, h_update)

    def back_turn(v):
        return v.transpose(0, 2, 1)

    return (predictions.reshape(R), input_grad, new_matrix, m_first, m_second, back_turn(new_adapters),
            back_turn(a_first), back_turn(a_second), new_heads, h_first, h_second, norm_pairs)


def solution(mesh):
    n_dp, n_member = mesh.shape["dp"], mesh.shape["member"]
    rows, cols = P(AXES, None), P(None, None, AXES)
    heads = P("member", None)
    return jax.shard_map(
        functools.partial(shards, n_dp, n_member),
        mesh=mesh,
        in_specs=(rows, P(AXES), P(AXES), rows, rows, rows, cols, cols, cols, heads, heads, heads),
        out_specs=(P(AXES), rows, rows, rows, rows, cols, cols, cols, heads, heads, heads, P()),
        check_vma=False,
    )
```

```python
import functools

import jax
import jax.numpy as jnp
from jax import lax
from jax.experimental import pallas as pl
from jax.experimental.pallas import tpu as pltpu
from jax.sharding import PartitionSpec as P

LANES = 128
F32, BF16 = jnp.float32, jnp.bfloat16
STEP = 10
beta_one = 0.5
beta_two = 0.5
epsilon = 1e-06
weight_decay = 0.01
learn_rate = 0.25
AXES = ("dp", "member")
VMEM = pl.BlockSpec(memory_space=pltpu.VMEM)
SMEM = pl.BlockSpec(memory_space=pltpu.SMEM)
LIMIT = 48 * 1024 * 1024


def shape(dims, dtype=F32):
    return jax.ShapeDtypeStruct(dims, dtype)


def this_core():
    return lax.rem(lax.axis_index("member"), 2)


def pack_kernel(count_ref, matrix_ref, adapters_ref, heads_ref, cot_ref, packed_ref, q_ref):
    own, D = matrix_ref.shape
    K = adapters_ref.shape[2]
    packed_ref[:, :D] = matrix_ref[...].astype(BF16)
    parts = [adapters_ref[k] for k in range(3)] + [jnp.zeros((own, LANES - 3 * K), F32)]
    packed_ref[:, D:D + LANES] = jnp.concatenate(parts, axis=1).astype(BF16)
    L = packed_ref.shape[1] - D - LANES
    rows = []
    for t in range(own):
        h, c = divmod(t * L, D)
        rows.append(heads_ref[h:h + 1, c:c + L])
    packed_ref[:, D + LANES:] = jnp.concatenate(rows, axis=0).astype(BF16)
    lane = lax.broadcasted_iota(jnp.int32, cot_ref.shape, 1)
    q_ref[...] = jnp.where(lane < count_ref[0], cot_ref[...], 0.0) * (1.0 / K)


def pack_call(counts, matrix, adapters_t, heads, cot):
    own, D = matrix.shape
    L = heads.shape[0] * D // own
    return pl.pallas_call(
        pack_kernel,
        out_shape=(shape((own, D + LANES + L), BF16), shape(cot.shape)),
        in_specs=[SMEM, VMEM, VMEM, VMEM, VMEM],
        out_specs=(VMEM, VMEM),
        name="pack_weights",
    )(counts, matrix, adapters_t, heads, cot)


def grad_kernel(
    x0_ref, x1_ref, q0_ref, q1_ref, packed_ref,
    keep_ref, sent_ref, heads_grad_ref, pred_ref, rows_ref, turned_ref, back_ref,
    cols_ref, heads_ref, weight_ref, x_ref, xq_ref, q_ref, z0_ref, z1_ref, gp0_ref, gp1_ref,
    post_ref, pred_acc, sums_ref, gr_ref, grads_ref, *, own,
):
    half, D = x0_ref.shape
    R = 2 * half
    K = heads_grad_ref.shape[0]
    members = K // 2
    n = back_ref.shape[0]
    step_id, steps = pl.program_id(0), pl.num_programs(0)
    core = this_core()
    base = core * members
    z_refs, gp_refs = (z0_ref, z1_ref), (gp0_ref, gp1_ref)

    def set_up():
        weight_ref[...] = packed_ref[:, :D].astype(F32)
        cols = packed_ref[:, D:D + LANES].astype(F32)
        cols_ref[...] = cols
        rows_ref[...] = cols.T
        turned_ref[...] = weight_ref[...].T.astype(BF16)
        L = packed_ref.shape[1] - D - LANES
        per_head = D // L
        for c in range(0, L, LANES):
            gr_ref[:K * per_head, :] = packed_ref[:K * per_head, D + LANES + c:D + 2 * LANES + c].astype(F32)
            for k in range(per_head):
                heads_ref[:, k * L + c:k * L + c + LANES] = gr_ref[pl.ds(k, K, stride=per_head), :]
        x_ref[:half, :] = x0_ref[...]
        x_ref[half:, :] = x1_ref[...]
        for side, (x_side, q_side) in enumerate(((x0_ref, q0_ref), (x1_ref, q1_ref))):
            at = slice(side * half, (side + 1) * half)
            q_row = q_side[...]
            q_ref[at, :] = jnp.broadcast_to(q_row, (LANES, half)).T
            half_q = 0.5 * q_row
            q_hi = half_q.astype(BF16)
            q_lo = (half_q - q_hi.astype(F32)).astype(BF16)
            xq_ref[:D, at] = (x_side[...].astype(F32).T * half_q).astype(BF16)
            sub = lax.broadcasted_iota(jnp.int32, (16, half), 0)
            extra = jnp.where(sub == 0, q_hi.astype(F32), jnp.where(sub == 1, q_lo.astype(F32), 0.0))
            xq_ref[D:, at] = extra.astype(BF16)
        for ref in (pred_acc, gr_ref, sums_ref, grads_ref, gp1_ref, heads_grad_ref):
            ref[...] = jnp.zeros_like(ref)

    def forward(i, z_ref):
        r = rows_ref[pl.ds(base + i, 1), :].astype(BF16)
        z_ref[...] = jnp.dot(x_ref[...] * r, packed_ref[:, :D], preferred_element_type=F32)

    def middle(i, k, z_ref, gp_ref, lo, hi, total):
        s = 0.5 * rows_ref[pl.ds(K + base + i, 1), :]
        b = 0.5 * rows_ref[pl.ds(2 * K + base + i, 1), :]
        hb = heads_ref[pl.ds(base + i, 1), :]
        step = 16
        for c in range(lo, hi, step):
            y = z_ref[c:c + step, :] * s + b
            t = jnp.tanh(y)
            a = 1.0 + t
            h = y * a
            d = a + h * (1.0 - t)
            gp = (hb * d).astype(BF16)
            gp_ref[c:c + step, :] = gp
            back_ref[k, c:c + step, :] = gp
            hh = h * hb
            pred_acc[c:c + step, :] += sum(hh[:, l:l + LANES] for l in range(0, D, LANES))
            q = q_ref[c:c + step, :]
            qh = jnp.concatenate([h[:, l:l + LANES] * q for l in range(0, D, LANES)], axis=1)
            part = sum(qh[j:j + 8] for j in range(0, step, 8))
            total = part if total is None else total + part
        return total

    def outer(gp_ref):
        post_ref[...] = jnp.dot(xq_ref[...], gp_ref[...], preferred_element_type=F32)

    def spread(i, lo, hi, total):
        s = rows_ref[pl.ds(K + base + i, 1), :]
        step = 16
        lane = lax.broadcasted_iota(jnp.int32, (step, LANES), 1)
        for c in range(lo, hi, step):
            g = post_ref[c:c + step, :]
            r = jnp.sum(jnp.where(lane == base + i, cols_ref[c:c + step, :], 0.0), axis=1, keepdims=True)
            t = g * weight_ref[c:c + step, :]
            rt = t * r
            part = sum(rt[j:j + 8] for j in range(0, step, 8))
            total = part if total is None else total + part
            st = t * s
            fold = sum(st[:, l:l + LANES] for l in range(0, D, LANES))
            gr_ref[c:c + step, :] += jnp.where(lane == base + i, jnp.sum(fold, axis=1, keepdims=True), 0.0)
            grads_ref[c:c + step, :D] += (g * s) * r
        return total

    def finish(i, total):
        sums_ref[pl.ds(K + base + i, 1), :] = jnp.sum(total, axis=0, keepdims=True)
        sums_ref[pl.ds(2 * K + base + i, 1), :] = post_ref[D:D + 1, :] + post_ref[D + 1:D + 2, :]

    def member(i, k, now, other, nxt):
        total = middle(i, k, z_refs[now], gp_refs[now], 0, R, None)
        forward(nxt, z_refs[other])
        outer(gp_refs[other])
        heads_grad_ref[pl.ds(base + i, 1), :] = jnp.sum(total, axis=0, keepdims=True)
        finish(i - 1, spread(i - 1, 0, D, None))

    @pl.when(step_id == 0)
    def _():
        set_up()
        forward(0, z_refs[0])

    for k in range(n):
        i, now, other = step_id * n + k, k % 2, (k + 1) % 2
        member(i, k, now, other, jnp.minimum(i + 1, members - 1))

    @pl.when(step_id == steps - 1)
    def _():
        outer(gp_refs[1])
        finish(members - 1, spread(members - 1, 0, D, None))
        for side in range(2):
            at = slice(side * half, (side + 1) * half)
            pred_ref[side:side + 1, :] = jnp.sum(pred_acc[at, :].T, axis=0, keepdims=True)
        grads_ref[:, D:] = sums_ref[...].T + gr_ref[...]
        for j in range(D // (2 * own)):
            low = grads_ref[2 * j * own:(2 * j + 1) * own, :]
            high = grads_ref[(2 * j + 1) * own:(2 * j + 2) * own, :]
            keep_ref[j * own:(j + 1) * own, :] = jnp.where(core == 0, low, high)
            sent_ref[j * own:(j + 1) * own, :] = jnp.where(core == 0, high, low).astype(BF16)


def grad_call(x0, x1, q0, q1, packed, K, own, n=2):
    half, D = x0.shape
    R = 2 * half
    members = K // 2
    flops = 4 * members * R * D * D
    return pl.pallas_call(
        functools.partial(grad_kernel, own=own),
        grid=(members // n,),
        out_shape=(
            shape((D // 2, D + LANES)), shape((D // 2, D + LANES), BF16), shape((K, D)), shape((2, half)),
            shape((LANES, D)), shape((D, D), BF16), shape((members, R, D), BF16),
        ),
        in_specs=[VMEM] * 5,
        out_specs=(VMEM, VMEM, VMEM, VMEM, VMEM, VMEM, pl.BlockSpec((n, R, D), lambda i: (i, 0, 0))),
        scratch_shapes=[
            pltpu.VMEM((D, LANES), F32), pltpu.VMEM((K, D), F32), pltpu.VMEM((D, D), F32),
            pltpu.VMEM((R, D), BF16), pltpu.VMEM((D + 16, R), BF16), pltpu.VMEM((R, LANES), F32),
            pltpu.VMEM((R, D), F32), pltpu.VMEM((R, D), F32), pltpu.VMEM((R, D), BF16), pltpu.VMEM((R, D), BF16),
            pltpu.VMEM((D + 16, D), F32), pltpu.VMEM((R, LANES), F32), pltpu.VMEM((LANES, D), F32),
            pltpu.VMEM((D, LANES), F32), pltpu.VMEM((D, D + LANES), F32),
        ],
        compiler_params=pltpu.CompilerParams(vmem_limit_bytes=LIMIT),
        cost_estimate=pl.CostEstimate(flops=2 * flops, bytes_accessed=members * R * D * 2, transcendentals=members * R * D),
        name="member_grads",
    )(x0, x1, q0, q1, packed)


def back_kernel(*refs, members, start, first, last):
    rows_ref, turned_ref, gp_ref = refs[:3]
    rest = list(refs[3:])
    acc_in = None if first else rest.pop(0)
    q_ref = rest.pop(0) if last else None
    came_ref = rest.pop(0) if last == "own" else None
    out_ref, acc_ref = rest
    n, R, D = gp_ref.shape
    step = pl.program_id(0)
    K = 2 * members
    base = this_core() * members + start

    @pl.when(step == 0)
    def _():
        acc_ref[...] = jnp.zeros_like(acc_ref) if first else acc_in[...]

    left, right = [], []
    for k in range(n):
        i = base + step * n + k
        r = rows_ref[pl.ds(i, 1), :].astype(BF16)
        s = rows_ref[pl.ds(K + i, 1), :].astype(BF16)
        left.append(gp_ref[k] * s)
        right.append(turned_ref[...] * r)
    acc_ref[...] += jnp.dot(jnp.concatenate(left, axis=1), jnp.concatenate(right, axis=0), preferred_element_type=F32)

    @pl.when(step == pl.num_programs(0) - 1)
    def _():
        if not last:
            out_ref[...] = acc_ref[...]
        else:
            q_wide = jnp.broadcast_to(0.5 * q_ref[...], (LANES, R)).T
            for l in range(0, D, LANES):
                value = acc_ref[:, l:l + LANES] * q_wide
                out_ref[:, l:l + LANES] = value if came_ref is None else value + came_ref[:, l:l + LANES]


def back_call(rows, turned, back, where, start, count, acc=None, q=None, came=None, n=4):
    members, R2, D = back.shape
    R = R2 // 2
    last = None if q is None else "other" if came is None else "own"
    more = [v for v in (acc, q, came) if v is not None]
    return pl.pallas_call(
        functools.partial(back_kernel, members=members, start=start, first=acc is None, last=last),
        grid=(count // n,),
        out_shape=shape((R, D)),
        in_specs=[VMEM, VMEM, pl.BlockSpec((n, R, D), lambda i: (start // n + i, where, 0))] + [VMEM] * len(more),
        out_specs=VMEM,
        scratch_shapes=[pltpu.VMEM((R, D), F32)],
        compiler_params=pltpu.CompilerParams(vmem_limit_bytes=LIMIT // 2),
        cost_estimate=pl.CostEstimate(flops=2 * count * R * D * D, bytes_accessed=count * R * D * 2, transcendentals=0),
        name="input_grads_other" if where else "input_grads_own",
    )(rows, turned, back, *more)


def direction(weight, first_old, second_old, gradient):
    first_new = beta_one * first_old + (1.0 - beta_one) * gradient
    second_new = beta_two * second_old + (1.0 - beta_two) * gradient * gradient
    fix_one = 1.0 - beta_one**STEP
    fix_two = 1.0 - beta_two**STEP
    update = (
        first_new / fix_one / (jnp.sqrt(second_new / fix_two) + epsilon) + weight_decay * weight
    )
    return (first_new, second_new, update)


def lane_sums(value):
    total = jnp.sum(value, axis=0, keepdims=True)
    width = total.shape[1]
    if width < LANES:
        return jnp.concatenate([total, jnp.zeros((1, LANES - width), F32)], axis=1)
    return sum(total[:, l:l + LANES] for l in range(0, width, LANES))


def direction_kernel(count, *refs):
    mine_ref, heads_ref = refs[:2]
    came = refs[2:2 + count]
    (m_ref, m1_ref, m2_ref, a_ref, a1_ref, a2_ref, h_ref, h1_ref, h2_ref,
     m1_out, m2_out, mu_out, a1_out, a2_out, au_out, h1_out, h2_out, hu_out, sums_out) = refs[2 + count:]
    own, D = m_ref.shape
    K = a_ref.shape[2]
    n_heads = h_ref.shape[0]
    grad = mine_ref[...]
    heads = heads_ref[:, :D]
    for c in came:
        grad = grad + c[:own, :].astype(F32)
        heads = heads + c[own:own + n_heads, :D].astype(F32)
    weight_rows, update_rows = [], []
    first, second, update = direction(m_ref[...], m1_ref[...], m2_ref[...], grad[:, :D])
    m1_out[...], m2_out[...], mu_out[...] = first, second, update
    weight_rows.append(lane_sums(m_ref[...] * m_ref[...]))
    update_rows.append(lane_sums(update * update))
    for k in range(3):
        first, second, update = direction(a_ref[k], a1_ref[k], a2_ref[k], grad[:, D + k * K:D + (k + 1) * K])
        a1_out[k], a2_out[k], au_out[k] = first, second, update
        weight_rows.append(lane_sums(a_ref[k] * a_ref[k]))
        update_rows.append(lane_sums(update * update))
    first, second, update = direction(h_ref[...], h1_ref[...], h2_ref[...], heads)
    h1_out[...], h2_out[...], hu_out[...] = first, second, update
    share = 1.0 / lax.axis_size("dp")
    weight_rows.append(lane_sums(h_ref[...] * h_ref[...]) * share)
    update_rows.append(lane_sums(update * update) * share)
    sums_out[...] = jnp.concatenate(weight_rows + update_rows + [jnp.zeros((6, LANES), F32)], axis=0)


def direction_call(mine, heads, came, states):
    m, a, h = states[0], states[3], states[6]
    outs = [shape(v.shape) for v in (m, m, m, a, a, a, h, h, h)] + [shape((16, LANES))]
    return pl.pallas_call(
        functools.partial(direction_kernel, len(came)),
        out_shape=tuple(outs),
        in_specs=[VMEM] * (2 + len(came) + 9),
        out_specs=tuple([VMEM] * 10),
        name="directions",
    )(mine, heads, *came, *states)


def update_kernel(count, *refs):
    sums_refs = refs[:count]
    m_ref, a_ref, h_ref, mu_ref, au_ref, hu_ref, m_out, a_out, h_out, norms_out = refs[count:]
    total = sums_refs[0][...]
    for ref in sums_refs[1:]:
        total = total + ref[...]
    norms = jnp.sqrt(jnp.sum(total, axis=1, keepdims=True))
    weight_norm, update_norm = norms[0:5], norms[5:10]
    rate = learn_rate * (weight_norm / update_norm)
    m_out[...] = m_ref[...] - rate[0:1] * mu_ref[...]
    for k in range(3):
        a_out[k] = a_ref[k] - rate[1 + k:2 + k] * au_ref[k]
    h_out[...] = h_ref[...] - rate[4:5] * hu_ref[...]
    row = jnp.sqrt(jnp.sum(total.T, axis=0, keepdims=True))
    norms_out[...] = jnp.concatenate([row[:, 0:5], row[:, 5:10]], axis=0)


def update_call(sums, m, a, h, mu, au, hu):
    return pl.pallas_call(
        functools.partial(update_kernel, len(sums)),
        out_shape=(shape(m.shape), shape(a.shape), shape(h.shape), shape((2, 5))),
        in_specs=[VMEM] * (len(sums) + 6),
        out_specs=(VMEM,) * 4,
        name="updates",
    )(*sums, m, a, h, mu, au, hu)


def bit_groups(n_dp, n_member):
    def split(low, count):
        bits = count.bit_length() - 1
        groups = []
        while bits > 0:
            take = 2 if bits >= 2 else 1
            bits -= take
            groups.append((low << bits, 1 << take))
        return groups

    return split(n_member, n_dp), split(2, n_member // 2) + [(1, 2)]


def swap(value, total, mask):
    return lax.ppermute(value, AXES, [(i, i ^ mask) for i in range(total)])


def gather_groups(value, groups, total, index):
    for axis, (low, size) in enumerate(groups):
        place = (index // low) % size
        held = [value] + [swap(value, total, low * m) for m in range(1, size)]
        value = jnp.stack([lax.select_n(place ^ p, *held) for p in range(size)], axis=axis)
    return value


def beside(sends, work, *inputs):
    values, inputs = lax.optimization_barrier(([v for v, _, _ in sends], inputs))
    came = [swap(v, total, mask) for v, (_, total, mask) in zip(values, sends)]
    done = work(*inputs)
    return lax.optimization_barrier((came, done))


def shards(n_dp, n_member, objects, counts, cotangent, matrix, matrix_first, matrix_second,
           adapters, adapter_first, adapter_second, head_weights, head_first, head_second):
    R, D = objects.shape
    K = adapters.shape[1]
    own, own_heads = matrix.shape[0], head_weights.shape[0]
    total = n_dp * n_member
    index = lax.axis_index("dp") * n_member + lax.axis_index("member")
    dp_groups, member_groups = bit_groups(n_dp, n_member)
    chip_groups = member_groups[:-1]
    turned = [v.transpose(0, 2, 1) for v in (adapters, adapter_first, adapter_second)]

    packed, q_own = pack_call(counts, matrix, turned[0], head_weights, cotangent.reshape(1, R))
    x_other = swap(objects, total, 1)
    q_other = swap(q_own, total, 1)
    full = gather_groups(packed, dp_groups + member_groups, total, index).reshape(D, -1)
    keep, sent, head_grads, preds, rows, wide_turned, back = grad_call(objects, x_other, q_own, q_other, full, K, own)

    chips = [size for _, size in chip_groups]
    head_grads = head_grads.reshape(chips + [2, own_heads, D])
    core = index % 2
    axis = len(chips)
    members = K // 2
    quarter = members // 4

    def arrange(main, heads):
        main = main.reshape([n_dp] + chips + [own, D + LANES])
        main = jnp.moveaxis(main, 0, len(chips)).reshape(chips + [n_dp * own, D + LANES])
        return jnp.concatenate([main, jnp.pad(heads, [(0, 0)] * (len(chips) + 1) + [(0, LANES)])], axis=len(chips))

    def backward(where, part, parts=1, **more):
        def work(rows, wide_turned, back, *acc):
            return back_call(rows, wide_turned, back, where, part * quarter, parts * quarter, *acc, n=quarter, **more)
        return work

    weights = (rows, wide_turned, back)
    other_heads = lax.dynamic_index_in_dim(head_grads, 1 - core, axis, keepdims=False)
    own_heads_grad = lax.dynamic_index_in_dim(head_grads, core, axis, keepdims=False)
    (came, pred_came), acc = beside(
        [(arrange(sent, other_heads.astype(BF16)), total, 1), (preds[1:2], total, 1)], backward(1, 0), *weights)
    wide = arrange(keep, own_heads_grad) + came.astype(F32)
    for axis in reversed(range(len(chips))):
        low, size = chip_groups[axis]
        place = (index // low) % size
        part = [lax.dynamic_index_in_dim(wide, place ^ m, axis, keepdims=False) for m in range(size)]
        sends = [(part[m].astype(BF16), total, low * m) for m in range(1, size)]
        if axis == len(chips) - 1:
            came, acc = beside(sends, backward(1, 1, 2), *weights, acc)
        else:
            came = [swap(*send) for send in sends]
        wide = part[0]
        for c in came:
            wide = wide + c.astype(F32)
    mine = wide[: n_dp * own].reshape([size for _, size in dp_groups] + [own, D + LANES])
    heads = wide[n_dp * own:]
    for axis in reversed(range(len(dp_groups))):
        low, size = dp_groups[axis]
        place = (index // low) % size
        part = [lax.dynamic_index_in_dim(mine, place ^ m, axis, keepdims=False) for m in range(size)]
        lead = part[0].shape[:-2]
        both = [jnp.concatenate([p.reshape(-1, D + LANES), heads], axis=0).astype(BF16) for p in part[1:]]
        sends = [(b, total, low * (m + 1)) for m, b in enumerate(both)]
        if axis == len(dp_groups) - 1:
            last, acc = beside(sends, backward(1, 3, q=q_other), *weights, acc)
        else:
            last = [swap(*send) for send in sends]
        mine = part[0]
        if axis:
            for c in last:
                mine = mine + c[:-own_heads].astype(F32).reshape(lead + (own, D + LANES))
                heads = heads + c[-own_heads:].astype(F32)
    ig_came = swap(acc, total, 1)

    states = [matrix, matrix_first, matrix_second, *turned, head_weights, head_first, head_second]
    (m_first, m_second, m_update, a_first, a_second, a_update, h_first, h_second, h_update, sums) = direction_call(
        mine, heads, last, states)

    rounds = [(1, 2)] + chip_groups[::-1] + dp_groups[::-1]
    plan = {0: backward(0, 0), 1: backward(0, 1, 2), len(rounds) - 1: backward(0, 3, q=q_own, came=ig_came)}
    pending, acc = [sums], ()
    for step, (low, size) in enumerate(rounds):
        sums = pending[0]
        for p in pending[1:]:
            sums = sums + p
        sends = [(sums, total, low * m) for m in range(1, size)]
        if step in plan:
            came, acc = beside(sends, plan[step], *weights, *acc)
            acc = (acc,)
        else:
            came = [swap(*send) for send in sends]
        pending = [sums] + list(came)
    input_grad = acc[0]
    new_matrix, new_adapters, new_heads, norm_pairs = update_call(
        pending, matrix, turned[0], head_weights, m_update, a_update, h_update)
    lane = lax.broadcasted_iota(jnp.int32, (1, R), 1)
    predictions = jnp.where(lane < counts[0], preds[0:1] + pred_came, 0.0) * (1.0 / K)

    def back_turn(v):
        return v.transpose(0, 2, 1)

    return (predictions.reshape(R), input_grad, new_matrix, m_first, m_second, back_turn(new_adapters),
            back_turn(a_first), back_turn(a_second), new_heads, h_first, h_second, norm_pairs.T)


def solution(mesh):
    n_dp, n_member = mesh.shape["dp"], mesh.shape["member"]
    rows, cols = P(AXES, None), P(None, None, AXES)
    heads = P("member", None)
    return jax.shard_map(
        functools.partial(shards, n_dp, n_member),
        mesh=mesh,
        in_specs=(rows, P(AXES), P(AXES), rows, rows, rows, cols, cols, cols, heads, heads, heads),
        out_specs=(P(AXES), rows, rows, rows, rows, cols, cols, cols, heads, heads, heads, P()),
        check_vma=False,
    )
```

```python
import functools

import jax
import jax.numpy as jnp
from jax import lax
from jax.experimental import pallas as pl
from jax.experimental.pallas import tpu as pltpu
from jax.sharding import PartitionSpec as P

LANES = 128
F32, BF16 = jnp.float32, jnp.bfloat16
STEP = 10
beta_one = 0.5
beta_two = 0.5
epsilon = 1e-06
weight_decay = 0.01
learn_rate = 0.25
AXES = ("dp", "member")
VMEM = pl.BlockSpec(memory_space=pltpu.VMEM)
SMEM = pl.BlockSpec(memory_space=pltpu.SMEM)
LIMIT = 48 * 1024 * 1024


def shape(dims, dtype=F32):
    return jax.ShapeDtypeStruct(dims, dtype)


def this_core():
    return lax.rem(lax.axis_index("member"), 2)


def pack_kernel(count_ref, matrix_ref, adapters_ref, heads_ref, cot_ref, packed_ref, q_ref):
    own, D = matrix_ref.shape
    K = adapters_ref.shape[2]
    packed_ref[:, :D] = matrix_ref[...].astype(BF16)
    parts = [adapters_ref[k] for k in range(3)] + [jnp.zeros((own, LANES - 3 * K), F32)]
    packed_ref[:, D:D + LANES] = jnp.concatenate(parts, axis=1).astype(BF16)
    L = packed_ref.shape[1] - D - LANES
    rows = []
    for t in range(own):
        h, c = divmod(t * L, D)
        rows.append(heads_ref[h:h + 1, c:c + L])
    packed_ref[:, D + LANES:] = jnp.concatenate(rows, axis=0).astype(BF16)
    lane = lax.broadcasted_iota(jnp.int32, cot_ref.shape, 1)
    q_ref[...] = jnp.where(lane < count_ref[0], cot_ref[...], 0.0) * (1.0 / K)


def pack_call(counts, matrix, adapters_t, heads, cot):
    own, D = matrix.shape
    L = heads.shape[0] * D // own
    return pl.pallas_call(
        pack_kernel,
        out_shape=(shape((own, D + LANES + L), BF16), shape(cot.shape)),
        in_specs=[SMEM, VMEM, VMEM, VMEM, VMEM],
        out_specs=(VMEM, VMEM),
        name="pack_weights",
    )(counts, matrix, adapters_t, heads, cot)


def grad_kernel(
    x0_ref, x1_ref, q0_ref, q1_ref, packed_ref,
    keep_ref, sent_ref, heads_grad_ref, pred_ref, rows_ref, turned_ref, back_ref,
    cols_ref, heads_ref, weight_ref, x_ref, xq_ref, q_ref, z0_ref, z1_ref, gp0_ref, gp1_ref,
    post_ref, pred_acc, sums_ref, gr_ref, grads_ref, *, own,
):
    half, D = x0_ref.shape
    R = 2 * half
    K = heads_grad_ref.shape[0]
    members = K // 2
    n = back_ref.shape[0]
    step_id, steps = pl.program_id(0), pl.num_programs(0)
    core = this_core()
    base = core * members
    z_refs, gp_refs = (z0_ref, z1_ref), (gp0_ref, gp1_ref)

    def set_up():
        weight_ref[...] = packed_ref[:, :D].astype(F32)
        cols = packed_ref[:, D:D + LANES].astype(F32)
        cols_ref[...] = cols
        rows_ref[...] = cols.T
        turned_ref[...] = packed_ref[:, :D].T
        L = packed_ref.shape[1] - D - LANES
        per_head = D // L
        for c in range(0, L, LANES):
            gr_ref[:K * per_head, :] = packed_ref[:K * per_head, D + LANES + c:D + 2 * LANES + c].astype(F32)
            for k in range(per_head):
                heads_ref[:, k * L + c:k * L + c + LANES] = gr_ref[pl.ds(k, K, stride=per_head), :]
        x_ref[:half, :] = x0_ref[...]
        x_ref[half:, :] = x1_ref[...]
        for side, (x_side, q_side) in enumerate(((x0_ref, q0_ref), (x1_ref, q1_ref))):
            at = slice(side * half, (side + 1) * half)
            q_row = q_side[...]
            q_ref[at, :] = jnp.broadcast_to(q_row, (LANES, half)).T
            half_q = 0.5 * q_row
            q_hi = half_q.astype(BF16)
            q_lo = (half_q - q_hi.astype(F32)).astype(BF16)
            xq_ref[:D, at] = (x_side[...].T.astype(F32) * half_q).astype(BF16)
            sub = lax.broadcasted_iota(jnp.int32, (16, half), 0)
            extra = jnp.where(sub == 0, q_hi.astype(F32), jnp.where(sub == 1, q_lo.astype(F32), 0.0))
            xq_ref[D:, at] = extra.astype(BF16)
        for ref in (pred_acc, gr_ref, sums_ref, grads_ref, gp1_ref, heads_grad_ref):
            ref[...] = jnp.zeros_like(ref)

    def forward(i, z_ref):
        r = rows_ref[pl.ds(base + i, 1), :].astype(BF16)
        z_ref[...] = jnp.dot(x_ref[...] * r, packed_ref[:, :D], preferred_element_type=F32)

    def middle(i, k, z_ref, gp_ref, lo, hi, total):
        s = 0.5 * rows_ref[pl.ds(K + base + i, 1), :]
        b = 0.5 * rows_ref[pl.ds(2 * K + base + i, 1), :]
        hb = heads_ref[pl.ds(base + i, 1), :]
        step = 16
        for c in range(lo, hi, step):
            y = z_ref[c:c + step, :] * s + b
            t = jnp.tanh(y)
            a = 1.0 + t
            h = y * a
            d = a + h * (1.0 - t)
            gp = (hb * d).astype(BF16)
            gp_ref[c:c + step, :] = gp
            back_ref[k, c:c + step, :] = gp
            hh = h * hb
            pred_acc[c:c + step, :] += sum(hh[:, l:l + LANES] for l in range(0, D, LANES))
            q = q_ref[c:c + step, :]
            qh = jnp.concatenate([h[:, l:l + LANES] * q for l in range(0, D, LANES)], axis=1)
            part = sum(qh[j:j + 8] for j in range(0, step, 8))
            total = part if total is None else total + part
        return total

    def outer(gp_ref):
        post_ref[...] = jnp.dot(xq_ref[...], gp_ref[...], preferred_element_type=F32)

    def spread(i, lo, hi, total):
        s = rows_ref[pl.ds(K + base + i, 1), :]
        step = 16
        lane = lax.broadcasted_iota(jnp.int32, (step, LANES), 1)
        for c in range(lo, hi, step):
            g = post_ref[c:c + step, :]
            r = jnp.sum(jnp.where(lane == base + i, cols_ref[c:c + step, :], 0.0), axis=1, keepdims=True)
            t = g * weight_ref[c:c + step, :]
            rt = t * r
            part = sum(rt[j:j + 8] for j in range(0, step, 8))
            total = part if total is None else total + part
            st = t * s
            fold = sum(st[:, l:l + LANES] for l in range(0, D, LANES))
            gr_ref[c:c + step, :] += jnp.where(lane == base + i, jnp.sum(fold, axis=1, keepdims=True), 0.0)
            grads_ref[c:c + step, :D] += (g * s) * r
        return total

    def finish(i, total):
        sums_ref[pl.ds(K + base + i, 1), :] = jnp.sum(total, axis=0, keepdims=True)
        sums_ref[pl.ds(2 * K + base + i, 1), :] = post_ref[D:D + 1, :] + post_ref[D + 1:D + 2, :]

    def member(i, k, now, other, nxt):
        total = middle(i, k, z_refs[now], gp_refs[now], 0, R, None)
        forward(nxt, z_refs[other])
        outer(gp_refs[other])
        heads_grad_ref[pl.ds(base + i, 1), :] = jnp.sum(total, axis=0, keepdims=True)
        finish(i - 1, spread(i - 1, 0, D, None))

    @pl.when(step_id == 0)
    def _():
        set_up()
        forward(0, z_refs[0])

    for k in range(n):
        i, now, other = step_id * n + k, k % 2, (k + 1) % 2
        member(i, k, now, other, jnp.minimum(i + 1, members - 1))

    @pl.when(step_id == steps - 1)
    def _():
        outer(gp_refs[1])
        finish(members - 1, spread(members - 1, 0, D, None))
        for side in range(2):
            at = slice(side * half, (side + 1) * half)
            pred_ref[side:side + 1, :] = jnp.sum(pred_acc[at, :].T, axis=0, keepdims=True)
        grads_ref[:, D:] = sums_ref[...].T + gr_ref[...]
        for j in range(D // (2 * own)):
            low = grads_ref[2 * j * own:(2 * j + 1) * own, :]
            high = grads_ref[(2 * j + 1) * own:(2 * j + 2) * own, :]
            keep_ref[j * own:(j + 1) * own, :] = jnp.where(core == 0, low, high)
            sent_ref[j * own:(j + 1) * own, :] = jnp.where(core == 0, high, low).astype(BF16)


def grad_call(x0, x1, q0, q1, packed, K, own, n=2):
    half, D = x0.shape
    R = 2 * half
    members = K // 2
    flops = 4 * members * R * D * D
    return pl.pallas_call(
        functools.partial(grad_kernel, own=own),
        grid=(members // n,),
        out_shape=(
            shape((D // 2, D + LANES)), shape((D // 2, D + LANES), BF16), shape((K, D)), shape((2, half)),
            shape((LANES, D)), shape((D, D), BF16), shape((members, R, D), BF16),
        ),
        in_specs=[VMEM] * 5,
        out_specs=(VMEM, VMEM, VMEM, VMEM, VMEM, VMEM, pl.BlockSpec((n, R, D), lambda i: (i, 0, 0))),
        scratch_shapes=[
            pltpu.VMEM((D, LANES), F32), pltpu.VMEM((K, D), F32), pltpu.VMEM((D, D), F32),
            pltpu.VMEM((R, D), BF16), pltpu.VMEM((D + 16, R), BF16), pltpu.VMEM((R, LANES), F32),
            pltpu.VMEM((R, D), F32), pltpu.VMEM((R, D), F32), pltpu.VMEM((R, D), BF16), pltpu.VMEM((R, D), BF16),
            pltpu.VMEM((D + 16, D), F32), pltpu.VMEM((R, LANES), F32), pltpu.VMEM((LANES, D), F32),
            pltpu.VMEM((D, LANES), F32), pltpu.VMEM((D, D + LANES), F32),
        ],
        compiler_params=pltpu.CompilerParams(vmem_limit_bytes=LIMIT),
        cost_estimate=pl.CostEstimate(flops=2 * flops, bytes_accessed=members * R * D * 2, transcendentals=members * R * D),
        name="member_grads",
    )(x0, x1, q0, q1, packed)


def back_kernel(*refs, members, start, first, last):
    rows_ref, turned_ref, gp_ref = refs[:3]
    rest = list(refs[3:])
    acc_in = None if first else rest.pop(0)
    q_ref = rest.pop(0) if last else None
    came_ref = rest.pop(0) if last == "own" else None
    out_ref, acc_ref = rest
    n, R, D = gp_ref.shape
    step = pl.program_id(0)
    K = 2 * members
    base = this_core() * members + start

    @pl.when(step == 0)
    def _():
        acc_ref[...] = jnp.zeros_like(acc_ref) if first else acc_in[...]

    left, right = [], []
    for k in range(n):
        i = base + step * n + k
        r = rows_ref[pl.ds(i, 1), :].astype(BF16)
        s = rows_ref[pl.ds(K + i, 1), :].astype(BF16)
        left.append(gp_ref[k] * s)
        right.append(turned_ref[...] * r)
    acc_ref[...] += jnp.dot(jnp.concatenate(left, axis=1), jnp.concatenate(right, axis=0), preferred_element_type=F32)

    @pl.when(step == pl.num_programs(0) - 1)
    def _():
        if not last:
            out_ref[...] = acc_ref[...]
        else:
            q_wide = jnp.broadcast_to(0.5 * q_ref[...], (LANES, R)).T
            for l in range(0, D, LANES):
                value = acc_ref[:, l:l + LANES] * q_wide
                out_ref[:, l:l + LANES] = value if came_ref is None else value + came_ref[:, l:l + LANES]


def back_call(rows, turned, back, where, start, count, acc=None, q=None, came=None, n=4):
    members, R2, D = back.shape
    R = R2 // 2
    last = None if q is None else "other" if came is None else "own"
    more = [v for v in (acc, q, came) if v is not None]
    return pl.pallas_call(
        functools.partial(back_kernel, members=members, start=start, first=acc is None, last=last),
        grid=(count // n,),
        out_shape=shape((R, D)),
        in_specs=[VMEM, VMEM, pl.BlockSpec((n, R, D), lambda i: (start // n + i, where, 0))] + [VMEM] * len(more),
        out_specs=VMEM,
        scratch_shapes=[pltpu.VMEM((R, D), F32)],
        compiler_params=pltpu.CompilerParams(vmem_limit_bytes=LIMIT),
        cost_estimate=pl.CostEstimate(flops=2 * count * R * D * D, bytes_accessed=count * R * D * 2, transcendentals=0),
        name="input_grads_other" if where else "input_grads_own",
    )(rows, turned, back, *more)


def direction(weight, first_old, second_old, gradient):
    first_new = beta_one * first_old + (1.0 - beta_one) * gradient
    second_new = beta_two * second_old + (1.0 - beta_two) * gradient * gradient
    fix_one = 1.0 - beta_one**STEP
    fix_two = 1.0 - beta_two**STEP
    update = (
        first_new / fix_one / (jnp.sqrt(second_new / fix_two) + epsilon) + weight_decay * weight
    )
    return (first_new, second_new, update)


def lane_sums(value):
    total = jnp.sum(value, axis=0, keepdims=True)
    width = total.shape[1]
    if width < LANES:
        return jnp.concatenate([total, jnp.zeros((1, LANES - width), F32)], axis=1)
    return sum(total[:, l:l + LANES] for l in range(0, width, LANES))


def direction_kernel(low, size, *refs):
    wide_ref = refs[0]
    count = size - 1
    came = refs[1:1 + count]
    (m_ref, m1_ref, m2_ref, a_ref, a1_ref, a2_ref, h_ref, h1_ref, h2_ref,
     m1_out, m2_out, mu_out, a1_out, a2_out, au_out, h1_out, h2_out, hu_out, sums_out) = refs[1 + count:]
    own, D = m_ref.shape
    K = a_ref.shape[2]
    n_heads = h_ref.shape[0]
    place = lax.rem(lax.axis_index("dp") // low, size)
    grad = wide_ref[:own, :]
    for v in range(1, size):
        grad = jnp.where(place == v, wide_ref[v * own:(v + 1) * own, :], grad)
    heads = wide_ref[size * own:size * own + n_heads, :D]
    for c in came:
        grad = grad + c[:own, :].astype(F32)
        heads = heads + c[own:own + n_heads, :D].astype(F32)
    weight_rows, update_rows = [], []
    first, second, update = direction(m_ref[...], m1_ref[...], m2_ref[...], grad[:, :D])
    m1_out[...], m2_out[...], mu_out[...] = first, second, update
    weight_rows.append(lane_sums(m_ref[...] * m_ref[...]))
    update_rows.append(lane_sums(update * update))
    for k in range(3):
        first, second, update = direction(a_ref[k], a1_ref[k], a2_ref[k], grad[:, D + k * K:D + (k + 1) * K])
        a1_out[k], a2_out[k], au_out[k] = first, second, update
        weight_rows.append(lane_sums(a_ref[k] * a_ref[k]))
        update_rows.append(lane_sums(update * update))
    first, second, update = direction(h_ref[...], h1_ref[...], h2_ref[...], heads)
    h1_out[...], h2_out[...], hu_out[...] = first, second, update
    share = 1.0 / lax.axis_size("dp")
    weight_rows.append(lane_sums(h_ref[...] * h_ref[...]) * share)
    update_rows.append(lane_sums(update * update) * share)
    sums_out[...] = jnp.concatenate(weight_rows + update_rows + [jnp.zeros((6, LANES), F32)], axis=0)


def direction_call(wide, came, low, states):
    m, a, h = states[0], states[3], states[6]
    outs = [shape(v.shape) for v in (m, m, m, a, a, a, h, h, h)] + [shape((16, LANES))]
    return pl.pallas_call(
        functools.partial(direction_kernel, low, len(came) + 1),
        out_shape=tuple(outs),
        in_specs=[VMEM] * (1 + len(came) + 9),
        out_specs=tuple([VMEM] * 10),
        name="directions",
    )(wide, *came, *states)


def update_kernel(count, *refs):
    sums_refs = refs[:count]
    m_ref, a_ref, h_ref, mu_ref, au_ref, hu_ref, m_out, a_out, h_out, norms_out = refs[count:]
    total = sums_refs[0][...]
    for ref in sums_refs[1:]:
        total = total + ref[...]
    norms = jnp.sqrt(jnp.sum(total, axis=1, keepdims=True))
    weight_norm, update_norm = norms[0:5], norms[5:10]
    rate = learn_rate * (weight_norm / update_norm)
    m_out[...] = m_ref[...] - rate[0:1] * mu_ref[...]
    for k in range(3):
        a_out[k] = a_ref[k] - rate[1 + k:2 + k] * au_ref[k]
    h_out[...] = h_ref[...] - rate[4:5] * hu_ref[...]
    row = jnp.sqrt(jnp.sum(total.T, axis=0, keepdims=True))
    norms_out[...] = jnp.concatenate([row[:, 0:5], row[:, 5:10]], axis=0)


def update_call(sums, m, a, h, mu, au, hu):
    return pl.pallas_call(
        functools.partial(update_kernel, len(sums)),
        out_shape=(shape(m.shape), shape(a.shape), shape(h.shape), shape((2, 5))),
        in_specs=[VMEM] * (len(sums) + 6),
        out_specs=(VMEM,) * 4,
        name="updates",
    )(*sums, m, a, h, mu, au, hu)


def bit_groups(n_dp, n_member):
    def split(low, count):
        bits = count.bit_length() - 1
        groups = []
        while bits > 0:
            take = 2 if bits >= 2 else 1
            bits -= take
            groups.append((low << bits, 1 << take))
        return groups

    return split(n_member, n_dp), split(2, n_member // 2) + [(1, 2)]


def swap(value, total, mask):
    return lax.ppermute(value, AXES, [(i, i ^ mask) for i in range(total)])


def gather_groups(value, groups, total, index, *also):
    brought = ()
    for axis, (low, size) in enumerate(groups):
        place = (index // low) % size
        held = [value] + [swap(value, total, low * m) for m in range(1, size)]
        if axis == 0:
            brought = tuple(swap(v, total, mask) for v, mask in also)
            held, brought = lax.optimization_barrier((held, brought))
        value = jnp.stack([lax.select_n(place ^ p, *held) for p in range(size)], axis=axis)
    return value, brought


def beside(sends, work, *inputs):
    values, inputs = lax.optimization_barrier(([v for v, _, _ in sends], inputs))
    came = [swap(v, total, mask) for v, (_, total, mask) in zip(values, sends)]
    done = work(*inputs)
    return lax.optimization_barrier((came, done))


def shards(n_dp, n_member, objects, counts, cotangent, matrix, matrix_first, matrix_second,
           adapters, adapter_first, adapter_second, head_weights, head_first, head_second):
    R, D = objects.shape
    K = adapters.shape[1]
    own, own_heads = matrix.shape[0], head_weights.shape[0]
    total = n_dp * n_member
    index = lax.axis_index("dp") * n_member + lax.axis_index("member")
    dp_groups, member_groups = bit_groups(n_dp, n_member)
    chip_groups = member_groups[:-1]
    turned = [v.transpose(0, 2, 1) for v in (adapters, adapter_first, adapter_second)]

    packed, q_own = pack_call(counts, matrix, turned[0], head_weights, cotangent.reshape(1, R))
    full, (x_other, q_other) = gather_groups(
        packed, dp_groups + member_groups, total, index, (objects, 1), (q_own, 1))
    full = full.reshape(D, -1)
    keep, sent, head_grads, preds, rows, wide_turned, back = grad_call(objects, x_other, q_own, q_other, full, K, own)

    chips = [size for _, size in chip_groups]
    head_grads = head_grads.reshape(chips + [2, own_heads, D])
    core = index % 2
    axis = len(chips)
    members = K // 2
    quarter = members // 4

    def arrange(main, heads):
        main = main.reshape([n_dp] + chips + [own, D + LANES])
        main = jnp.moveaxis(main, 0, len(chips)).reshape(chips + [n_dp * own, D + LANES])
        return jnp.concatenate([main, jnp.pad(heads, [(0, 0)] * (len(chips) + 1) + [(0, LANES)])], axis=len(chips))

    def backward(where, part, parts=1, **more):
        def work(rows, wide_turned, back, *acc):
            return back_call(rows, wide_turned, back, where, part * quarter, parts * quarter, *acc, n=quarter, **more)
        return work

    weights = (rows, wide_turned, back)
    other_heads = lax.dynamic_index_in_dim(head_grads, 1 - core, axis, keepdims=False)
    own_heads_grad = lax.dynamic_index_in_dim(head_grads, core, axis, keepdims=False)
    (came, pred_came), acc = beside(
        [(arrange(sent, other_heads.astype(BF16)), total, 1), (preds[1:2], total, 1)], backward(1, 0), *weights)
    wide = arrange(keep, own_heads_grad) + came.astype(F32)
    for axis in reversed(range(len(chips))):
        low, size = chip_groups[axis]
        place = (index // low) % size
        part = [lax.dynamic_index_in_dim(wide, place ^ m, axis, keepdims=False) for m in range(size)]
        sends = [(part[m].astype(BF16), total, low * m) for m in range(1, size)]
        if axis == len(chips) - 1:
            came, acc = beside(sends, backward(1, 1, 2), *weights, acc)
        else:
            came = [swap(*send) for send in sends]
        wide = part[0]
        for c in came:
            wide = wide + c.astype(F32)
    for axis in reversed(range(len(dp_groups))):
        low, size = dp_groups[axis]
        place = (index // low) % size
        outer_count = (wide.shape[0] - own_heads) // (own * size)
        main = wide[:-own_heads].reshape(outer_count, size * own, D + LANES)
        heads = wide[-own_heads:]

        def chunk(v):
            at = lax.dynamic_slice_in_dim(main, v * own, own, 1)
            return jnp.concatenate([at.reshape(-1, D + LANES), heads], axis=0)

        sends = [(chunk(place ^ m).astype(BF16), total, low * m) for m in range(1, size)]
        if axis == len(dp_groups) - 1:
            last, acc = beside(sends, backward(1, 3, q=q_other), *weights, acc)
        else:
            last = [swap(*send) for send in sends]
        if axis:
            wide = chunk(place)
            for c in last:
                wide = wide + c.astype(F32)
    ig_came = swap(acc, total, 1)

    states = [matrix, matrix_first, matrix_second, *turned, head_weights, head_first, head_second]
    (m_first, m_second, m_update, a_first, a_second, a_update, h_first, h_second, h_update, sums) = direction_call(
        wide, last, dp_groups[0][0] // n_member, states)

    rounds = [(1, 2)] + chip_groups[::-1] + dp_groups[::-1]
    plan = {0: backward(0, 0), 1: backward(0, 1, 2), len(rounds) - 1: backward(0, 3, q=q_own, came=ig_came)}
    pending, acc = [sums], ()
    for step, (low, size) in enumerate(rounds):
        sums = pending[0]
        for p in pending[1:]:
            sums = sums + p
        sends = [(sums, total, low * m) for m in range(1, size)]
        if step in plan:
            came, acc = beside(sends, plan[step], *weights, *acc)
            acc = (acc,)
        else:
            came = [swap(*send) for send in sends]
        pending = [sums] + list(came)
    input_grad = acc[0]
    new_matrix, new_adapters, new_heads, norm_pairs = update_call(
        pending, matrix, turned[0], head_weights, m_update, a_update, h_update)
    lane = lax.broadcasted_iota(jnp.int32, (1, R), 1)
    predictions = jnp.where(lane < counts[0], preds[0:1] + pred_came, 0.0) * (1.0 / K)

    def back_turn(v):
        return v.transpose(0, 2, 1)

    return (predictions.reshape(R), input_grad, new_matrix, m_first, m_second, back_turn(new_adapters),
            back_turn(a_first), back_turn(a_second), new_heads, h_first, h_second, norm_pairs.T)


def solution(mesh):
    n_dp, n_member = mesh.shape["dp"], mesh.shape["member"]
    rows, cols = P(AXES, None), P(None, None, AXES)
    heads = P("member", None)
    return jax.shard_map(
        functools.partial(shards, n_dp, n_member),
        mesh=mesh,
        in_specs=(rows, P(AXES), P(AXES), rows, rows, rows, cols, cols, cols, heads, heads, heads),
        out_specs=(P(AXES), rows, rows, rows, rows, cols, cols, cols, heads, heads, heads, P()),
        check_vma=False,
    )
```

```python
import functools

import jax
import jax.numpy as jnp
from jax import lax
from jax.experimental import pallas as pl
from jax.experimental.pallas import tpu as pltpu
from jax.sharding import PartitionSpec as P

LANES = 128
F32, BF16 = jnp.float32, jnp.bfloat16
STEP = 10
beta_one = 0.5
beta_two = 0.5
epsilon = 1e-06
weight_decay = 0.01
learn_rate = 0.25
AXES = ("dp", "member")
VMEM = pl.BlockSpec(memory_space=pltpu.VMEM)
SMEM = pl.BlockSpec(memory_space=pltpu.SMEM)
LIMIT = 28 * 1024 * 1024


def shape(dims, dtype=F32):
    return jax.ShapeDtypeStruct(dims, dtype)


def this_core():
    return lax.rem(lax.axis_index("member"), 2)


def pack_kernel(count_ref, matrix_ref, adapters_ref, heads_ref, cot_ref, packed_ref, q_ref):
    own, D = matrix_ref.shape
    K = adapters_ref.shape[2]
    packed_ref[:, :D] = matrix_ref[...].astype(BF16)
    parts = [adapters_ref[k] for k in range(3)] + [jnp.zeros((own, LANES - 3 * K), F32)]
    packed_ref[:, D:D + LANES] = jnp.concatenate(parts, axis=1).astype(BF16)
    L = packed_ref.shape[1] - D - LANES
    rows = []
    for t in range(own):
        h, c = divmod(t * L, D)
        rows.append(heads_ref[h:h + 1, c:c + L])
    packed_ref[:, D + LANES:] = jnp.concatenate(rows, axis=0).astype(BF16)
    lane = lax.broadcasted_iota(jnp.int32, cot_ref.shape, 1)
    q_ref[...] = jnp.where(lane < count_ref[0], cot_ref[...], 0.0) * (1.0 / K)


def pack_call(counts, matrix, adapters_t, heads, cot):
    own, D = matrix.shape
    L = heads.shape[0] * D // own
    return pl.pallas_call(
        pack_kernel,
        out_shape=(shape((own, D + LANES + L), BF16), shape(cot.shape)),
        in_specs=[SMEM, VMEM, VMEM, VMEM, VMEM],
        out_specs=(VMEM, VMEM),
        name="pack_weights",
    )(counts, matrix, adapters_t, heads, cot)


def grad_kernel(
    x_ref, rows_q_ref, packed_ref,
    keep_ref, sent_ref, heads_grad_ref, pred_ref, rows_ref, turned_ref, back_ref,
    cols_ref, heads_ref, weight_ref, xq_ref, q_ref, z0_ref, z1_ref, gp0_ref, gp1_ref,
    post_ref, pred_acc, sums_ref, gr_ref, grads_ref, *, own,
):
    R, D = x_ref.shape
    half = R // 2
    K = heads_grad_ref.shape[0]
    members = K // 2
    n = back_ref.shape[0]
    step_id, steps = pl.program_id(0), pl.num_programs(0)
    core = this_core()
    base = core * members
    z_refs, gp_refs = (z0_ref, z1_ref), (gp0_ref, gp1_ref)

    def set_up():
        weight_ref[...] = packed_ref[:, :D].astype(F32)
        cols = packed_ref[:, D:D + LANES].astype(F32)
        cols_ref[...] = cols
        rows_ref[...] = cols.T
        turned_ref[...] = packed_ref[:, :D].T
        L = packed_ref.shape[1] - D - LANES
        per_head = D // L
        for c in range(0, L, LANES):
            gr_ref[:K * per_head, :] = packed_ref[:K * per_head, D + LANES + c:D + 2 * LANES + c].astype(F32)
            for k in range(per_head):
                heads_ref[:, k * L + c:k * L + c + LANES] = gr_ref[pl.ds(k, K, stride=per_head), :]
        for ref in (pred_acc, gr_ref, sums_ref, grads_ref, gp1_ref, heads_grad_ref):
            ref[...] = jnp.zeros_like(ref)
        q_row = rows_q_ref[...]
        q_ref[...] = jnp.broadcast_to(q_row, (LANES, R)).T
        half_q = 0.5 * q_row
        q_hi = half_q.astype(BF16)
        q_lo = (half_q - q_hi.astype(F32)).astype(BF16)
        xq_ref[:D, :] = (x_ref[...].T.astype(F32) * half_q).astype(BF16)
        sub = lax.broadcasted_iota(jnp.int32, (16, R), 0)
        extra = jnp.where(sub == 0, q_hi.astype(F32), jnp.where(sub == 1, q_lo.astype(F32), 0.0))
        xq_ref[D:, :] = extra.astype(BF16)

    def forward(i, z_ref):
        r = rows_ref[pl.ds(base + i, 1), :].astype(BF16)
        z_ref[...] = jnp.dot(x_ref[...] * r, packed_ref[:, :D], preferred_element_type=F32)

    def middle(i, k, z_ref, gp_ref, lo, hi, total):
        s = 0.5 * rows_ref[pl.ds(K + base + i, 1), :]
        b = 0.5 * rows_ref[pl.ds(2 * K + base + i, 1), :]
        hb = heads_ref[pl.ds(base + i, 1), :]
        step = 16
        for c in range(lo, hi, step):
            y = z_ref[c:c + step, :] * s + b
            t = jnp.tanh(y)
            a = 1.0 + t
            h = y * a
            d = a + h * (1.0 - t)
            gp = (hb * d).astype(BF16)
            gp_ref[c:c + step, :] = gp
            back_ref[k, c:c + step, :] = gp
            hh = h * hb
            pred_acc[c:c + step, :] += sum(hh[:, l:l + LANES] for l in range(0, D, LANES))
            q = q_ref[c:c + step, :]
            qh = jnp.concatenate([h[:, l:l + LANES] * q for l in range(0, D, LANES)], axis=1)
            part = sum(qh[j:j + 8] for j in range(0, step, 8))
            total = part if total is None else total + part
        return total

    def outer(gp_ref):
        post_ref[...] = jnp.dot(xq_ref[...], gp_ref[...], preferred_element_type=F32)

    def spread(i, lo, hi, total):
        s = rows_ref[pl.ds(K + base + i, 1), :]
        step = 16
        lane = lax.broadcasted_iota(jnp.int32, (step, LANES), 1)
        for c in range(lo, hi, step):
            g = post_ref[c:c + step, :]
            r = jnp.sum(jnp.where(lane == base + i, cols_ref[c:c + step, :], 0.0), axis=1, keepdims=True)
            t = g * weight_ref[c:c + step, :]
            rt = t * r
            part = sum(rt[j:j + 8] for j in range(0, step, 8))
            total = part if total is None else total + part
            st = t * s
            fold = sum(st[:, l:l + LANES] for l in range(0, D, LANES))
            gr_ref[c:c + step, :] += jnp.where(lane == base + i, jnp.sum(fold, axis=1, keepdims=True), 0.0)
            grads_ref[c:c + step, :D] += (g * s) * r
        return total

    def finish(i, total):
        sums_ref[pl.ds(K + base + i, 1), :] = jnp.sum(total, axis=0, keepdims=True)
        sums_ref[pl.ds(2 * K + base + i, 1), :] = post_ref[D:D + 1, :] + post_ref[D + 1:D + 2, :]

    def member(i, k, now, other, nxt):
        total = middle(i, k, z_refs[now], gp_refs[now], 0, R, None)
        forward(nxt, z_refs[other])
        outer(gp_refs[other])
        heads_grad_ref[pl.ds(base + i, 1), :] = jnp.sum(total, axis=0, keepdims=True)
        finish(i - 1, spread(i - 1, 0, D, None))

    @pl.when(step_id == 0)
    def _():
        set_up()
        forward(0, z_refs[0])

    for k in range(n):
        i, now, other = step_id * n + k, k % 2, (k + 1) % 2
        member(i, k, now, other, jnp.minimum(i + 1, members - 1))

    @pl.when(step_id == steps - 1)
    def _():
        outer(gp_refs[1])
        finish(members - 1, spread(members - 1, 0, D, None))
        for side in range(2):
            at = slice(side * half, (side + 1) * half)
            pred_ref[side:side + 1, :] = jnp.sum(pred_acc[at, :].T, axis=0, keepdims=True)
        grads_ref[:, D:] = sums_ref[...].T + gr_ref[...]
        for j in range(D // (2 * own)):
            low = grads_ref[2 * j * own:(2 * j + 1) * own, :]
            high = grads_ref[(2 * j + 1) * own:(2 * j + 2) * own, :]
            keep_ref[j * own:(j + 1) * own, :] = jnp.where(core == 0, low, high)
            sent_ref[j * own:(j + 1) * own, :] = jnp.where(core == 0, high, low).astype(BF16)


def grad_call(x, q, packed, K, own, n=2):
    R, D = x.shape
    half = R // 2
    members = K // 2
    flops = 4 * members * R * D * D
    return pl.pallas_call(
        functools.partial(grad_kernel, own=own),
        grid=(members // n,),
        out_shape=(
            shape((D // 2, D + LANES)), shape((D // 2, D + LANES), BF16), shape((K, D)), shape((2, half)),
            shape((LANES, D)), shape((D, D), BF16), shape((members, R, D), BF16),
        ),
        in_specs=[VMEM] * 3,
        out_specs=(VMEM, VMEM, VMEM, VMEM, VMEM, VMEM, pl.BlockSpec((n, R, D), lambda i: (i, 0, 0))),
        scratch_shapes=[
            pltpu.VMEM((D, LANES), F32), pltpu.VMEM((K, D), F32), pltpu.VMEM((D, D), F32),
            pltpu.VMEM((D + 16, R), BF16), pltpu.VMEM((R, LANES), F32),
            pltpu.VMEM((R, D), F32), pltpu.VMEM((R, D), F32), pltpu.VMEM((R, D), BF16), pltpu.VMEM((R, D), BF16),
            pltpu.VMEM((D + 16, D), F32), pltpu.VMEM((R, LANES), F32), pltpu.VMEM((LANES, D), F32),
            pltpu.VMEM((D, LANES), F32), pltpu.VMEM((D, D + LANES), F32),
        ],
        compiler_params=pltpu.CompilerParams(vmem_limit_bytes=LIMIT),
        cost_estimate=pl.CostEstimate(flops=2 * flops, bytes_accessed=members * R * D * 2, transcendentals=members * R * D),
        name="member_grads",
    )(x, q, packed)


def back_kernel(*refs, members, start, first, last):
    rows_ref, turned_ref, gp_ref = refs[:3]
    rest = list(refs[3:])
    acc_in = None if first else rest.pop(0)
    q_ref = rest.pop(0) if last else None
    if last == "own":
        came_ref, pred_ref, pred_came_ref, count_ref = [rest.pop(0) for _ in range(4)]
        out_ref, pred_out_ref, acc_ref = rest
    else:
        came_ref = None
        out_ref, acc_ref = rest
    n, R, D = gp_ref.shape
    step = pl.program_id(0)
    K = 2 * members
    base = this_core() * members + start

    @pl.when(step == 0)
    def _():
        acc_ref[...] = jnp.zeros_like(acc_ref) if first else acc_in[...]

    left, right = [], []
    for k in range(n):
        i = base + step * n + k
        r = rows_ref[pl.ds(i, 1), :].astype(BF16)
        s = rows_ref[pl.ds(K + i, 1), :].astype(BF16)
        left.append(gp_ref[k] * s)
        right.append(turned_ref[...] * r)
    acc_ref[...] += jnp.dot(jnp.concatenate(left, axis=1), jnp.concatenate(right, axis=0), preferred_element_type=F32)

    @pl.when(step == pl.num_programs(0) - 1)
    def _():
        if not last:
            out_ref[...] = acc_ref[...]
        else:
            q_wide = jnp.broadcast_to(0.5 * q_ref[...], (LANES, R)).T
            for l in range(0, D, LANES):
                value = acc_ref[:, l:l + LANES] * q_wide
                out_ref[:, l:l + LANES] = value if came_ref is None else value + came_ref[:, l:l + LANES]
        if last == "own":
            lane = lax.broadcasted_iota(jnp.int32, (1, R), 1)
            total = pred_ref[0:1, :] + pred_came_ref[...]
            pred_out_ref[...] = jnp.where(lane < count_ref[0], total, 0.0) * (1.0 / K)


def back_call(rows, turned, back, where, start, count, acc=None, q=None, came=None, n=4):
    members, R2, D = back.shape
    R = R2 // 2
    last = None if q is None else "other" if came is None else "own"
    more = [v for v in (acc, q, *(came or ())) if v is not None]
    specs = [VMEM] * len(more)
    if last == "own":
        specs[-1] = SMEM
    return pl.pallas_call(
        functools.partial(back_kernel, members=members, start=start, first=acc is None, last=last),
        grid=(count // n,),
        out_shape=(shape((R, D)), shape((1, R))) if last == "own" else shape((R, D)),
        in_specs=[VMEM, VMEM, pl.BlockSpec((n, R, D), lambda i: (start // n + i, where, 0))] + specs,
        out_specs=(VMEM, VMEM) if last == "own" else VMEM,
        scratch_shapes=[pltpu.VMEM((R, D), F32)],
        compiler_params=pltpu.CompilerParams(vmem_limit_bytes=LIMIT),
        cost_estimate=pl.CostEstimate(flops=2 * count * R * D * D, bytes_accessed=count * R * D * 2, transcendentals=0),
        name="input_grads_other" if where else "input_grads_own",
    )(rows, turned, back, *more)


def direction(weight, first_old, second_old, gradient):
    first_new = beta_one * first_old + (1.0 - beta_one) * gradient
    second_new = beta_two * second_old + (1.0 - beta_two) * gradient * gradient
    fix_one = 1.0 - beta_one**STEP
    fix_two = 1.0 - beta_two**STEP
    update = (
        first_new / fix_one / (jnp.sqrt(second_new / fix_two) + epsilon) + weight_decay * weight
    )
    return (first_new, second_new, update)


def lane_sums(value):
    total = jnp.sum(value, axis=0, keepdims=True)
    width = total.shape[1]
    if width < LANES:
        return jnp.concatenate([total, jnp.zeros((1, LANES - width), F32)], axis=1)
    return sum(total[:, l:l + LANES] for l in range(0, width, LANES))


def direction_kernel(low, size, *refs):
    wide_ref = refs[0]
    count = size - 1
    came = refs[1:1 + count]
    (m_ref, m1_ref, m2_ref, a_ref, a1_ref, a2_ref, h_ref, h1_ref, h2_ref,
     m1_out, m2_out, mu_out, a1_out, a2_out, au_out, h1_out, h2_out, hu_out, sums_out) = refs[1 + count:]
    own, D = m_ref.shape
    K = a_ref.shape[2]
    n_heads = h_ref.shape[0]
    place = lax.rem(lax.axis_index("dp") // low, size)
    grad = wide_ref[:own, :]
    for v in range(1, size):
        grad = jnp.where(place == v, wide_ref[v * own:(v + 1) * own, :], grad)
    heads = wide_ref[size * own:size * own + n_heads, :D]
    for c in came:
        grad = grad + c[:own, :].astype(F32)
        heads = heads + c[own:own + n_heads, :D].astype(F32)
    weight_rows, update_rows = [], []
    first, second, update = direction(m_ref[...], m1_ref[...], m2_ref[...], grad[:, :D])
    m1_out[...], m2_out[...], mu_out[...] = first, second, update
    weight_rows.append(lane_sums(m_ref[...] * m_ref[...]))
    update_rows.append(lane_sums(update * update))
    for k in range(3):
        first, second, update = direction(a_ref[k], a1_ref[k], a2_ref[k], grad[:, D + k * K:D + (k + 1) * K])
        a1_out[k], a2_out[k], au_out[k] = first, second, update
        weight_rows.append(lane_sums(a_ref[k] * a_ref[k]))
        update_rows.append(lane_sums(update * update))
    first, second, update = direction(h_ref[...], h1_ref[...], h2_ref[...], heads)
    h1_out[...], h2_out[...], hu_out[...] = first, second, update
    share = 1.0 / lax.axis_size("dp")
    weight_rows.append(lane_sums(h_ref[...] * h_ref[...]) * share)
    update_rows.append(lane_sums(update * update) * share)
    sums_out[...] = jnp.concatenate(weight_rows + update_rows + [jnp.zeros((6, LANES), F32)], axis=0)


def direction_call(wide, came, low, states):
    m, a, h = states[0], states[3], states[6]
    outs = [shape(v.shape) for v in (m, m, m, a, a, a, h, h, h)] + [shape((16, LANES))]
    return pl.pallas_call(
        functools.partial(direction_kernel, low, len(came) + 1),
        out_shape=tuple(outs),
        in_specs=[VMEM] * (1 + len(came) + 9),
        out_specs=tuple([VMEM] * 10),
        name="directions",
    )(wide, *came, *states)


def update_kernel(count, *refs):
    sums_refs = refs[:count]
    m_ref, a_ref, h_ref, mu_ref, au_ref, hu_ref, m_out, a_out, h_out, norms_out = refs[count:]
    total = sums_refs[0][...]
    for ref in sums_refs[1:]:
        total = total + ref[...]
    norms = jnp.sqrt(jnp.sum(total, axis=1, keepdims=True))
    weight_norm, update_norm = norms[0:5], norms[5:10]
    rate = learn_rate * (weight_norm / update_norm)
    m_out[...] = m_ref[...] - rate[0:1] * mu_ref[...]
    for k in range(3):
        a_out[k] = a_ref[k] - rate[1 + k:2 + k] * au_ref[k]
    h_out[...] = h_ref[...] - rate[4:5] * hu_ref[...]
    row = jnp.sqrt(jnp.sum(total.T, axis=0, keepdims=True))
    norms_out[...] = jnp.concatenate([row[:, 0:5], row[:, 5:10]], axis=0)


def update_call(sums, m, a, h, mu, au, hu):
    return pl.pallas_call(
        functools.partial(update_kernel, len(sums)),
        out_shape=(shape(m.shape), shape(a.shape), shape(h.shape), shape((2, 5))),
        in_specs=[VMEM] * (len(sums) + 6),
        out_specs=(VMEM,) * 4,
        name="updates",
    )(*sums, m, a, h, mu, au, hu)


def bit_groups(n_dp, n_member):
    def split(low, count):
        bits = count.bit_length() - 1
        groups = []
        while bits > 0:
            take = 2 if bits >= 2 else 1
            bits -= take
            groups.append((low << bits, 1 << take))
        return groups

    return split(n_member, n_dp), split(2, n_member // 2) + [(1, 2)]


def swap(value, total, mask):
    return lax.ppermute(value, AXES, [(i, i ^ mask) for i in range(total)])


def gather_groups(value, groups, total, index, objects, q):
    rows = (objects, q)
    for axis, (low, size) in enumerate(groups):
        place = (index // low) % size
        held = [value] + [swap(value, total, low * m) for m in range(1, size)]
        if axis == 0:
            rows = rows + tuple(swap(v, total, 1) for v in rows)
            held, rows = lax.optimization_barrier((held, rows))
        elif axis == 1:
            rows = (jnp.concatenate([rows[0], rows[2]], axis=0), jnp.concatenate([rows[1], rows[3]], axis=1))
            held, rows = lax.optimization_barrier((held, rows))
        value = jnp.stack([lax.select_n(place ^ p, *held) for p in range(size)], axis=axis)
    return (value,) + rows


def beside(sends, work, *inputs):
    values, inputs = lax.optimization_barrier(([v for v, _, _ in sends], inputs))
    came = [swap(v, total, mask) for v, (_, total, mask) in zip(values, sends)]
    done = work(*inputs)
    return lax.optimization_barrier((came, done))


def shards(n_dp, n_member, objects, counts, cotangent, matrix, matrix_first, matrix_second,
           adapters, adapter_first, adapter_second, head_weights, head_first, head_second):
    R, D = objects.shape
    K = adapters.shape[1]
    own, own_heads = matrix.shape[0], head_weights.shape[0]
    total = n_dp * n_member
    index = lax.axis_index("dp") * n_member + lax.axis_index("member")
    dp_groups, member_groups = bit_groups(n_dp, n_member)
    chip_groups = member_groups[:-1]
    turned = [v.transpose(0, 2, 1) for v in (adapters, adapter_first, adapter_second)]

    packed, q_own = pack_call(counts, matrix, turned[0], head_weights, cotangent.reshape(1, R))
    full, x_both, q_both = gather_groups(packed, dp_groups + member_groups, total, index, objects, q_own)
    full = full.reshape(D, -1)
    q_other = q_both[:, R:]
    keep, sent, head_grads, preds, rows, wide_turned, back = grad_call(x_both, q_both, full, K, own)

    chips = [size for _, size in chip_groups]
    head_grads = head_grads.reshape(chips + [2, own_heads, D])
    core = index % 2
    axis = len(chips)
    members = K // 2
    quarter = members // 4

    def arrange(main, heads):
        main = main.reshape([n_dp] + chips + [own, D + LANES])
        main = jnp.moveaxis(main, 0, len(chips)).reshape(chips + [n_dp * own, D + LANES])
        return jnp.concatenate([main, jnp.pad(heads, [(0, 0)] * (len(chips) + 1) + [(0, LANES)])], axis=len(chips))

    def backward(where, part, parts=1, **more):
        def work(rows, wide_turned, back, *acc):
            return back_call(rows, wide_turned, back, where, part * quarter, parts * quarter, *acc, n=1, **more)
        return work

    weights = (rows, wide_turned, back)
    other_heads = lax.dynamic_index_in_dim(head_grads, 1 - core, axis, keepdims=False)
    own_heads_grad = lax.dynamic_index_in_dim(head_grads, core, axis, keepdims=False)
    (came, pred_came), acc = beside(
        [(arrange(sent, other_heads.astype(BF16)), total, 1), (preds[1:2], total, 1)], backward(1, 0), *weights)
    wide = arrange(keep, own_heads_grad) + came.astype(F32)
    for axis in reversed(range(len(chips))):
        low, size = chip_groups[axis]
        place = (index // low) % size
        part = [lax.dynamic_index_in_dim(wide, place ^ m, axis, keepdims=False) for m in range(size)]
        sends = [(part[m].astype(BF16), total, low * m) for m in range(1, size)]
        if axis == len(chips) - 1:
            came, acc = beside(sends, backward(1, 1, 2), *weights, acc)
        else:
            came = [swap(*send) for send in sends]
        wide = part[0]
        for c in came:
            wide = wide + c.astype(F32)
    for axis in reversed(range(len(dp_groups))):
        low, size = dp_groups[axis]
        place = (index // low) % size
        outer_count = (wide.shape[0] - own_heads) // (own * size)
        main = wide[:-own_heads].reshape(outer_count, size * own, D + LANES)
        heads = wide[-own_heads:]

        def chunk(v):
            at = lax.dynamic_slice_in_dim(main, v * own, own, 1)
            return jnp.concatenate([at.reshape(-1, D + LANES), heads], axis=0)

        sends = [(chunk(place ^ m).astype(BF16), total, low * m) for m in range(1, size)]
        if axis == len(dp_groups) - 1:
            last, acc = beside(sends, backward(1, 3, q=q_other), *weights, acc)
        else:
            last = [swap(*send) for send in sends]
        if axis:
            wide = chunk(place)
            for c in last:
                wide = wide + c.astype(F32)
    ig_came = swap(acc, total, 1)

    states = [matrix, matrix_first, matrix_second, *turned, head_weights, head_first, head_second]
    (m_first, m_second, m_update, a_first, a_second, a_update, h_first, h_second, h_update, sums) = direction_call(
        wide, last, dp_groups[0][0] // n_member, states)

    rounds = [(1, 2)] + chip_groups[::-1] + dp_groups[::-1]
    plan = {0: backward(0, 0), 1: backward(0, 1, 2), len(rounds) - 1: backward(0, 3, q=q_own, came=(ig_came, preds, pred_came, counts))}
    pending, acc = [sums], ()
    for step, (low, size) in enumerate(rounds):
        sums = pending[0]
        for p in pending[1:]:
            sums = sums + p
        sends = [(sums, total, low * m) for m in range(1, size)]
        if step in plan:
            came, acc = beside(sends, plan[step], *weights, *acc)
            acc = (acc,)
        else:
            came = [swap(*send) for send in sends]
        pending = [sums] + list(came)
    input_grad, predictions = acc[0]
    new_matrix, new_adapters, new_heads, norm_pairs = update_call(
        pending, matrix, turned[0], head_weights, m_update, a_update, h_update)

    def back_turn(v):
        return v.transpose(0, 2, 1)

    return (predictions.reshape(R), input_grad, new_matrix, m_first, m_second, back_turn(new_adapters),
            back_turn(a_first), back_turn(a_second), new_heads, h_first, h_second, norm_pairs.T)


def solution(mesh):
    n_dp, n_member = mesh.shape["dp"], mesh.shape["member"]
    rows, cols = P(AXES, None), P(None, None, AXES)
    heads = P("member", None)
    return jax.shard_map(
        functools.partial(shards, n_dp, n_member),
        mesh=mesh,
        in_specs=(rows, P(AXES), P(AXES), rows, rows, rows, cols, cols, cols, heads, heads, heads),
        out_specs=(P(AXES), rows, rows, rows, rows, cols, cols, cols, heads, heads, heads, P()),
        check_vma=False,
    )
```

```python
import functools

import jax
import jax.numpy as jnp
from jax import lax
from jax.experimental import pallas as pl
from jax.experimental.pallas import tpu as pltpu
from jax.sharding import PartitionSpec as P

LANES = 128
F32, BF16 = jnp.float32, jnp.bfloat16
STEP = 10
beta_one = 0.5
beta_two = 0.5
epsilon = 1e-06
weight_decay = 0.01
learn_rate = 0.25
AXES = ("dp", "member")
VMEM = pl.BlockSpec(memory_space=pltpu.VMEM)
SMEM = pl.BlockSpec(memory_space=pltpu.SMEM)
LIMIT = 48 * 1024 * 1024


def shape(dims, dtype=F32):
    return jax.ShapeDtypeStruct(dims, dtype)


def this_core():
    return lax.rem(lax.axis_index("member"), 2)


def pack_kernel(count_ref, matrix_ref, adapters_ref, heads_ref, cot_ref, packed_ref, q_ref):
    own, D = matrix_ref.shape
    K = adapters_ref.shape[2]
    packed_ref[:, :D] = matrix_ref[...].astype(BF16)
    parts = [adapters_ref[k] for k in range(3)] + [jnp.zeros((own, LANES - 3 * K), F32)]
    packed_ref[:, D:D + LANES] = jnp.concatenate(parts, axis=1).astype(BF16)
    L = packed_ref.shape[1] - D - LANES
    rows = []
    for t in range(own):
        h, c = divmod(t * L, D)
        rows.append(heads_ref[h:h + 1, c:c + L])
    packed_ref[:, D + LANES:] = jnp.concatenate(rows, axis=0).astype(BF16)
    lane = lax.broadcasted_iota(jnp.int32, cot_ref.shape, 1)
    q_ref[...] = jnp.where(lane < count_ref[0], cot_ref[...], 0.0) * (1.0 / K)


def pack_call(counts, matrix, adapters_t, heads, cot):
    own, D = matrix.shape
    L = heads.shape[0] * D // own
    return pl.pallas_call(
        pack_kernel,
        out_shape=(shape((own, D + LANES + L), BF16), shape(cot.shape)),
        in_specs=[SMEM, VMEM, VMEM, VMEM, VMEM],
        out_specs=(VMEM, VMEM),
        name="pack_weights",
    )(counts, matrix, adapters_t, heads, cot)


def grad_kernel(
    x_ref, rows_q_ref, packed_ref,
    keep_ref, sent_ref, heads_grad_ref, pred_ref, rows_ref, turned_ref, back_ref,
    cols_ref, heads_ref, weight_ref, xq_ref, q_ref, z0_ref, z1_ref, gp0_ref, gp1_ref,
    post_ref, pred_acc, sums_ref, gr_ref, grads_ref, *, own,
):
    R, D = x_ref.shape
    half = R // 2
    K = heads_grad_ref.shape[0]
    members = K // 2
    n = back_ref.shape[0]
    step_id, steps = pl.program_id(0), pl.num_programs(0)
    core = this_core()
    base = core * members
    z_refs, gp_refs = (z0_ref, z1_ref), (gp0_ref, gp1_ref)

    def set_up():
        weight_ref[...] = packed_ref[:, :D].astype(F32)
        cols = packed_ref[:, D:D + LANES].astype(F32)
        cols_ref[...] = cols
        rows_ref[...] = cols.T
        turned_ref[...] = packed_ref[:, :D].T
        L = packed_ref.shape[1] - D - LANES
        per_head = D // L
        for c in range(0, L, LANES):
            gr_ref[:K * per_head, :] = packed_ref[:K * per_head, D + LANES + c:D + 2 * LANES + c].astype(F32)
            for k in range(per_head):
                heads_ref[:, k * L + c:k * L + c + LANES] = gr_ref[pl.ds(k, K, stride=per_head), :]
        for ref in (pred_acc, gr_ref, sums_ref, grads_ref, gp1_ref, heads_grad_ref):
            ref[...] = jnp.zeros_like(ref)
        q_row = rows_q_ref[...]
        q_ref[...] = jnp.broadcast_to(q_row, (LANES, R)).T
        half_q = 0.5 * q_row
        q_hi = half_q.astype(BF16)
        q_lo = (half_q - q_hi.astype(F32)).astype(BF16)
        xq_ref[:D, :] = (x_ref[...].T.astype(F32) * half_q).astype(BF16)
        sub = lax.broadcasted_iota(jnp.int32, (16, R), 0)
        extra = jnp.where(sub == 0, q_hi.astype(F32), jnp.where(sub == 1, q_lo.astype(F32), 0.0))
        xq_ref[D:, :] = extra.astype(BF16)

    def forward(i, z_ref):
        r = rows_ref[pl.ds(base + i, 1), :].astype(BF16)
        z_ref[...] = jnp.dot(x_ref[...] * r, packed_ref[:, :D], preferred_element_type=F32)

    def middle(i, k, z_ref, gp_ref, lo, hi, total):
        s = 0.5 * rows_ref[pl.ds(K + base + i, 1), :]
        b = 0.5 * rows_ref[pl.ds(2 * K + base + i, 1), :]
        hb = heads_ref[pl.ds(base + i, 1), :]
        step = 16
        for c in range(lo, hi, step):
            y = z_ref[c:c + step, :] * s + b
            t = jnp.tanh(y)
            a = 1.0 + t
            h = y * a
            d = a + h * (1.0 - t)
            gp = (hb * d).astype(BF16)
            gp_ref[c:c + step, :] = gp
            back_ref[k, c:c + step, :] = gp
            hh = h * hb
            pred_acc[c:c + step, :] += sum(hh[:, l:l + LANES] for l in range(0, D, LANES))
            q = q_ref[c:c + step, :]
            qh = jnp.concatenate([h[:, l:l + LANES] * q for l in range(0, D, LANES)], axis=1)
            part = sum(qh[j:j + 8] for j in range(0, step, 8))
            total = part if total is None else total + part
        return total

    def outer(gp_ref):
        post_ref[...] = jnp.dot(xq_ref[...], gp_ref[...], preferred_element_type=F32)

    def spread(i, lo, hi, total):
        s = rows_ref[pl.ds(K + base + i, 1), :]
        step = 16
        lane = lax.broadcasted_iota(jnp.int32, (step, LANES), 1)
        for c in range(lo, hi, step):
            g = post_ref[c:c + step, :]
            r = jnp.sum(jnp.where(lane == base + i, cols_ref[c:c + step, :], 0.0), axis=1, keepdims=True)
            t = g * weight_ref[c:c + step, :]
            rt = t * r
            part = sum(rt[j:j + 8] for j in range(0, step, 8))
            total = part if total is None else total + part
            st = t * s
            fold = sum(st[:, l:l + LANES] for l in range(0, D, LANES))
            gr_ref[c:c + step, :] += jnp.where(lane == base + i, jnp.sum(fold, axis=1, keepdims=True), 0.0)
            grads_ref[c:c + step, :D] += (g * s) * r
        return total

    def finish(i, total):
        sums_ref[pl.ds(K + base + i, 1), :] = jnp.sum(total, axis=0, keepdims=True)
        sums_ref[pl.ds(2 * K + base + i, 1), :] = post_ref[D:D + 1, :] + post_ref[D + 1:D + 2, :]

    def member(i, k, now, other, nxt):
        total = middle(i, k, z_refs[now], gp_refs[now], 0, R, None)
        forward(nxt, z_refs[other])
        outer(gp_refs[other])
        heads_grad_ref[pl.ds(base + i, 1), :] = jnp.sum(total, axis=0, keepdims=True)
        finish(i - 1, spread(i - 1, 0, D, None))

    @pl.when(step_id == 0)
    def _():
        set_up()
        forward(0, z_refs[0])

    for k in range(n):
        i, now, other = step_id * n + k, k % 2, (k + 1) % 2
        member(i, k, now, other, jnp.minimum(i + 1, members - 1))

    @pl.when(step_id == steps - 1)
    def _():
        outer(gp_refs[1])
        finish(members - 1, spread(members - 1, 0, D, None))
        for side in range(2):
            at = slice(side * half, (side + 1) * half)
            pred_ref[side:side + 1, :] = jnp.sum(pred_acc[at, :].T, axis=0, keepdims=True)
        grads_ref[:, D:] = sums_ref[...].T + gr_ref[...]
        for j in range(D // (2 * own)):
            low = grads_ref[2 * j * own:(2 * j + 1) * own, :]
            high = grads_ref[(2 * j + 1) * own:(2 * j + 2) * own, :]
            keep_ref[j * own:(j + 1) * own, :] = jnp.where(core == 0, low, high)
            sent_ref[j * own:(j + 1) * own, :] = jnp.where(core == 0, high, low).astype(BF16)


def grad_call(x, q, packed, K, own, n=2):
    R, D = x.shape
    half = R // 2
    members = K // 2
    flops = 4 * members * R * D * D
    return pl.pallas_call(
        functools.partial(grad_kernel, own=own),
        grid=(members // n,),
        out_shape=(
            shape((D // 2, D + LANES)), shape((D // 2, D + LANES), BF16), shape((K, D)), shape((2, half)),
            shape((LANES, D)), shape((D, D), BF16), shape((members, R, D), BF16),
        ),
        in_specs=[VMEM] * 3,
        out_specs=(VMEM, VMEM, VMEM, VMEM, VMEM, VMEM, pl.BlockSpec((n, R, D), lambda i: (i, 0, 0))),
        scratch_shapes=[
            pltpu.VMEM((D, LANES), F32), pltpu.VMEM((K, D), F32), pltpu.VMEM((D, D), F32),
            pltpu.VMEM((D + 16, R), BF16), pltpu.VMEM((R, LANES), F32),
            pltpu.VMEM((R, D), F32), pltpu.VMEM((R, D), F32), pltpu.VMEM((R, D), BF16), pltpu.VMEM((R, D), BF16),
            pltpu.VMEM((D + 16, D), F32), pltpu.VMEM((R, LANES), F32), pltpu.VMEM((LANES, D), F32),
            pltpu.VMEM((D, LANES), F32), pltpu.VMEM((D, D + LANES), F32),
        ],
        compiler_params=pltpu.CompilerParams(vmem_limit_bytes=LIMIT),
        cost_estimate=pl.CostEstimate(flops=2 * flops, bytes_accessed=members * R * D * 2, transcendentals=members * R * D),
        name="member_grads",
    )(x, q, packed)


def back_kernel(*refs, members, start, first, last):
    rows_ref, turned_ref, gp_ref = refs[:3]
    rest = list(refs[3:])
    acc_in = None if first else rest.pop(0)
    q_ref = rest.pop(0) if last else None
    if last == "own":
        came_ref, pred_ref, pred_came_ref, count_ref = [rest.pop(0) for _ in range(4)]
        out_ref, pred_out_ref, acc_ref = rest
    else:
        came_ref = None
        out_ref, acc_ref = rest
    n, R, D = gp_ref.shape
    step = pl.program_id(0)
    K = 2 * members
    base = this_core() * members + start

    @pl.when(step == 0)
    def _():
        acc_ref[...] = jnp.zeros_like(acc_ref) if first else acc_in[...]

    left, right = [], []
    for k in range(n):
        i = base + step * n + k
        r = rows_ref[pl.ds(i, 1), :].astype(BF16)
        s = rows_ref[pl.ds(K + i, 1), :].astype(BF16)
        left.append(gp_ref[k] * s)
        right.append(turned_ref[...] * r)
    acc_ref[...] += jnp.dot(jnp.concatenate(left, axis=1), jnp.concatenate(right, axis=0), preferred_element_type=F32)

    @pl.when(step == pl.num_programs(0) - 1)
    def _():
        if not last:
            out_ref[...] = acc_ref[...]
        else:
            q_wide = jnp.broadcast_to(0.5 * q_ref[...], (LANES, R)).T
            for l in range(0, D, LANES):
                value = acc_ref[:, l:l + LANES] * q_wide
                out_ref[:, l:l + LANES] = value if came_ref is None else value + came_ref[:, l:l + LANES]
        if last == "own":
            lane = lax.broadcasted_iota(jnp.int32, (1, R), 1)
            total = pred_ref[0:1, :] + pred_came_ref[...]
            pred_out_ref[...] = jnp.where(lane < count_ref[0], total, 0.0) * (1.0 / K)


def back_call(rows, turned, back, where, start, count, acc=None, q=None, came=None, n=4):
    members, R2, D = back.shape
    R = R2 // 2
    last = None if q is None else "other" if came is None else "own"
    more = [v for v in (acc, q, *(came or ())) if v is not None]
    specs = [VMEM] * len(more)
    if last == "own":
        specs[-1] = SMEM
    return pl.pallas_call(
        functools.partial(back_kernel, members=members, start=start, first=acc is None, last=last),
        grid=(count // n,),
        out_shape=(shape((R, D)), shape((1, R))) if last == "own" else shape((R, D)),
        in_specs=[VMEM, VMEM, pl.BlockSpec((n, R, D), lambda i: (start // n + i, where, 0))] + specs,
        out_specs=(VMEM, VMEM) if last == "own" else VMEM,
        scratch_shapes=[pltpu.VMEM((R, D), F32)],
        compiler_params=pltpu.CompilerParams(vmem_limit_bytes=LIMIT),
        cost_estimate=pl.CostEstimate(flops=2 * count * R * D * D, bytes_accessed=count * R * D * 2, transcendentals=0),
        name="input_grads_other" if where else "input_grads_own",
    )(rows, turned, back, *more)


def direction(weight, first_old, second_old, gradient):
    first_new = beta_one * first_old + (1.0 - beta_one) * gradient
    second_new = beta_two * second_old + (1.0 - beta_two) * gradient * gradient
    fix_one = 1.0 - beta_one**STEP
    fix_two = 1.0 - beta_two**STEP
    update = (
        first_new / fix_one / (jnp.sqrt(second_new / fix_two) + epsilon) + weight_decay * weight
    )
    return (first_new, second_new, update)


def lane_sums(value):
    total = jnp.sum(value, axis=0, keepdims=True)
    width = total.shape[1]
    if width < LANES:
        return jnp.concatenate([total, jnp.zeros((1, LANES - width), F32)], axis=1)
    return sum(total[:, l:l + LANES] for l in range(0, width, LANES))


def direction_kernel(low, size, *refs):
    wide_ref = refs[0]
    count = size - 1
    came = refs[1:1 + count]
    (m_ref, m1_ref, m2_ref, a_ref, a1_ref, a2_ref, h_ref, h1_ref, h2_ref,
     m1_out, m2_out, mu_out, a1_out, a2_out, au_out, h1_out, h2_out, hu_out, sums_out) = refs[1 + count:]
    own, D = m_ref.shape
    K = a_ref.shape[2]
    n_heads = h_ref.shape[0]
    place = lax.rem(lax.axis_index("dp") // low, size)
    grad = wide_ref[:own, :]
    for v in range(1, size):
        grad = jnp.where(place == v, wide_ref[v * own:(v + 1) * own, :], grad)
    heads = wide_ref[size * own:size * own + n_heads, :D]
    for c in came:
        grad = grad + c[:own, :].astype(F32)
        heads = heads + c[own:own + n_heads, :D].astype(F32)
    weight_rows, update_rows = [], []
    first, second, update = direction(m_ref[...], m1_ref[...], m2_ref[...], grad[:, :D])
    m1_out[...], m2_out[...], mu_out[...] = first, second, update
    weight_rows.append(lane_sums(m_ref[...] * m_ref[...]))
    update_rows.append(lane_sums(update * update))
    for k in range(3):
        first, second, update = direction(a_ref[k], a1_ref[k], a2_ref[k], grad[:, D + k * K:D + (k + 1) * K])
        a1_out[k], a2_out[k], au_out[k] = first, second, update
        weight_rows.append(lane_sums(a_ref[k] * a_ref[k]))
        update_rows.append(lane_sums(update * update))
    first, second, update = direction(h_ref[...], h1_ref[...], h2_ref[...], heads)
    h1_out[...], h2_out[...], hu_out[...] = first, second, update
    share = 1.0 / lax.axis_size("dp")
    weight_rows.append(lane_sums(h_ref[...] * h_ref[...]) * share)
    update_rows.append(lane_sums(update * update) * share)
    sums_out[...] = jnp.concatenate(weight_rows + update_rows + [jnp.zeros((6, LANES), F32)], axis=0)


def direction_call(wide, came, low, states):
    m, a, h = states[0], states[3], states[6]
    outs = [shape(v.shape) for v in (m, m, m, a, a, a, h, h, h)] + [shape((16, LANES))]
    return pl.pallas_call(
        functools.partial(direction_kernel, low, len(came) + 1),
        out_shape=tuple(outs),
        in_specs=[VMEM] * (1 + len(came) + 9),
        out_specs=tuple([VMEM] * 10),
        name="directions",
    )(wide, *came, *states)


def update_kernel(count, *refs):
    sums_refs = refs[:count]
    m_ref, a_ref, h_ref, mu_ref, au_ref, hu_ref, m_out, a_out, h_out, norms_out = refs[count:]
    total = sums_refs[0][...]
    for ref in sums_refs[1:]:
        total = total + ref[...]
    norms = jnp.sqrt(jnp.sum(total, axis=1, keepdims=True))
    weight_norm, update_norm = norms[0:5], norms[5:10]
    rate = learn_rate * (weight_norm / update_norm)
    m_out[...] = m_ref[...] - rate[0:1] * mu_ref[...]
    for k in range(3):
        a_out[k] = a_ref[k] - rate[1 + k:2 + k] * au_ref[k]
    h_out[...] = h_ref[...] - rate[4:5] * hu_ref[...]
    row = jnp.sqrt(jnp.sum(total.T, axis=0, keepdims=True))
    norms_out[...] = jnp.concatenate([row[:, 0:5], row[:, 5:10]], axis=0)


def update_call(sums, m, a, h, mu, au, hu):
    return pl.pallas_call(
        functools.partial(update_kernel, len(sums)),
        out_shape=(shape(m.shape), shape(a.shape), shape(h.shape), shape((2, 5))),
        in_specs=[VMEM] * (len(sums) + 6),
        out_specs=(VMEM,) * 4,
        name="updates",
    )(*sums, m, a, h, mu, au, hu)


def bit_groups(n_dp, n_member):
    def split(low, count):
        bits = count.bit_length() - 1
        groups = []
        while bits > 0:
            take = 2 if bits >= 2 else 1
            bits -= take
            groups.append((low << bits, 1 << take))
        return groups

    return split(n_member, n_dp), split(2, n_member // 2) + [(1, 2)]


def swap(value, total, mask):
    return lax.ppermute(value, AXES, [(i, i ^ mask) for i in range(total)])


def gather_groups(value, groups, total, index, objects, q):
    rows = (objects, q)
    for axis, (low, size) in enumerate(groups):
        place = (index // low) % size
        held = [value] + [swap(value, total, low * m) for m in range(1, size)]
        if axis == 0:
            rows = rows + tuple(swap(v, total, 1) for v in rows)
            held, rows = lax.optimization_barrier((held, rows))
        elif axis == 1:
            rows = (jnp.concatenate([rows[0], rows[2]], axis=0), jnp.concatenate([rows[1], rows[3]], axis=1))
            held, rows = lax.optimization_barrier((held, rows))
        value = jnp.stack([lax.select_n(place ^ p, *held) for p in range(size)], axis=axis)
    return (value,) + rows


def beside(sends, work, *inputs):
    values, inputs = lax.optimization_barrier(([v for v, _, _ in sends], inputs))
    came = [swap(v, total, mask) for v, (_, total, mask) in zip(values, sends)]
    done = work(*inputs)
    return lax.optimization_barrier((came, done))


def shards(n_dp, n_member, objects, counts, cotangent, matrix, matrix_first, matrix_second,
           adapters, adapter_first, adapter_second, head_weights, head_first, head_second):
    R, D = objects.shape
    K = adapters.shape[1]
    own, own_heads = matrix.shape[0], head_weights.shape[0]
    total = n_dp * n_member
    index = lax.axis_index("dp") * n_member + lax.axis_index("member")
    dp_groups, member_groups = bit_groups(n_dp, n_member)
    chip_groups = member_groups[:-1]
    turned = [v.transpose(0, 2, 1) for v in (adapters, adapter_first, adapter_second)]

    packed, q_own = pack_call(counts, matrix, turned[0], head_weights, cotangent.reshape(1, R))
    full, x_both, q_both = gather_groups(packed, dp_groups + member_groups, total, index, objects, q_own)
    full = full.reshape(D, -1)
    q_other = q_both[:, R:]
    keep, sent, head_grads, preds, rows, wide_turned, back = grad_call(x_both, q_both, full, K, own)

    chips = [size for _, size in chip_groups]
    head_grads = head_grads.reshape(chips + [2, own_heads, D])
    core = index % 2
    axis = len(chips)
    members = K // 2
    quarter = members // 4

    def arrange(main, heads):
        main = main.reshape([n_dp] + chips + [own, D + LANES])
        main = jnp.moveaxis(main, 0, len(chips)).reshape(chips + [n_dp * own, D + LANES])
        return jnp.concatenate([main, jnp.pad(heads, [(0, 0)] * (len(chips) + 1) + [(0, LANES)])], axis=len(chips))

    def backward(where, part, parts=1, **more):
        def work(rows, wide_turned, back, *acc):
            return back_call(rows, wide_turned, back, where, part * quarter, parts * quarter, *acc, n=2, **more)
        return work

    weights = (rows, wide_turned, back)
    other_heads = lax.dynamic_index_in_dim(head_grads, 1 - core, axis, keepdims=False)
    own_heads_grad = lax.dynamic_index_in_dim(head_grads, core, axis, keepdims=False)
    (came, pred_came), acc = beside(
        [(arrange(sent, other_heads.astype(BF16)), total, 1), (preds[1:2], total, 1)], backward(1, 0), *weights)
    wide = arrange(keep, own_heads_grad) + came.astype(F32)
    for axis in reversed(range(len(chips))):
        low, size = chip_groups[axis]
        place = (index // low) % size
        part = [lax.dynamic_index_in_dim(wide, place ^ m, axis, keepdims=False) for m in range(size)]
        sends = [(part[m].astype(BF16), total, low * m) for m in range(1, size)]
        if axis == len(chips) - 1:
            came, acc = beside(sends, backward(1, 1, 2), *weights, acc)
        else:
            came = [swap(*send) for send in sends]
        wide = part[0]
        for c in came:
            wide = wide + c.astype(F32)
    for axis in reversed(range(len(dp_groups))):
        low, size = dp_groups[axis]
        place = (index // low) % size
        outer_count = (wide.shape[0] - own_heads) // (own * size)
        main = wide[:-own_heads].reshape(outer_count, size * own, D + LANES)
        heads = wide[-own_heads:]

        def chunk(v):
            at = lax.dynamic_slice_in_dim(main, v * own, own, 1)
            return jnp.concatenate([at.reshape(-1, D + LANES), heads], axis=0)

        sends = [(chunk(place ^ m).astype(BF16), total, low * m) for m in range(1, size)]
        if axis == len(dp_groups) - 1:
            last, acc = beside(sends, backward(1, 3, q=q_other), *weights, acc)
        else:
            last = [swap(*send) for send in sends]
        if axis:
            wide = chunk(place)
            for c in last:
                wide = wide + c.astype(F32)
    ig_came = swap(acc, total, 1)

    states = [matrix, matrix_first, matrix_second, *turned, head_weights, head_first, head_second]
    (m_first, m_second, m_update, a_first, a_second, a_update, h_first, h_second, h_update, sums) = direction_call(
        wide, last, dp_groups[0][0] // n_member, states)

    rounds = [(1, 2)] + chip_groups[::-1] + dp_groups[::-1]
    plan = {0: backward(0, 0), 1: backward(0, 1, 2), len(rounds) - 1: backward(0, 3, q=q_own, came=(ig_came, preds, pred_came, counts))}
    pending, acc = [sums], ()
    for step, (low, size) in enumerate(rounds):
        sums = pending[0]
        for p in pending[1:]:
            sums = sums + p
        sends = [(sums, total, low * m) for m in range(1, size)]
        if step in plan:
            came, acc = beside(sends, plan[step], *weights, *acc)
            acc = (acc,)
        else:
            came = [swap(*send) for send in sends]
        pending = [sums] + list(came)
    input_grad, predictions = acc[0]
    new_matrix, new_adapters, new_heads, norm_pairs = update_call(
        pending, matrix, turned[0], head_weights, m_update, a_update, h_update)

    def back_turn(v):
        return v.transpose(0, 2, 1)

    return (predictions.reshape(R), input_grad, new_matrix, m_first, m_second, back_turn(new_adapters),
            back_turn(a_first), back_turn(a_second), new_heads, h_first, h_second, norm_pairs.T)


def solution(mesh):
    n_dp, n_member = mesh.shape["dp"], mesh.shape["member"]
    rows, cols = P(AXES, None), P(None, None, AXES)
    heads = P("member", None)
    return jax.shard_map(
        functools.partial(shards, n_dp, n_member),
        mesh=mesh,
        in_specs=(rows, P(AXES), P(AXES), rows, rows, rows, cols, cols, cols, heads, heads, heads),
        out_specs=(P(AXES), rows, rows, rows, rows, cols, cols, cols, heads, heads, heads, P()),
        check_vma=False,
    )
```

```python
import functools

import jax
import jax.numpy as jnp
from jax import lax
from jax.experimental import pallas as pl
from jax.experimental.pallas import tpu as pltpu
from jax.sharding import PartitionSpec as P

LANES = 128
F32, BF16 = jnp.float32, jnp.bfloat16
STEP = 10
beta_one = 0.5
beta_two = 0.5
epsilon = 1e-06
weight_decay = 0.01
learn_rate = 0.25
AXES = ("dp", "member")
VMEM = pl.BlockSpec(memory_space=pltpu.VMEM)
SMEM = pl.BlockSpec(memory_space=pltpu.SMEM)
ANY = pl.BlockSpec(memory_space=pl.ANY)
LIMIT = 48 * 1024 * 1024


def shape(dims, dtype=F32):
    return jax.ShapeDtypeStruct(dims, dtype)


def this_core():
    return lax.rem(lax.axis_index("member"), 2)


def pack_kernel(count_ref, matrix_ref, adapters_ref, heads_ref, cot_ref, packed_ref, q_ref):
    own, D = matrix_ref.shape
    K = adapters_ref.shape[2]
    packed_ref[:, :D] = matrix_ref[...].astype(BF16)
    parts = [adapters_ref[k] for k in range(3)] + [jnp.zeros((own, LANES - 3 * K), F32)]
    packed_ref[:, D:D + LANES] = jnp.concatenate(parts, axis=1).astype(BF16)
    L = packed_ref.shape[1] - D - LANES
    rows = []
    for t in range(own):
        h, c = divmod(t * L, D)
        rows.append(heads_ref[h:h + 1, c:c + L])
    packed_ref[:, D + LANES:] = jnp.concatenate(rows, axis=0).astype(BF16)
    lane = lax.broadcasted_iota(jnp.int32, cot_ref.shape, 1)
    q_ref[...] = jnp.where(lane < count_ref[0], cot_ref[...], 0.0) * (1.0 / K)


def pack_call(counts, matrix, adapters_t, heads, cot):
    own, D = matrix.shape
    L = heads.shape[0] * D // own
    return pl.pallas_call(
        pack_kernel,
        out_shape=(shape((own, D + LANES + L), BF16), shape(cot.shape)),
        in_specs=[SMEM, VMEM, VMEM, VMEM, VMEM],
        out_specs=(VMEM, VMEM),
        name="pack_weights",
    )(counts, matrix, adapters_t, heads, cot)


def grad_kernel(
    x_ref, rows_q_ref, packed_ref,
    keep_ref, sent_ref, heads_grad_ref, pred_ref, rows_ref, turned_ref, back_ref,
    cols_ref, heads_ref, weight_ref, xq_ref, q_ref, z0_ref, z1_ref, gp0_ref, gp1_ref,
    post_ref, pred_acc, sums_ref, gr_ref, grads_ref, *, own,
):
    R, D = x_ref.shape
    half = R // 2
    K = heads_grad_ref.shape[0]
    members = K // 2
    n = back_ref.shape[0]
    step_id, steps = pl.program_id(0), pl.num_programs(0)
    core = this_core()
    base = core * members
    z_refs, gp_refs = (z0_ref, z1_ref), (gp0_ref, gp1_ref)

    def set_up():
        weight_ref[...] = packed_ref[:, :D].astype(F32)
        cols = packed_ref[:, D:D + LANES].astype(F32)
        cols_ref[...] = cols
        rows_ref[...] = cols.T
        turned_ref[...] = packed_ref[:, :D].T
        L = packed_ref.shape[1] - D - LANES
        per_head = D // L
        for c in range(0, L, LANES):
            gr_ref[:K * per_head, :] = packed_ref[:K * per_head, D + LANES + c:D + 2 * LANES + c].astype(F32)
            for k in range(per_head):
                heads_ref[:, k * L + c:k * L + c + LANES] = gr_ref[pl.ds(k, K, stride=per_head), :]
        for ref in (pred_acc, gr_ref, sums_ref, grads_ref, gp1_ref, heads_grad_ref):
            ref[...] = jnp.zeros_like(ref)
        q_row = rows_q_ref[...]
        q_ref[...] = jnp.broadcast_to(q_row, (LANES, R)).T
        half_q = 0.5 * q_row
        q_hi = half_q.astype(BF16)
        q_lo = (half_q - q_hi.astype(F32)).astype(BF16)
        xq_ref[:D, :] = (x_ref[...].T.astype(F32) * half_q).astype(BF16)
        sub = lax.broadcasted_iota(jnp.int32, (16, R), 0)
        extra = jnp.where(sub == 0, q_hi.astype(F32), jnp.where(sub == 1, q_lo.astype(F32), 0.0))
        xq_ref[D:, :] = extra.astype(BF16)

    def forward(i, z_ref):
        r = rows_ref[pl.ds(base + i, 1), :].astype(BF16)
        z_ref[...] = jnp.dot(x_ref[...] * r, packed_ref[:, :D], preferred_element_type=F32)

    def middle(i, k, z_ref, gp_ref, lo, hi, total):
        s = 0.5 * rows_ref[pl.ds(K + base + i, 1), :]
        b = 0.5 * rows_ref[pl.ds(2 * K + base + i, 1), :]
        hb = heads_ref[pl.ds(base + i, 1), :]
        step = 16
        for c in range(lo, hi, step):
            y = z_ref[c:c + step, :] * s + b
            t = jnp.tanh(y)
            a = 1.0 + t
            h = y * a
            d = a + h * (1.0 - t)
            gp = (hb * d).astype(BF16)
            gp_ref[c:c + step, :] = gp
            back_ref[k, c:c + step, :] = gp
            hh = h * hb
            pred_acc[c:c + step, :] += sum(hh[:, l:l + LANES] for l in range(0, D, LANES))
            q = q_ref[c:c + step, :]
            qh = jnp.concatenate([h[:, l:l + LANES] * q for l in range(0, D, LANES)], axis=1)
            part = sum(qh[j:j + 8] for j in range(0, step, 8))
            total = part if total is None else total + part
        return total

    def outer(gp_ref):
        post_ref[...] = jnp.dot(xq_ref[...], gp_ref[...], preferred_element_type=F32)

    def spread(i, lo, hi, total):
        s = rows_ref[pl.ds(K + base + i, 1), :]
        step = 16
        lane = lax.broadcasted_iota(jnp.int32, (step, LANES), 1)
        for c in range(lo, hi, step):
            g = post_ref[c:c + step, :]
            r = jnp.sum(jnp.where(lane == base + i, cols_ref[c:c + step, :], 0.0), axis=1, keepdims=True)
            t = g * weight_ref[c:c + step, :]
            rt = t * r
            part = sum(rt[j:j + 8] for j in range(0, step, 8))
            total = part if total is None else total + part
            st = t * s
            fold = sum(st[:, l:l + LANES] for l in range(0, D, LANES))
            gr_ref[c:c + step, :] += jnp.where(lane == base + i, jnp.sum(fold, axis=1, keepdims=True), 0.0)
            grads_ref[c:c + step, :D] += (g * s) * r
        return total

    def finish(i, total):
        sums_ref[pl.ds(K + base + i, 1), :] = jnp.sum(total, axis=0, keepdims=True)
        sums_ref[pl.ds(2 * K + base + i, 1), :] = post_ref[D:D + 1, :] + post_ref[D + 1:D + 2, :]

    def member(i, k, now, other, nxt):
        total = middle(i, k, z_refs[now], gp_refs[now], 0, R, None)
        forward(nxt, z_refs[other])
        outer(gp_refs[other])
        heads_grad_ref[pl.ds(base + i, 1), :] = jnp.sum(total, axis=0, keepdims=True)
        finish(i - 1, spread(i - 1, 0, D, None))

    @pl.when(step_id == 0)
    def _():
        set_up()
        forward(0, z_refs[0])

    for k in range(n):
        i, now, other = step_id * n + k, k % 2, (k + 1) % 2
        member(i, k, now, other, jnp.minimum(i + 1, members - 1))

    @pl.when(step_id == steps - 1)
    def _():
        outer(gp_refs[1])
        finish(members - 1, spread(members - 1, 0, D, None))
        for side in range(2):
            at = slice(side * half, (side + 1) * half)
            pred_ref[side:side + 1, :] = jnp.sum(pred_acc[at, :].T, axis=0, keepdims=True)
        grads_ref[:, D:] = sums_ref[...].T + gr_ref[...]
        for j in range(D // (2 * own)):
            low = grads_ref[2 * j * own:(2 * j + 1) * own, :]
            high = grads_ref[(2 * j + 1) * own:(2 * j + 2) * own, :]
            keep_ref[j * own:(j + 1) * own, :] = jnp.where(core == 0, low, high)
            sent_ref[j * own:(j + 1) * own, :] = jnp.where(core == 0, high, low).astype(BF16)


def grad_call(x, q, packed, K, own, n=2):
    R, D = x.shape
    half = R // 2
    members = K // 2
    flops = 4 * members * R * D * D
    return pl.pallas_call(
        functools.partial(grad_kernel, own=own),
        grid=(members // n,),
        out_shape=(
            shape((D // 2, D + LANES)), shape((D // 2, D + LANES), BF16), shape((K, D)), shape((2, half)),
            shape((LANES, D)), shape((D, D), BF16), shape((members, R, D), BF16),
        ),
        in_specs=[VMEM] * 3,
        out_specs=(VMEM, VMEM, VMEM, VMEM, VMEM, VMEM, pl.BlockSpec((n, R, D), lambda i: (i, 0, 0))),
        scratch_shapes=[
            pltpu.VMEM((D, LANES), F32), pltpu.VMEM((K, D), F32), pltpu.VMEM((D, D), F32),
            pltpu.VMEM((D + 16, R), BF16), pltpu.VMEM((R, LANES), F32),
            pltpu.VMEM((R, D), F32), pltpu.VMEM((R, D), F32), pltpu.VMEM((R, D), BF16), pltpu.VMEM((R, D), BF16),
            pltpu.VMEM((D + 16, D), F32), pltpu.VMEM((R, LANES), F32), pltpu.VMEM((LANES, D), F32),
            pltpu.VMEM((D, LANES), F32), pltpu.VMEM((D, D + LANES), F32),
        ],
        compiler_params=pltpu.CompilerParams(vmem_limit_bytes=LIMIT),
        cost_estimate=pl.CostEstimate(flops=2 * flops, bytes_accessed=members * R * D * 2, transcendentals=members * R * D),
        name="member_grads",
    )(x, q, packed)


def back_kernel(*refs, where, start, first, last):
    rows_ref, turned_ref, gp_hbm = refs[:3]
    rest = list(refs[3:])
    acc_in = None if first else rest.pop(0)
    q_ref = rest.pop(0) if last else None
    if last == "own":
        came_ref, pred_ref, pred_came_ref, count_ref = [rest.pop(0) for _ in range(4)]
        out_ref, pred_out_ref, gp_ref, sems = rest
    else:
        came_ref = None
        out_ref, gp_ref, sems = rest
    n, R, D = gp_ref.shape
    K = 2 * gp_hbm.shape[0]
    base = this_core() * gp_hbm.shape[0] + start
    copies = [
        pltpu.make_async_copy(gp_hbm.at[start + k, pl.ds(where * R, R)], gp_ref.at[k], sems.at[k]) for k in range(n)]
    for copy in copies:
        copy.start()
    if q_ref is not None:
        q_wide = jnp.broadcast_to(0.5 * q_ref[...], (LANES, R)).T
    if last == "own":
        lane = lax.broadcasted_iota(jnp.int32, (1, R), 1)
        total = pred_ref[0:1, :] + pred_came_ref[...]
        pred_out_ref[...] = jnp.where(lane < count_ref[0], total, 0.0) * (1.0 / K)
    for k in range(0, n, 2):
        left, right = [], []
        for j in (k, k + 1):
            r = rows_ref[pl.ds(base + j, 1), :].astype(BF16)
            s = rows_ref[pl.ds(K + base + j, 1), :].astype(BF16)
            right.append(turned_ref[...] * r)
            copies[j].wait()
            left.append(gp_ref[j] * s)
        value = jnp.dot(jnp.concatenate(left, axis=1), jnp.concatenate(right, axis=0), preferred_element_type=F32)
        if k or not first:
            value = value + (out_ref if k else acc_in)[...]
        if last and k + 2 == n:
            for l in range(0, D, LANES):
                part = value[:, l:l + LANES] * q_wide
                out_ref[:, l:l + LANES] = part if came_ref is None else part + came_ref[:, l:l + LANES]
        else:
            out_ref[...] = value


def back_call(rows, turned, back, where, start, count, acc=None, q=None, came=None):
    members, R2, D = back.shape
    R = R2 // 2
    last = None if q is None else "other" if came is None else "own"
    more = [v for v in (acc, q, *(came or ())) if v is not None]
    specs = [VMEM] * len(more)
    if last == "own":
        specs[-1] = SMEM
    return pl.pallas_call(
        functools.partial(back_kernel, where=where, start=start, first=acc is None, last=last),
        out_shape=(shape((R, D)), shape((1, R))) if last == "own" else shape((R, D)),
        in_specs=[VMEM, VMEM, ANY] + specs,
        out_specs=(VMEM, VMEM) if last == "own" else VMEM,
        scratch_shapes=[pltpu.VMEM((count, R, D), BF16), pltpu.SemaphoreType.DMA((count,))],
        compiler_params=pltpu.CompilerParams(vmem_limit_bytes=LIMIT),
        cost_estimate=pl.CostEstimate(flops=2 * count * R * D * D, bytes_accessed=count * R * D * 2, transcendentals=0),
        name="input_grads_other" if where else "input_grads_own",
    )(rows, turned, back, *more)


def direction(weight, first_old, second_old, gradient):
    first_new = beta_one * first_old + (1.0 - beta_one) * gradient
    second_new = beta_two * second_old + (1.0 - beta_two) * gradient * gradient
    fix_one = 1.0 - beta_one**STEP
    fix_two = 1.0 - beta_two**STEP
    update = (
        first_new / fix_one / (jnp.sqrt(second_new / fix_two) + epsilon) + weight_decay * weight
    )
    return (first_new, second_new, update)


def lane_sums(value):
    total = jnp.sum(value, axis=0, keepdims=True)
    width = total.shape[1]
    if width < LANES:
        return jnp.concatenate([total, jnp.zeros((1, LANES - width), F32)], axis=1)
    return sum(total[:, l:l + LANES] for l in range(0, width, LANES))


def direction_kernel(low, size, *refs):
    wide_ref = refs[0]
    count = size - 1
    came = refs[1:1 + count]
    (m_ref, m1_ref, m2_ref, a_ref, a1_ref, a2_ref, h_ref, h1_ref, h2_ref,
     m1_out, m2_out, mu_out, a1_out, a2_out, au_out, h1_out, h2_out, hu_out, sums_out) = refs[1 + count:]
    own, D = m_ref.shape
    K = a_ref.shape[2]
    n_heads = h_ref.shape[0]
    place = lax.rem(lax.axis_index("dp") // low, size)
    grad = wide_ref[:own, :]
    for v in range(1, size):
        grad = jnp.where(place == v, wide_ref[v * own:(v + 1) * own, :], grad)
    heads = wide_ref[size * own:size * own + n_heads, :D]
    for c in came:
        grad = grad + c[:own, :].astype(F32)
        heads = heads + c[own:own + n_heads, :D].astype(F32)
    weight_rows, update_rows = [], []
    first, second, update = direction(m_ref[...], m1_ref[...], m2_ref[...], grad[:, :D])
    m1_out[...], m2_out[...], mu_out[...] = first, second, update
    weight_rows.append(lane_sums(m_ref[...] * m_ref[...]))
    update_rows.append(lane_sums(update * update))
    for k in range(3):
        first, second, update = direction(a_ref[k], a1_ref[k], a2_ref[k], grad[:, D + k * K:D + (k + 1) * K])
        a1_out[k], a2_out[k], au_out[k] = first, second, update
        weight_rows.append(lane_sums(a_ref[k] * a_ref[k]))
        update_rows.append(lane_sums(update * update))
    first, second, update = direction(h_ref[...], h1_ref[...], h2_ref[...], heads)
    h1_out[...], h2_out[...], hu_out[...] = first, second, update
    share = 1.0 / lax.axis_size("dp")
    weight_rows.append(lane_sums(h_ref[...] * h_ref[...]) * share)
    update_rows.append(lane_sums(update * update) * share)
    sums_out[...] = jnp.concatenate(weight_rows + update_rows + [jnp.zeros((6, LANES), F32)], axis=0)


def direction_call(wide, came, low, states):
    m, a, h = states[0], states[3], states[6]
    outs = [shape(v.shape) for v in (m, m, m, a, a, a, h, h, h)] + [shape((16, LANES))]
    return pl.pallas_call(
        functools.partial(direction_kernel, low, len(came) + 1),
        out_shape=tuple(outs),
        in_specs=[VMEM] * (1 + len(came) + 9),
        out_specs=tuple([VMEM] * 10),
        name="directions",
    )(wide, *came, *states)


def update_kernel(count, *refs):
    sums_refs = refs[:count]
    m_ref, a_ref, h_ref, mu_ref, au_ref, hu_ref, m_out, a_out, h_out, norms_out = refs[count:]
    total = sums_refs[0][...]
    for ref in sums_refs[1:]:
        total = total + ref[...]
    norms = jnp.sqrt(jnp.sum(total, axis=1, keepdims=True))
    weight_norm, update_norm = norms[0:5], norms[5:10]
    rate = learn_rate * (weight_norm / update_norm)
    m_out[...] = m_ref[...] - rate[0:1] * mu_ref[...]
    for k in range(3):
        a_out[k] = a_ref[k] - rate[1 + k:2 + k] * au_ref[k]
    h_out[...] = h_ref[...] - rate[4:5] * hu_ref[...]
    row = jnp.sqrt(jnp.sum(total.T, axis=0, keepdims=True))
    norms_out[...] = jnp.concatenate([row[:, 0:5], row[:, 5:10]], axis=0)


def update_call(sums, m, a, h, mu, au, hu):
    return pl.pallas_call(
        functools.partial(update_kernel, len(sums)),
        out_shape=(shape(m.shape), shape(a.shape), shape(h.shape), shape((2, 5))),
        in_specs=[VMEM] * (len(sums) + 6),
        out_specs=(VMEM,) * 4,
        name="updates",
    )(*sums, m, a, h, mu, au, hu)


def bit_groups(n_dp, n_member):
    def split(low, count):
        bits = count.bit_length() - 1
        groups = []
        while bits > 0:
            take = 2 if bits >= 2 else 1
            bits -= take
            groups.append((low << bits, 1 << take))
        return groups

    return split(n_member, n_dp), split(2, n_member // 2) + [(1, 2)]


def swap(value, total, mask):
    return lax.ppermute(value, AXES, [(i, i ^ mask) for i in range(total)])


def gather_groups(value, groups, total, index, objects, q):
    rows = (objects, q)
    for axis, (low, size) in enumerate(groups):
        place = (index // low) % size
        held = [value] + [swap(value, total, low * m) for m in range(1, size)]
        if axis == 0:
            rows = rows + tuple(swap(v, total, 1) for v in rows)
            held, rows = lax.optimization_barrier((held, rows))
        elif axis == 1:
            rows = (jnp.concatenate([rows[0], rows[2]], axis=0), jnp.concatenate([rows[1], rows[3]], axis=1))
            held, rows = lax.optimization_barrier((held, rows))
        value = jnp.stack([lax.select_n(place ^ p, *held) for p in range(size)], axis=axis)
    return (value,) + rows


def beside(sends, work, *inputs):
    values, inputs = lax.optimization_barrier(([v for v, _, _ in sends], inputs))
    came = [swap(v, total, mask) for v, (_, total, mask) in zip(values, sends)]
    done = work(*inputs)
    return lax.optimization_barrier((came, done))


def shards(n_dp, n_member, objects, counts, cotangent, matrix, matrix_first, matrix_second,
           adapters, adapter_first, adapter_second, head_weights, head_first, head_second):
    R, D = objects.shape
    K = adapters.shape[1]
    own, own_heads = matrix.shape[0], head_weights.shape[0]
    total = n_dp * n_member
    index = lax.axis_index("dp") * n_member + lax.axis_index("member")
    dp_groups, member_groups = bit_groups(n_dp, n_member)
    chip_groups = member_groups[:-1]
    turned = [v.transpose(0, 2, 1) for v in (adapters, adapter_first, adapter_second)]

    packed, q_own = pack_call(counts, matrix, turned[0], head_weights, cotangent.reshape(1, R))
    full, x_both, q_both = gather_groups(packed, dp_groups + member_groups, total, index, objects, q_own)
    full = full.reshape(D, -1)
    q_other = q_both[:, R:]
    keep, sent, head_grads, preds, rows, wide_turned, back = grad_call(x_both, q_both, full, K, own)

    chips = [size for _, size in chip_groups]
    head_grads = head_grads.reshape(chips + [2, own_heads, D])
    core = index % 2
    axis = len(chips)
    members = K // 2
    quarter = members // 4

    def arrange(main, heads):
        main = main.reshape([n_dp] + chips + [own, D + LANES])
        main = jnp.moveaxis(main, 0, len(chips)).reshape(chips + [n_dp * own, D + LANES])
        return jnp.concatenate([main, jnp.pad(heads, [(0, 0)] * (len(chips) + 1) + [(0, LANES)])], axis=len(chips))

    def backward(where, part, parts=1, **more):
        def work(rows, wide_turned, back, *acc):
            return back_call(rows, wide_turned, back, where, part * quarter, parts * quarter, *acc, **more)
        return work

    weights = (rows, wide_turned, back)
    other_heads = lax.dynamic_index_in_dim(head_grads, 1 - core, axis, keepdims=False)
    own_heads_grad = lax.dynamic_index_in_dim(head_grads, core, axis, keepdims=False)
    (came, pred_came), acc = beside(
        [(arrange(sent, other_heads.astype(BF16)), total, 1), (preds[1:2], total, 1)], backward(1, 0), *weights)
    wide = arrange(keep, own_heads_grad) + came.astype(F32)
    for axis in reversed(range(len(chips))):
        low, size = chip_groups[axis]
        place = (index // low) % size
        part = [lax.dynamic_index_in_dim(wide, place ^ m, axis, keepdims=False) for m in range(size)]
        sends = [(part[m].astype(BF16), total, low * m) for m in range(1, size)]
        if axis == len(chips) - 1:
            came, acc = beside(sends, backward(1, 1, 2), *weights, acc)
        else:
            came = [swap(*send) for send in sends]
        wide = part[0]
        for c in came:
            wide = wide + c.astype(F32)
    for axis in reversed(range(len(dp_groups))):
        low, size = dp_groups[axis]
        place = (index // low) % size
        outer_count = (wide.shape[0] - own_heads) // (own * size)
        main = wide[:-own_heads].reshape(outer_count, size * own, D + LANES)
        heads = wide[-own_heads:]

        def chunk(v):
            at = lax.dynamic_slice_in_dim(main, v * own, own, 1)
            return jnp.concatenate([at.reshape(-1, D + LANES), heads], axis=0)

        sends = [(chunk(place ^ m).astype(BF16), total, low * m) for m in range(1, size)]
        if axis == len(dp_groups) - 1:
            last, acc = beside(sends, backward(1, 3, q=q_other), *weights, acc)
        else:
            last = [swap(*send) for send in sends]
        if axis:
            wide = chunk(place)
            for c in last:
                wide = wide + c.astype(F32)
    ig_came = swap(acc, total, 1)

    states = [matrix, matrix_first, matrix_second, *turned, head_weights, head_first, head_second]
    (m_first, m_second, m_update, a_first, a_second, a_update, h_first, h_second, h_update, sums) = direction_call(
        wide, last, dp_groups[0][0] // n_member, states)

    rounds = [(1, 2)] + chip_groups[::-1] + dp_groups[::-1]
    plan = {1: backward(0, 0, 2), len(rounds) - 1: backward(0, 2, 2, q=q_own, came=(ig_came, preds, pred_came, counts))}
    pending, acc = [sums], ()
    for step, (low, size) in enumerate(rounds):
        sums = pending[0]
        for p in pending[1:]:
            sums = sums + p
        sends = [(sums, total, low * m) for m in range(1, size)]
        if step in plan:
            came, acc = beside(sends, plan[step], *weights, *acc)
            acc = (acc,)
        else:
            came = [swap(*send) for send in sends]
        pending = [sums] + list(came)
    input_grad, predictions = acc[0]
    new_matrix, new_adapters, new_heads, norm_pairs = update_call(
        pending, matrix, turned[0], head_weights, m_update, a_update, h_update)

    def back_turn(v):
        return v.transpose(0, 2, 1)

    return (predictions.reshape(R), input_grad, new_matrix, m_first, m_second, back_turn(new_adapters),
            back_turn(a_first), back_turn(a_second), new_heads, h_first, h_second, norm_pairs.T)


def solution(mesh):
    n_dp, n_member = mesh.shape["dp"], mesh.shape["member"]
    rows, cols = P(AXES, None), P(None, None, AXES)
    heads = P("member", None)
    return jax.shard_map(
        functools.partial(shards, n_dp, n_member),
        mesh=mesh,
        in_specs=(rows, P(AXES), P(AXES), rows, rows, rows, cols, cols, cols, heads, heads, heads),
        out_specs=(P(AXES), rows, rows, rows, rows, cols, cols, cols, heads, heads, heads, P()),
        check_vma=False,
    )
```

```python
import functools

import jax
import jax.numpy as jnp
from jax import lax
from jax.experimental import pallas as pl
from jax.experimental.pallas import tpu as pltpu
from jax.sharding import PartitionSpec as P

LANES = 128
F32, BF16 = jnp.float32, jnp.bfloat16
STEP = 10
beta_one = 0.5
beta_two = 0.5
epsilon = 1e-06
weight_decay = 0.01
learn_rate = 0.25
AXES = ("dp", "member")
VMEM = pl.BlockSpec(memory_space=pltpu.VMEM)
SMEM = pl.BlockSpec(memory_space=pltpu.SMEM)
ANY = pl.BlockSpec(memory_space=pl.ANY)
LIMIT = 48 * 1024 * 1024


def shape(dims, dtype=F32):
    return jax.ShapeDtypeStruct(dims, dtype)


def this_core():
    return lax.rem(lax.axis_index("member"), 2)


def pack_kernel(count_ref, matrix_ref, adapters_ref, heads_ref, cot_ref, packed_ref, q_ref):
    own, D = matrix_ref.shape
    K = adapters_ref.shape[2]
    packed_ref[:, :D] = matrix_ref[...].astype(BF16)
    parts = [adapters_ref[k] for k in range(3)] + [jnp.zeros((own, LANES - 3 * K), F32)]
    packed_ref[:, D:D + LANES] = jnp.concatenate(parts, axis=1).astype(BF16)
    L = packed_ref.shape[1] - D - LANES
    rows = []
    for t in range(own):
        h, c = divmod(t * L, D)
        rows.append(heads_ref[h:h + 1, c:c + L])
    packed_ref[:, D + LANES:] = jnp.concatenate(rows, axis=0).astype(BF16)
    lane = lax.broadcasted_iota(jnp.int32, cot_ref.shape, 1)
    q_ref[...] = jnp.where(lane < count_ref[0], cot_ref[...], 0.0) * (1.0 / K)


def pack_call(counts, matrix, adapters_t, heads, cot):
    own, D = matrix.shape
    L = heads.shape[0] * D // own
    return pl.pallas_call(
        pack_kernel,
        out_shape=(shape((own, D + LANES + L), BF16), shape(cot.shape)),
        in_specs=[SMEM, VMEM, VMEM, VMEM, VMEM],
        out_specs=(VMEM, VMEM),
        name="pack_weights",
    )(counts, matrix, adapters_t, heads, cot)


def grad_kernel(
    x_ref, rows_q_ref, packed_ref,
    keep_ref, sent_ref, heads_grad_ref, pred_ref, rows_ref, turned_ref, back0_ref, back1_ref,
    cols_ref, heads_ref, weight_ref, xq_ref, q_ref, z0_ref, z1_ref, gp0_ref, gp1_ref,
    post_ref, pred_acc, sums_ref, gr_ref, grads_ref, *, own,
):
    R, D = x_ref.shape
    half = R // 2
    K = heads_grad_ref.shape[0]
    members = K // 2
    n = back0_ref.shape[0]
    step_id, steps = pl.program_id(0), pl.num_programs(0)
    core = this_core()
    base = core * members
    z_refs, gp_refs = (z0_ref, z1_ref), (gp0_ref, gp1_ref)

    def set_up():
        weight_ref[...] = packed_ref[:, :D].astype(F32)
        cols = packed_ref[:, D:D + LANES].astype(F32)
        cols_ref[...] = cols
        rows_ref[...] = cols.T
        turned_ref[...] = packed_ref[:, :D].T
        L = packed_ref.shape[1] - D - LANES
        per_head = D // L
        for c in range(0, L, LANES):
            gr_ref[:K * per_head, :] = packed_ref[:K * per_head, D + LANES + c:D + 2 * LANES + c].astype(F32)
            for k in range(per_head):
                heads_ref[:, k * L + c:k * L + c + LANES] = gr_ref[pl.ds(k, K, stride=per_head), :]
        for ref in (pred_acc, gr_ref, sums_ref, grads_ref, gp1_ref, heads_grad_ref):
            ref[...] = jnp.zeros_like(ref)
        q_row = rows_q_ref[...]
        q_ref[...] = jnp.broadcast_to(q_row, (LANES, R)).T
        half_q = 0.5 * q_row
        q_hi = half_q.astype(BF16)
        q_lo = (half_q - q_hi.astype(F32)).astype(BF16)
        xq_ref[:D, :] = (x_ref[...].T.astype(F32) * half_q).astype(BF16)
        sub = lax.broadcasted_iota(jnp.int32, (16, R), 0)
        extra = jnp.where(sub == 0, q_hi.astype(F32), jnp.where(sub == 1, q_lo.astype(F32), 0.0))
        xq_ref[D:, :] = extra.astype(BF16)

    def forward(i, z_ref):
        r = rows_ref[pl.ds(base + i, 1), :].astype(BF16)
        z_ref[...] = jnp.dot(x_ref[...] * r, packed_ref[:, :D], preferred_element_type=F32)

    def middle(i, k, z_ref, gp_ref, lo, hi, total):
        s = 0.5 * rows_ref[pl.ds(K + base + i, 1), :]
        b = 0.5 * rows_ref[pl.ds(2 * K + base + i, 1), :]
        hb = heads_ref[pl.ds(base + i, 1), :]
        step = 16
        for c in range(lo, hi, step):
            y = z_ref[c:c + step, :] * s + b
            t = jnp.tanh(y)
            a = 1.0 + t
            h = y * a
            d = a + h * (1.0 - t)
            gp = (hb * d).astype(BF16)
            gp_ref[c:c + step, :] = gp
            back_ref, at = (back0_ref, c) if c < half else (back1_ref, c - half)
            back_ref[k, at:at + step, :] = gp
            hh = h * hb
            pred_acc[c:c + step, :] += sum(hh[:, l:l + LANES] for l in range(0, D, LANES))
            q = q_ref[c:c + step, :]
            qh = jnp.concatenate([h[:, l:l + LANES] * q for l in range(0, D, LANES)], axis=1)
            part = sum(qh[j:j + 8] for j in range(0, step, 8))
            total = part if total is None else total + part
        return total

    def outer(gp_ref):
        post_ref[...] = jnp.dot(xq_ref[...], gp_ref[...], preferred_element_type=F32)

    def spread(i, lo, hi, total):
        s = rows_ref[pl.ds(K + base + i, 1), :]
        step = 16
        lane = lax.broadcasted_iota(jnp.int32, (step, LANES), 1)
        for c in range(lo, hi, step):
            g = post_ref[c:c + step, :]
            r = jnp.sum(jnp.where(lane == base + i, cols_ref[c:c + step, :], 0.0), axis=1, keepdims=True)
            t = g * weight_ref[c:c + step, :]
            rt = t * r
            part = sum(rt[j:j + 8] for j in range(0, step, 8))
            total = part if total is None else total + part
            st = t * s
            fold = sum(st[:, l:l + LANES] for l in range(0, D, LANES))
            gr_ref[c:c + step, :] += jnp.where(lane == base + i, jnp.sum(fold, axis=1, keepdims=True), 0.0)
            grads_ref[c:c + step, :D] += (g * s) * r
        return total

    def finish(i, total):
        sums_ref[pl.ds(K + base + i, 1), :] = jnp.sum(total, axis=0, keepdims=True)
        sums_ref[pl.ds(2 * K + base + i, 1), :] = post_ref[D:D + 1, :] + post_ref[D + 1:D + 2, :]

    def member(i, k, now, other, nxt):
        total = middle(i, k, z_refs[now], gp_refs[now], 0, R, None)
        forward(nxt, z_refs[other])
        outer(gp_refs[other])
        heads_grad_ref[pl.ds(base + i, 1), :] = jnp.sum(total, axis=0, keepdims=True)
        finish(i - 1, spread(i - 1, 0, D, None))

    @pl.when(step_id == 0)
    def _():
        set_up()
        forward(0, z_refs[0])

    for k in range(n):
        i, now, other = step_id * n + k, k % 2, (k + 1) % 2
        member(i, k, now, other, jnp.minimum(i + 1, members - 1))

    @pl.when(step_id == steps - 1)
    def _():
        outer(gp_refs[1])
        finish(members - 1, spread(members - 1, 0, D, None))
        for side in range(2):
            at = slice(side * half, (side + 1) * half)
            pred_ref[side:side + 1, :] = jnp.sum(pred_acc[at, :].T, axis=0, keepdims=True)
        grads_ref[:, D:] = sums_ref[...].T + gr_ref[...]
        for j in range(D // (2 * own)):
            low = grads_ref[2 * j * own:(2 * j + 1) * own, :]
            high = grads_ref[(2 * j + 1) * own:(2 * j + 2) * own, :]
            keep_ref[j * own:(j + 1) * own, :] = jnp.where(core == 0, low, high)
            sent_ref[j * own:(j + 1) * own, :] = jnp.where(core == 0, high, low).astype(BF16)


def grad_call(x, q, packed, K, own, n=2):
    R, D = x.shape
    half = R // 2
    members = K // 2
    flops = 4 * members * R * D * D
    return pl.pallas_call(
        functools.partial(grad_kernel, own=own),
        grid=(members // n,),
        out_shape=(
            shape((D // 2, D + LANES)), shape((D // 2, D + LANES), BF16), shape((K, D)), shape((2, half)),
            shape((LANES, D)), shape((D, D), BF16), shape((members, half, D), BF16), shape((members, half, D), BF16),
        ),
        in_specs=[VMEM] * 3,
        out_specs=(VMEM,) * 6 + (pl.BlockSpec((n, half, D), lambda i: (i, 0, 0)),) * 2,
        scratch_shapes=[
            pltpu.VMEM((D, LANES), F32), pltpu.VMEM((K, D), F32), pltpu.VMEM((D, D), F32),
            pltpu.VMEM((D + 16, R), BF16), pltpu.VMEM((R, LANES), F32),
            pltpu.VMEM((R, D), F32), pltpu.VMEM((R, D), F32), pltpu.VMEM((R, D), BF16), pltpu.VMEM((R, D), BF16),
            pltpu.VMEM((D + 16, D), F32), pltpu.VMEM((R, LANES), F32), pltpu.VMEM((LANES, D), F32),
            pltpu.VMEM((D, LANES), F32), pltpu.VMEM((D, D + LANES), F32),
        ],
        compiler_params=pltpu.CompilerParams(vmem_limit_bytes=LIMIT),
        cost_estimate=pl.CostEstimate(flops=2 * flops, bytes_accessed=members * R * D * 2, transcendentals=members * R * D),
        name="member_grads",
    )(x, q, packed)


def back_kernel(*refs, start, first, last):
    rows_ref, turned_ref, gp_hbm = refs[:3]
    rest = list(refs[3:])
    acc_in = None if first else rest.pop(0)
    q_ref = rest.pop(0) if last else None
    if last == "own":
        came_ref, pred_ref, pred_came_ref, count_ref = [rest.pop(0) for _ in range(4)]
        out_ref, pred_out_ref, gp_ref, sems = rest
    else:
        came_ref = None
        out_ref, gp_ref, sems = rest
    n, R, D = gp_ref.shape
    K = 2 * gp_hbm.shape[0]
    base = this_core() * gp_hbm.shape[0] + start
    copies = [
        pltpu.make_async_copy(gp_hbm.at[start + k], gp_ref.at[k], sems.at[k]) for k in range(n)]
    for copy in copies:
        copy.start()
    if q_ref is not None:
        q_wide = jnp.broadcast_to(0.5 * q_ref[...], (LANES, R)).T
    if last == "own":
        lane = lax.broadcasted_iota(jnp.int32, (1, R), 1)
        total = pred_ref[0:1, :] + pred_came_ref[...]
        pred_out_ref[...] = jnp.where(lane < count_ref[0], total, 0.0) * (1.0 / K)
    for k in range(0, n, 2):
        left, right = [], []
        for j in (k, k + 1):
            r = rows_ref[pl.ds(base + j, 1), :].astype(BF16)
            s = rows_ref[pl.ds(K + base + j, 1), :].astype(BF16)
            right.append(turned_ref[...] * r)
            copies[j].wait()
            left.append(gp_ref[j] * s)
        value = jnp.dot(jnp.concatenate(left, axis=1), jnp.concatenate(right, axis=0), preferred_element_type=F32)
        if k or not first:
            value = value + (out_ref if k else acc_in)[...]
        if last and k + 2 == n:
            for l in range(0, D, LANES):
                part = value[:, l:l + LANES] * q_wide
                out_ref[:, l:l + LANES] = part if came_ref is None else part + came_ref[:, l:l + LANES]
        else:
            out_ref[...] = value


def back_call(rows, turned, back, start, count, acc=None, q=None, came=None):
    members, R, D = back.shape
    last = None if q is None else "other" if came is None else "own"
    more = [v for v in (acc, q, *(came or ())) if v is not None]
    specs = [VMEM] * len(more)
    if last == "own":
        specs[-1] = SMEM
    return pl.pallas_call(
        functools.partial(back_kernel, start=start, first=acc is None, last=last),
        out_shape=(shape((R, D)), shape((1, R))) if last == "own" else shape((R, D)),
        in_specs=[VMEM, VMEM, ANY] + specs,
        out_specs=(VMEM, VMEM) if last == "own" else VMEM,
        scratch_shapes=[pltpu.VMEM((count, R, D), BF16), pltpu.SemaphoreType.DMA((count,))],
        compiler_params=pltpu.CompilerParams(vmem_limit_bytes=LIMIT),
        cost_estimate=pl.CostEstimate(flops=2 * count * R * D * D, bytes_accessed=count * R * D * 2, transcendentals=0),
        name="input_grads",
    )(rows, turned, back, *more)


def direction(weight, first_old, second_old, gradient):
    first_new = beta_one * first_old + (1.0 - beta_one) * gradient
    second_new = beta_two * second_old + (1.0 - beta_two) * gradient * gradient
    fix_one = 1.0 - beta_one**STEP
    fix_two = 1.0 - beta_two**STEP
    update = (
        first_new / fix_one / (jnp.sqrt(second_new / fix_two) + epsilon) + weight_decay * weight
    )
    return (first_new, second_new, update)


def lane_sums(value):
    total = jnp.sum(value, axis=0, keepdims=True)
    width = total.shape[1]
    if width < LANES:
        return jnp.concatenate([total, jnp.zeros((1, LANES - width), F32)], axis=1)
    return sum(total[:, l:l + LANES] for l in range(0, width, LANES))


def direction_kernel(low, size, *refs):
    wide_ref = refs[0]
    count = size - 1
    came = refs[1:1 + count]
    (m_ref, m1_ref, m2_ref, a_ref, a1_ref, a2_ref, h_ref, h1_ref, h2_ref,
     m1_out, m2_out, mu_out, a1_out, a2_out, au_out, h1_out, h2_out, hu_out, sums_out) = refs[1 + count:]
    own, D = m_ref.shape
    K = a_ref.shape[2]
    n_heads = h_ref.shape[0]
    place = lax.rem(lax.axis_index("dp") // low, size)
    grad = wide_ref[:own, :]
    for v in range(1, size):
        grad = jnp.where(place == v, wide_ref[v * own:(v + 1) * own, :], grad)
    heads = wide_ref[size * own:size * own + n_heads, :D]
    for c in came:
        grad = grad + c[:own, :].astype(F32)
        heads = heads + c[own:own + n_heads, :D].astype(F32)
    weight_rows, update_rows = [], []
    first, second, update = direction(m_ref[...], m1_ref[...], m2_ref[...], grad[:, :D])
    m1_out[...], m2_out[...], mu_out[...] = first, second, update
    weight_rows.append(lane_sums(m_ref[...] * m_ref[...]))
    update_rows.append(lane_sums(update * update))
    for k in range(3):
        first, second, update = direction(a_ref[k], a1_ref[k], a2_ref[k], grad[:, D + k * K:D + (k + 1) * K])
        a1_out[k], a2_out[k], au_out[k] = first, second, update
        weight_rows.append(lane_sums(a_ref[k] * a_ref[k]))
        update_rows.append(lane_sums(update * update))
    first, second, update = direction(h_ref[...], h1_ref[...], h2_ref[...], heads)
    h1_out[...], h2_out[...], hu_out[...] = first, second, update
    share = 1.0 / lax.axis_size("dp")
    weight_rows.append(lane_sums(h_ref[...] * h_ref[...]) * share)
    update_rows.append(lane_sums(update * update) * share)
    sums_out[...] = jnp.concatenate(weight_rows + update_rows + [jnp.zeros((6, LANES), F32)], axis=0)


def direction_call(wide, came, low, states):
    m, a, h = states[0], states[3], states[6]
    outs = [shape(v.shape) for v in (m, m, m, a, a, a, h, h, h)] + [shape((16, LANES))]
    return pl.pallas_call(
        functools.partial(direction_kernel, low, len(came) + 1),
        out_shape=tuple(outs),
        in_specs=[VMEM] * (1 + len(came) + 9),
        out_specs=tuple([VMEM] * 10),
        name="directions",
    )(wide, *came, *states)


def update_kernel(count, *refs):
    sums_refs = refs[:count]
    m_ref, a_ref, h_ref, mu_ref, au_ref, hu_ref, m_out, a_out, h_out, norms_out = refs[count:]
    total = sums_refs[0][...]
    for ref in sums_refs[1:]:
        total = total + ref[...]
    norms = jnp.sqrt(jnp.sum(total, axis=1, keepdims=True))
    weight_norm, update_norm = norms[0:5], norms[5:10]
    rate = learn_rate * (weight_norm / update_norm)
    m_out[...] = m_ref[...] - rate[0:1] * mu_ref[...]
    for k in range(3):
        a_out[k] = a_ref[k] - rate[1 + k:2 + k] * au_ref[k]
    h_out[...] = h_ref[...] - rate[4:5] * hu_ref[...]
    row = jnp.sqrt(jnp.sum(total.T, axis=0, keepdims=True))
    norms_out[...] = jnp.concatenate([row[:, 0:5], row[:, 5:10]], axis=0)


def update_call(sums, m, a, h, mu, au, hu):
    return pl.pallas_call(
        functools.partial(update_kernel, len(sums)),
        out_shape=(shape(m.shape), shape(a.shape), shape(h.shape), shape((2, 5))),
        in_specs=[VMEM] * (len(sums) + 6),
        out_specs=(VMEM,) * 4,
        name="updates",
    )(*sums, m, a, h, mu, au, hu)


def bit_groups(n_dp, n_member):
    def split(low, count):
        bits = count.bit_length() - 1
        groups = []
        while bits > 0:
            take = 2 if bits >= 2 else 1
            bits -= take
            groups.append((low << bits, 1 << take))
        return groups

    return split(n_member, n_dp), split(2, n_member // 2) + [(1, 2)]


def swap(value, total, mask):
    return lax.ppermute(value, AXES, [(i, i ^ mask) for i in range(total)])


def gather_groups(value, groups, total, index, objects, q):
    value, objects, q = lax.optimization_barrier((value, objects, q))
    rows = (objects, q)
    for axis, (low, size) in enumerate(groups):
        place = (index // low) % size
        held = [value] + [swap(value, total, low * m) for m in reversed(range(1, size))][::-1]
        if axis == 0:
            rows = rows + tuple(swap(v, total, 1) for v in rows)
            held, rows = lax.optimization_barrier((held, rows))
        elif axis == 1:
            rows = (jnp.concatenate([rows[0], rows[2]], axis=0), jnp.concatenate([rows[1], rows[3]], axis=1))
            held, rows = lax.optimization_barrier((held, rows))
        value = jnp.stack([lax.select_n(place ^ p, *held) for p in range(size)], axis=axis)
    return (value,) + rows


def beside(sends, work, *inputs):
    values, inputs = lax.optimization_barrier(([v for v, _, _ in sends], inputs))
    came = [swap(v, total, mask) for v, (_, total, mask) in reversed(list(zip(values, sends)))][::-1]
    done = work(*inputs)
    return lax.optimization_barrier((came, done))


def shards(n_dp, n_member, objects, counts, cotangent, matrix, matrix_first, matrix_second,
           adapters, adapter_first, adapter_second, head_weights, head_first, head_second):
    R, D = objects.shape
    K = adapters.shape[1]
    own, own_heads = matrix.shape[0], head_weights.shape[0]
    total = n_dp * n_member
    index = lax.axis_index("dp") * n_member + lax.axis_index("member")
    dp_groups, member_groups = bit_groups(n_dp, n_member)
    chip_groups = member_groups[:-1]
    turned = [v.transpose(0, 2, 1) for v in (adapters, adapter_first, adapter_second)]

    packed, q_own = pack_call(counts, matrix, turned[0], head_weights, cotangent.reshape(1, R))
    full, x_both, q_both = gather_groups(packed, dp_groups + member_groups, total, index, objects, q_own)
    full = full.reshape(D, -1)
    q_other = q_both[:, R:]
    keep, sent, head_grads, preds, rows, wide_turned, back_own, back_other = grad_call(x_both, q_both, full, K, own)

    chips = [size for _, size in chip_groups]
    head_grads = head_grads.reshape(chips + [2, own_heads, D])
    core = index % 2
    axis = len(chips)
    members = K // 2
    quarter = members // 4

    def arrange(main, heads):
        main = main.reshape([n_dp] + chips + [own, D + LANES])
        main = jnp.moveaxis(main, 0, len(chips)).reshape(chips + [n_dp * own, D + LANES])
        return jnp.concatenate([main, jnp.pad(heads, [(0, 0)] * (len(chips) + 1) + [(0, LANES)])], axis=len(chips))

    def backward(part, parts=1, **more):
        def work(rows, wide_turned, back, *acc):
            return back_call(rows, wide_turned, back, part * quarter, parts * quarter, *acc, **more)
        return work

    weights = (rows, wide_turned, back_other)
    other_heads = lax.dynamic_index_in_dim(head_grads, 1 - core, axis, keepdims=False)
    own_heads_grad = lax.dynamic_index_in_dim(head_grads, core, axis, keepdims=False)
    (came, pred_came), acc = beside(
        [(arrange(sent, other_heads.astype(BF16)), total, 1), (preds[1:2], total, 1)], backward(0), *weights)
    wide = arrange(keep, own_heads_grad) + came.astype(F32)
    for axis in reversed(range(len(chips))):
        low, size = chip_groups[axis]
        place = (index // low) % size
        part = [lax.dynamic_index_in_dim(wide, place ^ m, axis, keepdims=False) for m in range(size)]
        sends = [(part[m].astype(BF16), total, low * m) for m in range(1, size)]
        if axis == len(chips) - 1:
            came, acc = beside(sends, backward(1, 2), *weights, acc)
        else:
            came = [swap(*send) for send in sends]
        wide = part[0]
        for c in came:
            wide = wide + c.astype(F32)
    for axis in reversed(range(len(dp_groups))):
        low, size = dp_groups[axis]
        place = (index // low) % size
        outer_count = (wide.shape[0] - own_heads) // (own * size)
        main = wide[:-own_heads].reshape(outer_count, size * own, D + LANES)
        heads = wide[-own_heads:]

        def chunk(v):
            at = lax.dynamic_slice_in_dim(main, v * own, own, 1)
            return jnp.concatenate([at.reshape(-1, D + LANES), heads], axis=0)

        sends = [(chunk(place ^ m).astype(BF16), total, low * m) for m in range(1, size)]
        if axis == len(dp_groups) - 1:
            last, acc = beside(sends, backward(3, q=q_other), *weights, acc)
        else:
            last = [swap(*send) for send in sends]
        if axis:
            wide = chunk(place)
            for c in last:
                wide = wide + c.astype(F32)
    ig_came = swap(acc, total, 1)

    states = [matrix, matrix_first, matrix_second, *turned, head_weights, head_first, head_second]
    (m_first, m_second, m_update, a_first, a_second, a_update, h_first, h_second, h_update, sums) = direction_call(
        wide, last, dp_groups[0][0] // n_member, states)

    rounds = [(1, 2)] + chip_groups[::-1] + dp_groups[::-1]
    plan = {1: backward(0, 2), len(rounds) - 1: backward(2, 2, q=q_own, came=(ig_came, preds, pred_came, counts))}
    pending, acc = [sums], ()
    for step, (low, size) in enumerate(rounds):
        sums = pending[0]
        for p in pending[1:]:
            sums = sums + p
        sends = [(sums, total, low * m) for m in range(1, size)]
        if step in plan:
            came, acc = beside(sends, plan[step], rows, wide_turned, back_own, *acc)
            acc = (acc,)
        else:
            came = [swap(*send) for send in sends]
        pending = [sums] + list(came)
    input_grad, predictions = acc[0]
    new_matrix, new_adapters, new_heads, norm_pairs = update_call(
        pending, matrix, turned[0], head_weights, m_update, a_update, h_update)

    def back_turn(v):
        return v.transpose(0, 2, 1)

    return (predictions.reshape(R), input_grad, new_matrix, m_first, m_second, back_turn(new_adapters),
            back_turn(a_first), back_turn(a_second), new_heads, h_first, h_second, norm_pairs.T)


def solution(mesh):
    n_dp, n_member = mesh.shape["dp"], mesh.shape["member"]
    rows, cols = P(AXES, None), P(None, None, AXES)
    heads = P("member", None)
    return jax.shard_map(
        functools.partial(shards, n_dp, n_member),
        mesh=mesh,
        in_specs=(rows, P(AXES), P(AXES), rows, rows, rows, cols, cols, cols, heads, heads, heads),
        out_specs=(P(AXES), rows, rows, rows, rows, cols, cols, cols, heads, heads, heads, P()),
        check_vma=False,
    )
```

```python
import functools

import jax
import jax.numpy as jnp
from jax import lax
from jax.experimental import pallas as pl
from jax.experimental.pallas import tpu as pltpu
from jax.sharding import PartitionSpec as P

LANES = 128
F32, BF16 = jnp.float32, jnp.bfloat16
STEP = 10
beta_one = 0.5
beta_two = 0.5
epsilon = 1e-06
weight_decay = 0.01
learn_rate = 0.25
AXES = ("dp", "member")
VMEM = pl.BlockSpec(memory_space=pltpu.VMEM)
SMEM = pl.BlockSpec(memory_space=pltpu.SMEM)
ANY = pl.BlockSpec(memory_space=pl.ANY)
LIMIT = 48 * 1024 * 1024
SMALL = pltpu.CompilerParams(vmem_limit_bytes=8 * 1024 * 1024)


def shape(dims, dtype=F32):
    return jax.ShapeDtypeStruct(dims, dtype)


def this_core():
    return lax.rem(lax.axis_index("member"), 2)


def pack_kernel(count_ref, matrix_ref, adapters_ref, heads_ref, cot_ref, packed_ref, q_ref):
    own, D = matrix_ref.shape
    K = adapters_ref.shape[2]
    packed_ref[:, :D] = matrix_ref[...].astype(BF16)
    parts = [adapters_ref[k] for k in range(3)] + [jnp.zeros((own, LANES - 3 * K), F32)]
    packed_ref[:, D:D + LANES] = jnp.concatenate(parts, axis=1).astype(BF16)
    L = packed_ref.shape[1] - D - LANES
    rows = []
    for t in range(own):
        h, c = divmod(t * L, D)
        rows.append(heads_ref[h:h + 1, c:c + L])
    packed_ref[:, D + LANES:] = jnp.concatenate(rows, axis=0).astype(BF16)
    lane = lax.broadcasted_iota(jnp.int32, cot_ref.shape, 1)
    q_ref[...] = jnp.where(lane < count_ref[0], cot_ref[...], 0.0) * (1.0 / K)


def pack_call(counts, matrix, adapters_t, heads, cot):
    own, D = matrix.shape
    L = heads.shape[0] * D // own
    return pl.pallas_call(
        pack_kernel,
        out_shape=(shape((own, D + LANES + L), BF16), shape(cot.shape)),
        in_specs=[SMEM, VMEM, VMEM, VMEM, VMEM],
        out_specs=(VMEM, VMEM),
        compiler_params=SMALL,
        name="pack_weights",
    )(counts, matrix, adapters_t, heads, cot)


def grad_kernel(
    x_ref, rows_q_ref, packed_ref,
    keep_ref, sent_ref, heads_grad_ref, pred_ref, rows_ref, turned_ref, back0_ref, back1_ref,
    cols_ref, heads_ref, weight_ref, xq_ref, q_ref, z0_ref, z1_ref, gp0_ref, gp1_ref,
    post_ref, pred_acc, sums_ref, gr_ref, grads_ref, *, own,
):
    R, D = x_ref.shape
    half = R // 2
    K = heads_grad_ref.shape[0]
    members = K // 2
    n = back0_ref.shape[0]
    step_id, steps = pl.program_id(0), pl.num_programs(0)
    core = this_core()
    base = core * members
    z_refs, gp_refs = (z0_ref, z1_ref), (gp0_ref, gp1_ref)

    def set_up():
        weight_ref[...] = packed_ref[:, :D].astype(F32)
        cols = packed_ref[:, D:D + LANES].astype(F32)
        cols_ref[...] = cols
        rows_ref[...] = cols.T
        turned_ref[...] = packed_ref[:, :D].T
        L = packed_ref.shape[1] - D - LANES
        per_head = D // L
        for c in range(0, L, LANES):
            gr_ref[:K * per_head, :] = packed_ref[:K * per_head, D + LANES + c:D + 2 * LANES + c].astype(F32)
            for k in range(per_head):
                heads_ref[:, k * L + c:k * L + c + LANES] = gr_ref[pl.ds(k, K, stride=per_head), :]
        for ref in (pred_acc, gr_ref, sums_ref, grads_ref, gp1_ref, heads_grad_ref):
            ref[...] = jnp.zeros_like(ref)
        q_row = rows_q_ref[...]
        q_ref[...] = jnp.broadcast_to(q_row, (LANES, R)).T
        half_q = 0.5 * q_row
        q_hi = half_q.astype(BF16)
        q_lo = (half_q - q_hi.astype(F32)).astype(BF16)
        xq_ref[:D, :] = (x_ref[...].T.astype(F32) * half_q).astype(BF16)
        sub = lax.broadcasted_iota(jnp.int32, (16, R), 0)
        extra = jnp.where(sub == 0, q_hi.astype(F32), jnp.where(sub == 1, q_lo.astype(F32), 0.0))
        xq_ref[D:, :] = extra.astype(BF16)

    def forward(i, z_ref):
        r = rows_ref[pl.ds(base + i, 1), :].astype(BF16)
        z_ref[...] = jnp.dot(x_ref[...] * r, packed_ref[:, :D], preferred_element_type=F32)

    def middle(i, k, z_ref, gp_ref, lo, hi, total):
        s = 0.5 * rows_ref[pl.ds(K + base + i, 1), :]
        b = 0.5 * rows_ref[pl.ds(2 * K + base + i, 1), :]
        hb = heads_ref[pl.ds(base + i, 1), :]
        step = 16
        for c in range(lo, hi, step):
            y = z_ref[c:c + step, :] * s + b
            t = jnp.tanh(y)
            a = 1.0 + t
            h = y * a
            d = a + h * (1.0 - t)
            gp = (hb * d).astype(BF16)
            gp_ref[c:c + step, :] = gp
            back_ref, at = (back0_ref, c) if c < half else (back1_ref, c - half)
            back_ref[k, at:at + step, :] = gp
            hh = h * hb
            pred_acc[c:c + step, :] += sum(hh[:, l:l + LANES] for l in range(0, D, LANES))
            q = q_ref[c:c + step, :]
            qh = jnp.concatenate([h[:, l:l + LANES] * q for l in range(0, D, LANES)], axis=1)
            part = sum(qh[j:j + 8] for j in range(0, step, 8))
            total = part if total is None else total + part
        return total

    def outer(gp_ref):
        post_ref[...] = jnp.dot(xq_ref[...], gp_ref[...], preferred_element_type=F32)

    def spread(i, lo, hi, total):
        s = rows_ref[pl.ds(K + base + i, 1), :]
        step = 16
        lane = lax.broadcasted_iota(jnp.int32, (step, LANES), 1)
        for c in range(lo, hi, step):
            g = post_ref[c:c + step, :]
            r = jnp.sum(jnp.where(lane == base + i, cols_ref[c:c + step, :], 0.0), axis=1, keepdims=True)
            t = g * weight_ref[c:c + step, :]
            rt = t * r
            part = sum(rt[j:j + 8] for j in range(0, step, 8))
            total = part if total is None else total + part
            st = t * s
            fold = sum(st[:, l:l + LANES] for l in range(0, D, LANES))
            gr_ref[c:c + step, :] += jnp.where(lane == base + i, jnp.sum(fold, axis=1, keepdims=True), 0.0)
            grads_ref[c:c + step, :D] += (g * s) * r
        return total

    def finish(i, total):
        sums_ref[pl.ds(K + base + i, 1), :] = jnp.sum(total, axis=0, keepdims=True)
        sums_ref[pl.ds(2 * K + base + i, 1), :] = post_ref[D:D + 1, :] + post_ref[D + 1:D + 2, :]

    def member(i, k, now, other, nxt):
        total = middle(i, k, z_refs[now], gp_refs[now], 0, R, None)
        forward(nxt, z_refs[other])
        outer(gp_refs[other])
        heads_grad_ref[pl.ds(base + i, 1), :] = jnp.sum(total, axis=0, keepdims=True)
        finish(i - 1, spread(i - 1, 0, D, None))

    @pl.when(step_id == 0)
    def _():
        set_up()
        forward(0, z_refs[0])

    for k in range(n):
        i, now, other = step_id * n + k, k % 2, (k + 1) % 2
        member(i, k, now, other, jnp.minimum(i + 1, members - 1))

    @pl.when(step_id == steps - 1)
    def _():
        outer(gp_refs[1])
        finish(members - 1, spread(members - 1, 0, D, None))
        for side in range(2):
            at = slice(side * half, (side + 1) * half)
            pred_ref[side:side + 1, :] = jnp.sum(pred_acc[at, :].T, axis=0, keepdims=True)
        grads_ref[:, D:] = sums_ref[...].T + gr_ref[...]
        for j in range(D // (2 * own)):
            low = grads_ref[2 * j * own:(2 * j + 1) * own, :]
            high = grads_ref[(2 * j + 1) * own:(2 * j + 2) * own, :]
            keep_ref[j * own:(j + 1) * own, :] = jnp.where(core == 0, low, high)
            sent_ref[j * own:(j + 1) * own, :] = jnp.where(core == 0, high, low).astype(BF16)


def grad_call(x, q, packed, K, own, n=2):
    R, D = x.shape
    half = R // 2
    members = K // 2
    flops = 4 * members * R * D * D
    return pl.pallas_call(
        functools.partial(grad_kernel, own=own),
        grid=(members // n,),
        out_shape=(
            shape((D // 2, D + LANES)), shape((D // 2, D + LANES), BF16), shape((K, D)), shape((2, half)),
            shape((LANES, D)), shape((D, D), BF16), shape((members, half, D), BF16), shape((members, half, D), BF16),
        ),
        in_specs=[VMEM] * 3,
        out_specs=(VMEM,) * 6 + (pl.BlockSpec((n, half, D), lambda i: (i, 0, 0)),) * 2,
        scratch_shapes=[
            pltpu.VMEM((D, LANES), F32), pltpu.VMEM((K, D), F32), pltpu.VMEM((D, D), F32),
            pltpu.VMEM((D + 16, R), BF16), pltpu.VMEM((R, LANES), F32),
            pltpu.VMEM((R, D), F32), pltpu.VMEM((R, D), F32), pltpu.VMEM((R, D), BF16), pltpu.VMEM((R, D), BF16),
            pltpu.VMEM((D + 16, D), F32), pltpu.VMEM((R, LANES), F32), pltpu.VMEM((LANES, D), F32),
            pltpu.VMEM((D, LANES), F32), pltpu.VMEM((D, D + LANES), F32),
        ],
        compiler_params=pltpu.CompilerParams(vmem_limit_bytes=LIMIT),
        cost_estimate=pl.CostEstimate(flops=2 * flops, bytes_accessed=members * R * D * 2, transcendentals=members * R * D),
        name="member_grads",
    )(x, q, packed)


def back_kernel(*refs, start, first, last):
    rows_ref, turned_ref, gp_hbm = refs[:3]
    rest = list(refs[3:])
    acc_in = None if first else rest.pop(0)
    q_ref = rest.pop(0) if last else None
    if last == "own":
        came_ref, pred_ref, pred_came_ref, count_ref = [rest.pop(0) for _ in range(4)]
        out_ref, pred_out_ref, gp_ref, sems = rest
    else:
        came_ref = None
        out_ref, gp_ref, sems = rest
    n, R, D = gp_ref.shape
    K = 2 * gp_hbm.shape[0]
    base = this_core() * gp_hbm.shape[0] + start
    copies = [
        pltpu.make_async_copy(gp_hbm.at[start + k], gp_ref.at[k], sems.at[k]) for k in range(n)]
    for copy in copies:
        copy.start()
    if q_ref is not None:
        q_wide = jnp.broadcast_to(0.5 * q_ref[...], (LANES, R)).T
    if last == "own":
        lane = lax.broadcasted_iota(jnp.int32, (1, R), 1)
        total = pred_ref[0:1, :] + pred_came_ref[...]
        pred_out_ref[...] = jnp.where(lane < count_ref[0], total, 0.0) * (1.0 / K)
    for k in range(0, n, 2):
        left, right = [], []
        for j in (k, k + 1):
            r = rows_ref[pl.ds(base + j, 1), :].astype(BF16)
            s = rows_ref[pl.ds(K + base + j, 1), :].astype(BF16)
            right.append(turned_ref[...] * r)
            copies[j].wait()
            left.append(gp_ref[j] * s)
        value = jnp.dot(jnp.concatenate(left, axis=1), jnp.concatenate(right, axis=0), preferred_element_type=F32)
        if k or not first:
            value = value + (out_ref if k else acc_in)[...]
        if last and k + 2 == n:
            for l in range(0, D, LANES):
                part = value[:, l:l + LANES] * q_wide
                out_ref[:, l:l + LANES] = part if came_ref is None else part + came_ref[:, l:l + LANES]
        else:
            out_ref[...] = value


def back_call(rows, turned, back, start, count, acc=None, q=None, came=None):
    members, R, D = back.shape
    last = None if q is None else "other" if came is None else "own"
    more = [v for v in (acc, q, *(came or ())) if v is not None]
    specs = [VMEM] * len(more)
    if last == "own":
        specs[-1] = SMEM
    return pl.pallas_call(
        functools.partial(back_kernel, start=start, first=acc is None, last=last),
        out_shape=(shape((R, D)), shape((1, R))) if last == "own" else shape((R, D)),
        in_specs=[VMEM, VMEM, ANY] + specs,
        out_specs=(VMEM, VMEM) if last == "own" else VMEM,
        scratch_shapes=[pltpu.VMEM((count, R, D), BF16), pltpu.SemaphoreType.DMA((count,))],
        compiler_params=pltpu.CompilerParams(vmem_limit_bytes=LIMIT),
        cost_estimate=pl.CostEstimate(flops=2 * count * R * D * D, bytes_accessed=count * R * D * 2, transcendentals=0),
        name="input_grads",
    )(rows, turned, back, *more)


def direction(weight, first_old, second_old, gradient):
    first_new = beta_one * first_old + (1.0 - beta_one) * gradient
    second_new = beta_two * second_old + (1.0 - beta_two) * gradient * gradient
    fix_one = 1.0 - beta_one**STEP
    fix_two = 1.0 - beta_two**STEP
    update = (
        first_new / fix_one / (jnp.sqrt(second_new / fix_two) + epsilon) + weight_decay * weight
    )
    return (first_new, second_new, update)


def lane_sums(value):
    total = jnp.sum(value, axis=0, keepdims=True)
    width = total.shape[1]
    if width < LANES:
        return jnp.concatenate([total, jnp.zeros((1, LANES - width), F32)], axis=1)
    return sum(total[:, l:l + LANES] for l in range(0, width, LANES))


def direction_kernel(low, size, *refs):
    wide_ref = refs[0]
    count = size - 1
    came = refs[1:1 + count]
    (m_ref, m1_ref, m2_ref, a_ref, a1_ref, a2_ref, h_ref, h1_ref, h2_ref,
     m1_out, m2_out, mu_out, a1_out, a2_out, au_out, h1_out, h2_out, hu_out, sums_out) = refs[1 + count:]
    own, D = m_ref.shape
    K = a_ref.shape[2]
    n_heads = h_ref.shape[0]
    place = lax.rem(lax.axis_index("dp") // low, size)
    grad = wide_ref[:own, :]
    for v in range(1, size):
        grad = jnp.where(place == v, wide_ref[v * own:(v + 1) * own, :], grad)
    heads = wide_ref[size * own:size * own + n_heads, :D]
    for c in came:
        grad = grad + c[:own, :].astype(F32)
        heads = heads + c[own:own + n_heads, :D].astype(F32)
    weight_rows, update_rows = [], []
    first, second, update = direction(m_ref[...], m1_ref[...], m2_ref[...], grad[:, :D])
    m1_out[...], m2_out[...], mu_out[...] = first, second, update
    weight_rows.append(lane_sums(m_ref[...] * m_ref[...]))
    update_rows.append(lane_sums(update * update))
    for k in range(3):
        first, second, update = direction(a_ref[k], a1_ref[k], a2_ref[k], grad[:, D + k * K:D + (k + 1) * K])
        a1_out[k], a2_out[k], au_out[k] = first, second, update
        weight_rows.append(lane_sums(a_ref[k] * a_ref[k]))
        update_rows.append(lane_sums(update * update))
    first, second, update = direction(h_ref[...], h1_ref[...], h2_ref[...], heads)
    h1_out[...], h2_out[...], hu_out[...] = first, second, update
    share = 1.0 / lax.axis_size("dp")
    weight_rows.append(lane_sums(h_ref[...] * h_ref[...]) * share)
    update_rows.append(lane_sums(update * update) * share)
    sums_out[...] = jnp.concatenate(weight_rows + update_rows + [jnp.zeros((6, LANES), F32)], axis=0)


def direction_call(wide, came, low, states):
    m, a, h = states[0], states[3], states[6]
    outs = [shape(v.shape) for v in (m, m, m, a, a, a, h, h, h)] + [shape((16, LANES))]
    return pl.pallas_call(
        functools.partial(direction_kernel, low, len(came) + 1),
        out_shape=tuple(outs),
        in_specs=[VMEM] * (1 + len(came) + 9),
        out_specs=tuple([VMEM] * 10),
        compiler_params=SMALL,
        name="directions",
    )(wide, *came, *states)


def update_kernel(count, *refs):
    sums_refs = refs[:count]
    m_ref, a_ref, h_ref, mu_ref, au_ref, hu_ref, m_out, a_out, h_out, norms_out = refs[count:]
    total = sums_refs[0][...]
    for ref in sums_refs[1:]:
        total = total + ref[...]
    norms = jnp.sqrt(jnp.sum(total, axis=1, keepdims=True))
    weight_norm, update_norm = norms[0:5], norms[5:10]
    rate = learn_rate * (weight_norm / update_norm)
    m_out[...] = m_ref[...] - rate[0:1] * mu_ref[...]
    for k in range(3):
        a_out[k] = a_ref[k] - rate[1 + k:2 + k] * au_ref[k]
    h_out[...] = h_ref[...] - rate[4:5] * hu_ref[...]
    row = jnp.sqrt(jnp.sum(total.T, axis=0, keepdims=True))
    norms_out[...] = jnp.concatenate([row[:, 0:5], row[:, 5:10]], axis=0)


def update_call(sums, m, a, h, mu, au, hu):
    return pl.pallas_call(
        functools.partial(update_kernel, len(sums)),
        out_shape=(shape(m.shape), shape(a.shape), shape(h.shape), shape((2, 5))),
        in_specs=[VMEM] * (len(sums) + 6),
        out_specs=(VMEM,) * 4,
        compiler_params=SMALL,
        name="updates",
    )(*sums, m, a, h, mu, au, hu)


def bit_groups(n_dp, n_member):
    def split(low, count):
        bits = count.bit_length() - 1
        groups = []
        while bits > 0:
            take = 2 if bits >= 2 else 1
            bits -= take
            groups.append((low << bits, 1 << take))
        return groups

    return split(n_member, n_dp), split(2, n_member // 2) + [(1, 2)]


def swap(value, total, mask):
    return lax.ppermute(value, AXES, [(i, i ^ mask) for i in range(total)])


def gather_groups(value, groups, total, index, objects, q):
    value, objects, q = lax.optimization_barrier((value, objects, q))
    rows = (objects, q)
    for axis, (low, size) in enumerate(groups):
        place = (index // low) % size
        held = [value] + [swap(value, total, low * m) for m in reversed(range(1, size))][::-1]
        if axis == 0:
            rows = rows + tuple(swap(v, total, 1) for v in rows)
            held, rows = lax.optimization_barrier((held, rows))
        elif axis == 1:
            rows = (jnp.concatenate([rows[0], rows[2]], axis=0), jnp.concatenate([rows[1], rows[3]], axis=1))
            held, rows = lax.optimization_barrier((held, rows))
        value = jnp.stack([lax.select_n(place ^ p, *held) for p in range(size)], axis=axis)
    return (value,) + rows


def beside(sends, work, *inputs):
    values, inputs = lax.optimization_barrier(([v for v, _, _ in sends], inputs))
    came = [swap(v, total, mask) for v, (_, total, mask) in reversed(list(zip(values, sends)))][::-1]
    done = work(*inputs)
    return lax.optimization_barrier((came, done))


def shards(n_dp, n_member, objects, counts, cotangent, matrix, matrix_first, matrix_second,
           adapters, adapter_first, adapter_second, head_weights, head_first, head_second):
    R, D = objects.shape
    K = adapters.shape[1]
    own, own_heads = matrix.shape[0], head_weights.shape[0]
    total = n_dp * n_member
    index = lax.axis_index("dp") * n_member + lax.axis_index("member")
    dp_groups, member_groups = bit_groups(n_dp, n_member)
    chip_groups = member_groups[:-1]
    turned = [v.transpose(0, 2, 1) for v in (adapters, adapter_first, adapter_second)]

    packed, q_own = pack_call(counts, matrix, turned[0], head_weights, cotangent.reshape(1, R))
    full, x_both, q_both = gather_groups(packed, dp_groups + member_groups, total, index, objects, q_own)
    full = full.reshape(D, -1)
    q_other = q_both[:, R:]
    keep, sent, head_grads, preds, rows, wide_turned, back_own, back_other = grad_call(x_both, q_both, full, K, own)

    chips = [size for _, size in chip_groups]
    head_grads = head_grads.reshape(chips + [2, own_heads, D])
    core = index % 2
    axis = len(chips)
    members = K // 2

    def arrange(main, heads):
        main = main.reshape([n_dp] + chips + [own, D + LANES])
        main = jnp.moveaxis(main, 0, len(chips)).reshape(chips + [n_dp * own, D + LANES])
        return jnp.concatenate([main, jnp.pad(heads, [(0, 0)] * (len(chips) + 1) + [(0, LANES)])], axis=len(chips))

    def backward(start, count, **more):
        def work(rows, wide_turned, back, *acc):
            return back_call(rows, wide_turned, back, start, count, *acc, **more)
        return work

    weights = (rows, wide_turned, back_other)
    other_heads = lax.dynamic_index_in_dim(head_grads, 1 - core, axis, keepdims=False)
    own_heads_grad = lax.dynamic_index_in_dim(head_grads, core, axis, keepdims=False)
    (came, pred_came), acc = beside(
        [(arrange(sent, other_heads.astype(BF16)), total, 1), (preds[1:2], total, 1)], backward(0, 2), *weights)
    wide = arrange(keep, own_heads_grad) + came.astype(F32)
    for axis in reversed(range(len(chips))):
        low, size = chip_groups[axis]
        place = (index // low) % size
        part = [lax.dynamic_index_in_dim(wide, place ^ m, axis, keepdims=False) for m in range(size)]
        sends = [(part[m].astype(BF16), total, low * m) for m in range(1, size)]
        if axis == len(chips) - 1:
            came, acc = beside(sends, backward(2, 8), *weights, acc)
        else:
            came = [swap(*send) for send in sends]
        wide = part[0]
        for c in came:
            wide = wide + c.astype(F32)
    for axis in reversed(range(len(dp_groups))):
        low, size = dp_groups[axis]
        place = (index // low) % size
        outer_count = (wide.shape[0] - own_heads) // (own * size)
        main = wide[:-own_heads].reshape(outer_count, size * own, D + LANES)
        heads = wide[-own_heads:]

        def chunk(v):
            at = lax.dynamic_slice_in_dim(main, v * own, own, 1)
            return jnp.concatenate([at.reshape(-1, D + LANES), heads], axis=0)

        sends = [(chunk(place ^ m).astype(BF16), total, low * m) for m in range(1, size)]
        if axis == len(dp_groups) - 1:
            last, acc = beside(sends, backward(10, 6, q=q_other), *weights, acc)
        else:
            last = [swap(*send) for send in sends]
        if axis:
            wide = chunk(place)
            for c in last:
                wide = wide + c.astype(F32)
    ig_came = swap(acc, total, 1)

    states = [matrix, matrix_first, matrix_second, *turned, head_weights, head_first, head_second]
    (m_first, m_second, m_update, a_first, a_second, a_update, h_first, h_second, h_update, sums) = direction_call(
        wide, last, dp_groups[0][0] // n_member, states)

    rounds = [(1, 2)] + chip_groups[::-1] + dp_groups[::-1]
    plan = {1: backward(0, 8), len(rounds) - 1: backward(8, 8, q=q_own, came=(ig_came, preds, pred_came, counts))}
    pending, acc = [sums], ()
    for step, (low, size) in enumerate(rounds):
        sums = pending[0]
        for p in pending[1:]:
            sums = sums + p
        sends = [(sums, total, low * m) for m in range(1, size)]
        if step in plan:
            came, acc = beside(sends, plan[step], rows, wide_turned, back_own, *acc)
            acc = (acc,)
        else:
            came = [swap(*send) for send in sends]
        pending = [sums] + list(came)
    input_grad, predictions = acc[0]
    new_matrix, new_adapters, new_heads, norm_pairs = update_call(
        pending, matrix, turned[0], head_weights, m_update, a_update, h_update)

    def back_turn(v):
        return v.transpose(0, 2, 1)

    return (predictions.reshape(R), input_grad, new_matrix, m_first, m_second, back_turn(new_adapters),
            back_turn(a_first), back_turn(a_second), new_heads, h_first, h_second, norm_pairs.T)


def solution(mesh):
    n_dp, n_member = mesh.shape["dp"], mesh.shape["member"]
    rows, cols = P(AXES, None), P(None, None, AXES)
    heads = P("member", None)
    return jax.shard_map(
        functools.partial(shards, n_dp, n_member),
        mesh=mesh,
        in_specs=(rows, P(AXES), P(AXES), rows, rows, rows, cols, cols, cols, heads, heads, heads),
        out_specs=(P(AXES), rows, rows, rows, rows, cols, cols, cols, heads, heads, heads, P()),
        check_vma=False,
    )
```

```python
import functools

import jax
import jax.numpy as jnp
from jax import lax
from jax.experimental import pallas as pl
from jax.experimental.pallas import tpu as pltpu
from jax.sharding import PartitionSpec as P

LANES = 128
F32, BF16 = jnp.float32, jnp.bfloat16
STEP = 10
beta_one = 0.5
beta_two = 0.5
epsilon = 1e-06
weight_decay = 0.01
learn_rate = 0.25
AXES = ("dp", "member")
VMEM = pl.BlockSpec(memory_space=pltpu.VMEM)
SMEM = pl.BlockSpec(memory_space=pltpu.SMEM)
ANY = pl.BlockSpec(memory_space=pl.ANY)
LIMIT = 48 * 1024 * 1024
SMALL = pltpu.CompilerParams(vmem_limit_bytes=8 * 1024 * 1024)


def shape(dims, dtype=F32):
    return jax.ShapeDtypeStruct(dims, dtype)


def this_core():
    return lax.rem(lax.axis_index("member"), 2)


def pack_kernel(count_ref, matrix_ref, adapters_ref, heads_ref, cot_ref, packed_ref, q_ref):
    own, D = matrix_ref.shape
    K = adapters_ref.shape[2]
    packed_ref[:, :D] = matrix_ref[...].astype(BF16)
    parts = [adapters_ref[k] for k in range(3)] + [jnp.zeros((own, LANES - 3 * K), F32)]
    packed_ref[:, D:D + LANES] = jnp.concatenate(parts, axis=1).astype(BF16)
    L = packed_ref.shape[1] - D - LANES
    rows = []
    for t in range(own):
        h, c = divmod(t * L, D)
        rows.append(heads_ref[h:h + 1, c:c + L])
    packed_ref[:, D + LANES:] = jnp.concatenate(rows, axis=0).astype(BF16)
    lane = lax.broadcasted_iota(jnp.int32, cot_ref.shape, 1)
    q_ref[...] = jnp.where(lane < count_ref[0], cot_ref[...], 0.0) * (1.0 / K)


def pack_call(counts, matrix, adapters_t, heads, cot):
    own, D = matrix.shape
    L = heads.shape[0] * D // own
    return pl.pallas_call(
        pack_kernel,
        out_shape=(shape((own, D + LANES + L), BF16), shape(cot.shape)),
        in_specs=[SMEM, VMEM, VMEM, VMEM, VMEM],
        out_specs=(VMEM, VMEM),
        name="pack_weights",
    )(counts, matrix, adapters_t, heads, cot)


def grad_kernel(
    x_ref, rows_q_ref, packed_ref,
    keep_ref, sent_ref, heads_grad_ref, pred_ref, rows_ref, turned_ref, back0_ref, back1_ref,
    cols_ref, heads_ref, weight_ref, xq_ref, q_ref, z0_ref, z1_ref, gp0_ref, gp1_ref,
    post_ref, pred_acc, sums_ref, gr_ref, grads_ref, *, own,
):
    R, D = x_ref.shape
    half = R // 2
    K = heads_grad_ref.shape[0]
    members = K // 2
    n = back0_ref.shape[0]
    step_id, steps = pl.program_id(0), pl.num_programs(0)
    core = this_core()
    base = core * members
    z_refs, gp_refs = (z0_ref, z1_ref), (gp0_ref, gp1_ref)

    def set_up():
        weight_ref[...] = packed_ref[:, :D].astype(F32)
        cols = packed_ref[:, D:D + LANES].astype(F32)
        cols_ref[...] = cols
        rows_ref[...] = cols.T
        turned_ref[...] = packed_ref[:, :D].T
        L = packed_ref.shape[1] - D - LANES
        per_head = D // L
        for c in range(0, L, LANES):
            gr_ref[:K * per_head, :] = packed_ref[:K * per_head, D + LANES + c:D + 2 * LANES + c].astype(F32)
            for k in range(per_head):
                heads_ref[:, k * L + c:k * L + c + LANES] = gr_ref[pl.ds(k, K, stride=per_head), :]
        for ref in (pred_acc, gr_ref, sums_ref, grads_ref, gp1_ref, heads_grad_ref):
            ref[...] = jnp.zeros_like(ref)
        q_row = rows_q_ref[...]
        q_ref[...] = jnp.broadcast_to(q_row, (LANES, R)).T
        half_q = 0.5 * q_row
        q_hi = half_q.astype(BF16)
        q_lo = (half_q - q_hi.astype(F32)).astype(BF16)
        xq_ref[:D, :] = (x_ref[...].T.astype(F32) * half_q).astype(BF16)
        sub = lax.broadcasted_iota(jnp.int32, (16, R), 0)
        extra = jnp.where(sub == 0, q_hi.astype(F32), jnp.where(sub == 1, q_lo.astype(F32), 0.0))
        xq_ref[D:, :] = extra.astype(BF16)

    def forward(i, z_ref):
        r = rows_ref[pl.ds(base + i, 1), :].astype(BF16)
        z_ref[...] = jnp.dot(x_ref[...] * r, packed_ref[:, :D], preferred_element_type=F32)

    def middle(i, k, z_ref, gp_ref, lo, hi, total):
        s = 0.5 * rows_ref[pl.ds(K + base + i, 1), :]
        b = 0.5 * rows_ref[pl.ds(2 * K + base + i, 1), :]
        hb = heads_ref[pl.ds(base + i, 1), :]
        step = 16
        for c in range(lo, hi, step):
            y = z_ref[c:c + step, :] * s + b
            t = jnp.tanh(y)
            a = 1.0 + t
            h = y * a
            d = a + h * (1.0 - t)
            gp = (hb * d).astype(BF16)
            gp_ref[c:c + step, :] = gp
            back_ref, at = (back0_ref, c) if c < half else (back1_ref, c - half)
            back_ref[k, at:at + step, :] = gp
            hh = h * hb
            pred_acc[c:c + step, :] += sum(hh[:, l:l + LANES] for l in range(0, D, LANES))
            q = q_ref[c:c + step, :]
            qh = jnp.concatenate([h[:, l:l + LANES] * q for l in range(0, D, LANES)], axis=1)
            part = sum(qh[j:j + 8] for j in range(0, step, 8))
            total = part if total is None else total + part
        return total

    def outer(gp_ref):
        post_ref[...] = jnp.dot(xq_ref[...], gp_ref[...], preferred_element_type=F32)

    def spread(i, lo, hi, total):
        s = rows_ref[pl.ds(K + base + i, 1), :]
        step = 16
        lane = lax.broadcasted_iota(jnp.int32, (step, LANES), 1)
        for c in range(lo, hi, step):
            g = post_ref[c:c + step, :]
            r = jnp.sum(jnp.where(lane == base + i, cols_ref[c:c + step, :], 0.0), axis=1, keepdims=True)
            t = g * weight_ref[c:c + step, :]
            rt = t * r
            part = sum(rt[j:j + 8] for j in range(0, step, 8))
            total = part if total is None else total + part
            st = t * s
            fold = sum(st[:, l:l + LANES] for l in range(0, D, LANES))
            gr_ref[c:c + step, :] += jnp.where(lane == base + i, jnp.sum(fold, axis=1, keepdims=True), 0.0)
            grads_ref[c:c + step, :D] += (g * s) * r
        return total

    def finish(i, total):
        sums_ref[pl.ds(K + base + i, 1), :] = jnp.sum(total, axis=0, keepdims=True)
        sums_ref[pl.ds(2 * K + base + i, 1), :] = post_ref[D:D + 1, :] + post_ref[D + 1:D + 2, :]

    def member(i, k, now, other, nxt):
        total = middle(i, k, z_refs[now], gp_refs[now], 0, R, None)
        forward(nxt, z_refs[other])
        outer(gp_refs[other])
        heads_grad_ref[pl.ds(base + i, 1), :] = jnp.sum(total, axis=0, keepdims=True)
        finish(i - 1, spread(i - 1, 0, D, None))

    @pl.when(step_id == 0)
    def _():
        set_up()
        forward(0, z_refs[0])

    for k in range(n):
        i, now, other = step_id * n + k, k % 2, (k + 1) % 2
        member(i, k, now, other, jnp.minimum(i + 1, members - 1))

    @pl.when(step_id == steps - 1)
    def _():
        outer(gp_refs[1])
        finish(members - 1, spread(members - 1, 0, D, None))
        for side in range(2):
            at = slice(side * half, (side + 1) * half)
            pred_ref[side:side + 1, :] = jnp.sum(pred_acc[at, :].T, axis=0, keepdims=True)
        grads_ref[:, D:] = sums_ref[...].T + gr_ref[...]
        for j in range(D // (2 * own)):
            low = grads_ref[2 * j * own:(2 * j + 1) * own, :]
            high = grads_ref[(2 * j + 1) * own:(2 * j + 2) * own, :]
            keep_ref[j * own:(j + 1) * own, :] = jnp.where(core == 0, low, high)
            sent_ref[j * own:(j + 1) * own, :] = jnp.where(core == 0, high, low).astype(BF16)


def grad_call(x, q, packed, K, own, n=2):
    R, D = x.shape
    half = R // 2
    members = K // 2
    flops = 4 * members * R * D * D
    return pl.pallas_call(
        functools.partial(grad_kernel, own=own),
        grid=(members // n,),
        out_shape=(
            shape((D // 2, D + LANES)), shape((D // 2, D + LANES), BF16), shape((K, D)), shape((2, half)),
            shape((LANES, D)), shape((D, D), BF16), shape((members, half, D), BF16), shape((members, half, D), BF16),
        ),
        in_specs=[VMEM] * 3,
        out_specs=(VMEM,) * 6 + (pl.BlockSpec((n, half, D), lambda i: (i, 0, 0)),) * 2,
        scratch_shapes=[
            pltpu.VMEM((D, LANES), F32), pltpu.VMEM((K, D), F32), pltpu.VMEM((D, D), F32),
            pltpu.VMEM((D + 16, R), BF16), pltpu.VMEM((R, LANES), F32),
            pltpu.VMEM((R, D), F32), pltpu.VMEM((R, D), F32), pltpu.VMEM((R, D), BF16), pltpu.VMEM((R, D), BF16),
            pltpu.VMEM((D + 16, D), F32), pltpu.VMEM((R, LANES), F32), pltpu.VMEM((LANES, D), F32),
            pltpu.VMEM((D, LANES), F32), pltpu.VMEM((D, D + LANES), F32),
        ],
        compiler_params=pltpu.CompilerParams(vmem_limit_bytes=LIMIT),
        cost_estimate=pl.CostEstimate(flops=2 * flops, bytes_accessed=members * R * D * 2, transcendentals=members * R * D),
        name="member_grads",
    )(x, q, packed)


def back_kernel(*refs, start, first, last):
    rows_ref, turned_ref, gp_hbm = refs[:3]
    rest = list(refs[3:])
    acc_in = None if first else rest.pop(0)
    q_ref = rest.pop(0) if last else None
    if last == "own":
        came_ref, pred_ref, pred_came_ref, count_ref = [rest.pop(0) for _ in range(4)]
        out_ref, pred_out_ref, gp_ref, sems = rest
    else:
        came_ref = None
        out_ref, gp_ref, sems = rest
    n, R, D = gp_ref.shape
    K = 2 * gp_hbm.shape[0]
    base = this_core() * gp_hbm.shape[0] + start
    copies = [
        pltpu.make_async_copy(gp_hbm.at[start + k], gp_ref.at[k], sems.at[k]) for k in range(n)]
    for copy in copies:
        copy.start()
    if q_ref is not None:
        q_wide = jnp.broadcast_to(0.5 * q_ref[...], (LANES, R)).T
    if last == "own":
        lane = lax.broadcasted_iota(jnp.int32, (1, R), 1)
        total = pred_ref[0:1, :] + pred_came_ref[...]
        pred_out_ref[...] = jnp.where(lane < count_ref[0], total, 0.0) * (1.0 / K)
    for k in range(0, n, 2):
        left, right = [], []
        for j in (k, k + 1):
            r = rows_ref[pl.ds(base + j, 1), :].astype(BF16)
            s = rows_ref[pl.ds(K + base + j, 1), :].astype(BF16)
            right.append(turned_ref[...] * r)
            copies[j].wait()
            left.append(gp_ref[j] * s)
        value = jnp.dot(jnp.concatenate(left, axis=1), jnp.concatenate(right, axis=0), preferred_element_type=F32)
        if k or not first:
            value = value + (out_ref if k else acc_in)[...]
        if last and k + 2 == n:
            for l in range(0, D, LANES):
                part = value[:, l:l + LANES] * q_wide
                out_ref[:, l:l + LANES] = part if came_ref is None else part + came_ref[:, l:l + LANES]
        else:
            out_ref[...] = value


def back_call(rows, turned, back, start, count, acc=None, q=None, came=None):
    members, R, D = back.shape
    last = None if q is None else "other" if came is None else "own"
    more = [v for v in (acc, q, *(came or ())) if v is not None]
    specs = [VMEM] * len(more)
    if last == "own":
        specs[-1] = SMEM
    return pl.pallas_call(
        functools.partial(back_kernel, start=start, first=acc is None, last=last),
        out_shape=(shape((R, D)), shape((1, R))) if last == "own" else shape((R, D)),
        in_specs=[VMEM, VMEM, ANY] + specs,
        out_specs=(VMEM, VMEM) if last == "own" else VMEM,
        scratch_shapes=[pltpu.VMEM((count, R, D), BF16), pltpu.SemaphoreType.DMA((count,))],
        compiler_params=pltpu.CompilerParams(vmem_limit_bytes=LIMIT),
        cost_estimate=pl.CostEstimate(flops=2 * count * R * D * D, bytes_accessed=count * R * D * 2, transcendentals=0),
        name="input_grads",
    )(rows, turned, back, *more)


def direction(weight, first_old, second_old, gradient):
    first_new = beta_one * first_old + (1.0 - beta_one) * gradient
    second_new = beta_two * second_old + (1.0 - beta_two) * gradient * gradient
    fix_one = 1.0 - beta_one**STEP
    fix_two = 1.0 - beta_two**STEP
    update = (
        first_new / fix_one / (jnp.sqrt(second_new / fix_two) + epsilon) + weight_decay * weight
    )
    return (first_new, second_new, update)


def lane_sums(value):
    total = jnp.sum(value, axis=0, keepdims=True)
    width = total.shape[1]
    if width < LANES:
        return jnp.concatenate([total, jnp.zeros((1, LANES - width), F32)], axis=1)
    return sum(total[:, l:l + LANES] for l in range(0, width, LANES))


def direction_kernel(low, size, *refs):
    wide_ref = refs[0]
    count = size - 1
    came = refs[1:1 + count]
    (m_ref, m1_ref, m2_ref, a_ref, a1_ref, a2_ref, h_ref, h1_ref, h2_ref,
     m1_out, m2_out, mu_out, a1_out, a2_out, au_out, h1_out, h2_out, hu_out, sums_out) = refs[1 + count:]
    own, D = m_ref.shape
    K = a_ref.shape[2]
    n_heads = h_ref.shape[0]
    place = lax.rem(lax.axis_index("dp") // low, size)
    grad = wide_ref[:own, :]
    for v in range(1, size):
        grad = jnp.where(place == v, wide_ref[v * own:(v + 1) * own, :], grad)
    heads = wide_ref[size * own:size * own + n_heads, :D]
    for c in came:
        grad = grad + c[:own, :].astype(F32)
        heads = heads + c[own:own + n_heads, :D].astype(F32)
    weight_rows, update_rows = [], []
    first, second, update = direction(m_ref[...], m1_ref[...], m2_ref[...], grad[:, :D])
    m1_out[...], m2_out[...], mu_out[...] = first, second, update
    weight_rows.append(lane_sums(m_ref[...] * m_ref[...]))
    update_rows.append(lane_sums(update * update))
    for k in range(3):
        first, second, update = direction(a_ref[k], a1_ref[k], a2_ref[k], grad[:, D + k * K:D + (k + 1) * K])
        a1_out[k], a2_out[k], au_out[k] = first, second, update
        weight_rows.append(lane_sums(a_ref[k] * a_ref[k]))
        update_rows.append(lane_sums(update * update))
    first, second, update = direction(h_ref[...], h1_ref[...], h2_ref[...], heads)
    h1_out[...], h2_out[...], hu_out[...] = first, second, update
    share = 1.0 / lax.axis_size("dp")
    weight_rows.append(lane_sums(h_ref[...] * h_ref[...]) * share)
    update_rows.append(lane_sums(update * update) * share)
    sums_out[...] = jnp.concatenate(weight_rows + update_rows + [jnp.zeros((6, LANES), F32)], axis=0)


def direction_call(wide, came, low, states):
    m, a, h = states[0], states[3], states[6]
    outs = [shape(v.shape) for v in (m, m, m, a, a, a, h, h, h)] + [shape((16, LANES))]
    return pl.pallas_call(
        functools.partial(direction_kernel, low, len(came) + 1),
        out_shape=tuple(outs),
        in_specs=[VMEM] * (1 + len(came) + 9),
        out_specs=tuple([VMEM] * 10),
        compiler_params=SMALL,
        name="directions",
    )(wide, *came, *states)


def update_kernel(count, *refs):
    sums_refs = refs[:count]
    m_ref, a_ref, h_ref, mu_ref, au_ref, hu_ref, m_out, a_out, h_out, norms_out = refs[count:]
    total = sums_refs[0][...]
    for ref in sums_refs[1:]:
        total = total + ref[...]
    norms = jnp.sqrt(jnp.sum(total, axis=1, keepdims=True))
    weight_norm, update_norm = norms[0:5], norms[5:10]
    rate = learn_rate * (weight_norm / update_norm)
    m_out[...] = m_ref[...] - rate[0:1] * mu_ref[...]
    for k in range(3):
        a_out[k] = a_ref[k] - rate[1 + k:2 + k] * au_ref[k]
    h_out[...] = h_ref[...] - rate[4:5] * hu_ref[...]
    row = jnp.sqrt(jnp.sum(total.T, axis=0, keepdims=True))
    norms_out[...] = jnp.concatenate([row[:, 0:5], row[:, 5:10]], axis=0)


def update_call(sums, m, a, h, mu, au, hu):
    return pl.pallas_call(
        functools.partial(update_kernel, len(sums)),
        out_shape=(shape(m.shape), shape(a.shape), shape(h.shape), shape((2, 5))),
        in_specs=[VMEM] * (len(sums) + 6),
        out_specs=(VMEM,) * 4,
        compiler_params=SMALL,
        name="updates",
    )(*sums, m, a, h, mu, au, hu)


def bit_groups(n_dp, n_member):
    def split(low, count):
        bits = count.bit_length() - 1
        groups = []
        while bits > 0:
            take = 2 if bits >= 2 else 1
            bits -= take
            groups.append((low << bits, 1 << take))
        return groups

    return split(n_member, n_dp), split(2, n_member // 2) + [(1, 2)]


def swap(value, total, mask):
    return lax.ppermute(value, AXES, [(i, i ^ mask) for i in range(total)])


def gather_groups(value, groups, total, index, objects, q):
    value, objects, q = lax.optimization_barrier((value, objects, q))
    rows = (objects, q)
    for axis, (low, size) in enumerate(groups):
        place = (index // low) % size
        held = [value] + [swap(value, total, low * m) for m in reversed(range(1, size))][::-1]
        if axis == 0:
            rows = rows + tuple(swap(v, total, 1) for v in rows)
            held, rows = lax.optimization_barrier((held, rows))
        elif axis == 1:
            rows = (jnp.concatenate([rows[0], rows[2]], axis=0), jnp.concatenate([rows[1], rows[3]], axis=1))
            held, rows = lax.optimization_barrier((held, rows))
        value = jnp.stack([lax.select_n(place ^ p, *held) for p in range(size)], axis=axis)
    return (value,) + rows


def beside(sends, work, *inputs):
    values, inputs = lax.optimization_barrier(([v for v, _, _ in sends], inputs))
    came = [swap(v, total, mask) for v, (_, total, mask) in reversed(list(zip(values, sends)))][::-1]
    done = work(*inputs)
    return lax.optimization_barrier((came, done))


def shards(n_dp, n_member, objects, counts, cotangent, matrix, matrix_first, matrix_second,
           adapters, adapter_first, adapter_second, head_weights, head_first, head_second):
    R, D = objects.shape
    K = adapters.shape[1]
    own, own_heads = matrix.shape[0], head_weights.shape[0]
    total = n_dp * n_member
    index = lax.axis_index("dp") * n_member + lax.axis_index("member")
    dp_groups, member_groups = bit_groups(n_dp, n_member)
    chip_groups = member_groups[:-1]
    turned = [v.transpose(0, 2, 1) for v in (adapters, adapter_first, adapter_second)]

    packed, q_own = pack_call(counts, matrix, turned[0], head_weights, cotangent.reshape(1, R))
    full, x_both, q_both = gather_groups(packed, dp_groups + member_groups, total, index, objects, q_own)
    full = full.reshape(D, -1)
    q_other = q_both[:, R:]
    keep, sent, head_grads, preds, rows, wide_turned, back_own, back_other = grad_call(x_both, q_both, full, K, own)

    chips = [size for _, size in chip_groups]
    head_grads = head_grads.reshape(chips + [2, own_heads, D])
    core = index % 2
    axis = len(chips)
    members = K // 2

    def arrange(main, heads):
        main = main.reshape([n_dp] + chips + [own, D + LANES])
        main = jnp.moveaxis(main, 0, len(chips)).reshape(chips + [n_dp * own, D + LANES])
        return jnp.concatenate([main, jnp.pad(heads, [(0, 0)] * (len(chips) + 1) + [(0, LANES)])], axis=len(chips))

    def backward(start, count, **more):
        def work(rows, wide_turned, back, *acc):
            return back_call(rows, wide_turned, back, start, count, *acc, **more)
        return work

    weights = (rows, wide_turned, back_other)
    other_heads = lax.dynamic_index_in_dim(head_grads, 1 - core, axis, keepdims=False)
    own_heads_grad = lax.dynamic_index_in_dim(head_grads, core, axis, keepdims=False)
    (came, pred_came), acc = beside(
        [(arrange(sent, other_heads.astype(BF16)), total, 1), (preds[1:2], total, 1)], backward(0, 2), *weights)
    wide = arrange(keep, own_heads_grad) + came.astype(F32)
    for axis in reversed(range(len(chips))):
        low, size = chip_groups[axis]
        place = (index // low) % size
        part = [lax.dynamic_index_in_dim(wide, place ^ m, axis, keepdims=False) for m in range(size)]
        sends = [(part[m].astype(BF16), total, low * m) for m in range(1, size)]
        if axis == len(chips) - 1:
            came, acc = beside(sends, backward(2, 8), *weights, acc)
        else:
            came = [swap(*send) for send in sends]
        wide = part[0]
        for c in came:
            wide = wide + c.astype(F32)
    for axis in reversed(range(len(dp_groups))):
        low, size = dp_groups[axis]
        place = (index // low) % size
        outer_count = (wide.shape[0] - own_heads) // (own * size)
        main = wide[:-own_heads].reshape(outer_count, size * own, D + LANES)
        heads = wide[-own_heads:]

        def chunk(v):
            at = lax.dynamic_slice_in_dim(main, v * own, own, 1)
            return jnp.concatenate([at.reshape(-1, D + LANES), heads], axis=0)

        sends = [(chunk(place ^ m).astype(BF16), total, low * m) for m in range(1, size)]
        if axis == len(dp_groups) - 1:
            last, acc = beside(sends, backward(10, 6, q=q_other), *weights, acc)
        else:
            last = [swap(*send) for send in sends]
        if axis:
            wide = chunk(place)
            for c in last:
                wide = wide + c.astype(F32)
    ig_came = swap(acc, total, 1)

    states = [matrix, matrix_first, matrix_second, *turned, head_weights, head_first, head_second]
    (m_first, m_second, m_update, a_first, a_second, a_update, h_first, h_second, h_update, sums) = direction_call(
        wide, last, dp_groups[0][0] // n_member, states)

    rounds = [(1, 2)] + chip_groups[::-1] + dp_groups[::-1]
    plan = {0: backward(0, 2), 1: backward(2, 6), len(rounds) - 1: backward(8, 8, q=q_own, came=(ig_came, preds, pred_came, counts))}
    pending, acc = [sums], ()
    for step, (low, size) in enumerate(rounds):
        sums = pending[0]
        for p in pending[1:]:
            sums = sums + p
        sends = [(sums, total, low * m) for m in range(1, size)]
        if step in plan:
            came, acc = beside(sends, plan[step], rows, wide_turned, back_own, *acc)
            acc = (acc,)
        else:
            came = [swap(*send) for send in sends]
        pending = [sums] + list(came)
    input_grad, predictions = acc[0]
    new_matrix, new_adapters, new_heads, norm_pairs = update_call(
        pending, matrix, turned[0], head_weights, m_update, a_update, h_update)

    def back_turn(v):
        return v.transpose(0, 2, 1)

    return (predictions.reshape(R), input_grad, new_matrix, m_first, m_second, back_turn(new_adapters),
            back_turn(a_first), back_turn(a_second), new_heads, h_first, h_second, norm_pairs.T)


def solution(mesh):
    n_dp, n_member = mesh.shape["dp"], mesh.shape["member"]
    rows, cols = P(AXES, None), P(None, None, AXES)
    heads = P("member", None)
    return jax.shard_map(
        functools.partial(shards, n_dp, n_member),
        mesh=mesh,
        in_specs=(rows, P(AXES), P(AXES), rows, rows, rows, cols, cols, cols, heads, heads, heads),
        out_specs=(P(AXES), rows, rows, rows, rows, cols, cols, cols, heads, heads, heads, P()),
        check_vma=False,
    )
```

```python
import functools

import jax
import jax.numpy as jnp
from jax import lax
from jax.experimental import pallas as pl
from jax.experimental.pallas import tpu as pltpu
from jax.sharding import PartitionSpec as P

LANES = 128
F32, BF16 = jnp.float32, jnp.bfloat16
STEP = 10
beta_one = 0.5
beta_two = 0.5
epsilon = 1e-06
weight_decay = 0.01
learn_rate = 0.25
AXES = ("dp", "member")
VMEM = pl.BlockSpec(memory_space=pltpu.VMEM)
SMEM = pl.BlockSpec(memory_space=pltpu.SMEM)
ANY = pl.BlockSpec(memory_space=pl.ANY)
LIMIT = 48 * 1024 * 1024
SMALL = pltpu.CompilerParams(vmem_limit_bytes=8 * 1024 * 1024)


def shape(dims, dtype=F32):
    return jax.ShapeDtypeStruct(dims, dtype)


def this_core():
    return lax.rem(lax.axis_index("member"), 2)


def pack_kernel(matrix_ref, adapters_ref, heads_ref, packed_ref):
    own, D = matrix_ref.shape
    K = adapters_ref.shape[2]
    packed_ref[:, :D] = matrix_ref[...].astype(BF16)
    parts = [adapters_ref[k] for k in range(3)] + [jnp.zeros((own, LANES - 3 * K), F32)]
    packed_ref[:, D:D + LANES] = jnp.concatenate(parts, axis=1).astype(BF16)
    L = packed_ref.shape[1] - D - LANES
    rows = []
    for t in range(own):
        h, c = divmod(t * L, D)
        rows.append(heads_ref[h:h + 1, c:c + L])
    packed_ref[:, D + LANES:] = jnp.concatenate(rows, axis=0).astype(BF16)


def pack_call(matrix, adapters_t, heads):
    own, D = matrix.shape
    L = heads.shape[0] * D // own
    return pl.pallas_call(
        pack_kernel,
        out_shape=shape((own, D + LANES + L), BF16),
        in_specs=[VMEM] * 3,
        out_specs=VMEM,
        name="pack_weights",
    )(matrix, adapters_t, heads)


def grad_kernel(
    x_ref, rows_q_ref, packed_ref,
    keep_ref, sent_ref, heads_grad_ref, pred_ref, rows_ref, turned_ref, back0_ref, back1_ref,
    cols_ref, heads_ref, weight_ref, xq_ref, q_ref, z0_ref, z1_ref, gp0_ref, gp1_ref,
    post_ref, pred_acc, sums_ref, gr_ref, grads_ref, *, own,
):
    R, D = x_ref.shape
    half = R // 2
    K = heads_grad_ref.shape[0]
    members = K // 2
    n = back0_ref.shape[0]
    step_id, steps = pl.program_id(0), pl.num_programs(0)
    core = this_core()
    base = core * members
    z_refs, gp_refs = (z0_ref, z1_ref), (gp0_ref, gp1_ref)

    def set_up():
        weight_ref[...] = packed_ref[:, :D].astype(F32)
        cols = packed_ref[:, D:D + LANES].astype(F32)
        cols_ref[...] = cols
        rows_ref[...] = cols.T
        turned_ref[...] = packed_ref[:, :D].T
        L = packed_ref.shape[1] - D - LANES
        per_head = D // L
        for c in range(0, L, LANES):
            gr_ref[:K * per_head, :] = packed_ref[:K * per_head, D + LANES + c:D + 2 * LANES + c].astype(F32)
            for k in range(per_head):
                heads_ref[:, k * L + c:k * L + c + LANES] = gr_ref[pl.ds(k, K, stride=per_head), :]
        for ref in (pred_acc, gr_ref, sums_ref, grads_ref, gp1_ref, heads_grad_ref):
            ref[...] = jnp.zeros_like(ref)
        q_row = rows_q_ref[...]
        q_ref[...] = jnp.broadcast_to(q_row, (LANES, R)).T
        half_q = 0.5 * q_row
        q_hi = half_q.astype(BF16)
        q_lo = (half_q - q_hi.astype(F32)).astype(BF16)
        xq_ref[:D, :] = (x_ref[...].T.astype(F32) * half_q).astype(BF16)
        sub = lax.broadcasted_iota(jnp.int32, (16, R), 0)
        extra = jnp.where(sub == 0, q_hi.astype(F32), jnp.where(sub == 1, q_lo.astype(F32), 0.0))
        xq_ref[D:, :] = extra.astype(BF16)

    def forward(i, z_ref):
        r = rows_ref[pl.ds(base + i, 1), :].astype(BF16)
        z_ref[...] = jnp.dot(x_ref[...] * r, packed_ref[:, :D], preferred_element_type=F32)

    def middle(i, k, z_ref, gp_ref, lo, hi, total):
        s = 0.5 * rows_ref[pl.ds(K + base + i, 1), :]
        b = 0.5 * rows_ref[pl.ds(2 * K + base + i, 1), :]
        hb = heads_ref[pl.ds(base + i, 1), :]
        step = 16
        for c in range(lo, hi, step):
            y = z_ref[c:c + step, :] * s + b
            t = jnp.tanh(y)
            a = 1.0 + t
            h = y * a
            d = a + h * (1.0 - t)
            gp = (hb * d).astype(BF16)
            gp_ref[c:c + step, :] = gp
            back_ref, at = (back0_ref, c) if c < half else (back1_ref, c - half)
            back_ref[k, at:at + step, :] = gp
            hh = h * hb
            pred_acc[c:c + step, :] += sum(hh[:, l:l + LANES] for l in range(0, D, LANES))
            q = q_ref[c:c + step, :]
            qh = jnp.concatenate([h[:, l:l + LANES] * q for l in range(0, D, LANES)], axis=1)
            part = sum(qh[j:j + 8] for j in range(0, step, 8))
            total = part if total is None else total + part
        return total

    def outer(gp_ref):
        post_ref[...] = jnp.dot(xq_ref[...], gp_ref[...], preferred_element_type=F32)

    def spread(i, lo, hi, total):
        s = rows_ref[pl.ds(K + base + i, 1), :]
        step = 16
        lane = lax.broadcasted_iota(jnp.int32, (step, LANES), 1)
        for c in range(lo, hi, step):
            g = post_ref[c:c + step, :]
            r = jnp.sum(jnp.where(lane == base + i, cols_ref[c:c + step, :], 0.0), axis=1, keepdims=True)
            t = g * weight_ref[c:c + step, :]
            rt = t * r
            part = sum(rt[j:j + 8] for j in range(0, step, 8))
            total = part if total is None else total + part
            st = t * s
            fold = sum(st[:, l:l + LANES] for l in range(0, D, LANES))
            gr_ref[c:c + step, :] += jnp.where(lane == base + i, jnp.sum(fold, axis=1, keepdims=True), 0.0)
            grads_ref[c:c + step, :D] += (g * s) * r
        return total

    def finish(i, total):
        sums_ref[pl.ds(K + base + i, 1), :] = jnp.sum(total, axis=0, keepdims=True)
        sums_ref[pl.ds(2 * K + base + i, 1), :] = post_ref[D:D + 1, :] + post_ref[D + 1:D + 2, :]

    def member(i, k, now, other, nxt):
        total = middle(i, k, z_refs[now], gp_refs[now], 0, R, None)
        forward(nxt, z_refs[other])
        outer(gp_refs[other])
        heads_grad_ref[pl.ds(base + i, 1), :] = jnp.sum(total, axis=0, keepdims=True)
        finish(i - 1, spread(i - 1, 0, D, None))

    @pl.when(step_id == 0)
    def _():
        set_up()
        forward(0, z_refs[0])

    for k in range(n):
        i, now, other = step_id * n + k, k % 2, (k + 1) % 2
        member(i, k, now, other, jnp.minimum(i + 1, members - 1))

    @pl.when(step_id == steps - 1)
    def _():
        outer(gp_refs[1])
        finish(members - 1, spread(members - 1, 0, D, None))
        for side in range(2):
            at = slice(side * half, (side + 1) * half)
            pred_ref[side:side + 1, :] = jnp.sum(pred_acc[at, :].T, axis=0, keepdims=True)
        grads_ref[:, D:] = sums_ref[...].T + gr_ref[...]
        for j in range(D // (2 * own)):
            low = grads_ref[2 * j * own:(2 * j + 1) * own, :]
            high = grads_ref[(2 * j + 1) * own:(2 * j + 2) * own, :]
            keep_ref[j * own:(j + 1) * own, :] = jnp.where(core == 0, low, high)
            sent_ref[j * own:(j + 1) * own, :] = jnp.where(core == 0, high, low).astype(BF16)


def grad_call(x, q, packed, K, own, n=2):
    R, D = x.shape
    half = R // 2
    members = K // 2
    flops = 4 * members * R * D * D
    return pl.pallas_call(
        functools.partial(grad_kernel, own=own),
        grid=(members // n,),
        out_shape=(
            shape((D // 2, D + LANES)), shape((D // 2, D + LANES), BF16), shape((K, D)), shape((2, half)),
            shape((LANES, D)), shape((D, D), BF16), shape((members, half, D), BF16), shape((members, half, D), BF16),
        ),
        in_specs=[VMEM] * 3,
        out_specs=(VMEM,) * 6 + (pl.BlockSpec((n, half, D), lambda i: (i, 0, 0)),) * 2,
        scratch_shapes=[
            pltpu.VMEM((D, LANES), F32), pltpu.VMEM((K, D), F32), pltpu.VMEM((D, D), F32),
            pltpu.VMEM((D + 16, R), BF16), pltpu.VMEM((R, LANES), F32),
            pltpu.VMEM((R, D), F32), pltpu.VMEM((R, D), F32), pltpu.VMEM((R, D), BF16), pltpu.VMEM((R, D), BF16),
            pltpu.VMEM((D + 16, D), F32), pltpu.VMEM((R, LANES), F32), pltpu.VMEM((LANES, D), F32),
            pltpu.VMEM((D, LANES), F32), pltpu.VMEM((D, D + LANES), F32),
        ],
        compiler_params=pltpu.CompilerParams(vmem_limit_bytes=LIMIT),
        cost_estimate=pl.CostEstimate(flops=2 * flops, bytes_accessed=members * R * D * 2, transcendentals=members * R * D),
        name="member_grads",
    )(x, q, packed)


def back_kernel(*refs, start, first, last):
    rows_ref, turned_ref, gp_hbm = refs[:3]
    rest = list(refs[3:])
    acc_in = None if first else rest.pop(0)
    q_ref = rest.pop(0) if last else None
    if last == "own":
        came_ref, pred_ref, pred_came_ref, count_ref = [rest.pop(0) for _ in range(4)]
        out_ref, pred_out_ref, gp_ref, sems = rest
    else:
        came_ref = None
        out_ref, gp_ref, sems = rest
    n, R, D = gp_ref.shape
    K = 2 * gp_hbm.shape[0]
    base = this_core() * gp_hbm.shape[0] + start
    copies = [
        pltpu.make_async_copy(gp_hbm.at[start + k], gp_ref.at[k], sems.at[k]) for k in range(n)]
    for copy in copies:
        copy.start()
    if q_ref is not None:
        q_wide = jnp.broadcast_to(0.5 * q_ref[...], (LANES, R)).T
    if last == "own":
        lane = lax.broadcasted_iota(jnp.int32, (1, R), 1)
        total = pred_ref[0:1, :] + pred_came_ref[...]
        pred_out_ref[...] = jnp.where(lane < count_ref[0], total, 0.0) * (1.0 / K)
    for k in range(0, n, 2):
        left, right = [], []
        for j in (k, k + 1):
            r = rows_ref[pl.ds(base + j, 1), :].astype(BF16)
            s = rows_ref[pl.ds(K + base + j, 1), :].astype(BF16)
            right.append(turned_ref[...] * r)
            copies[j].wait()
            left.append(gp_ref[j] * s)
        value = jnp.dot(jnp.concatenate(left, axis=1), jnp.concatenate(right, axis=0), preferred_element_type=F32)
        if k or not first:
            value = value + (out_ref if k else acc_in)[...]
        if last and k + 2 == n:
            for l in range(0, D, LANES):
                part = value[:, l:l + LANES] * q_wide
                out_ref[:, l:l + LANES] = part if came_ref is None else part + came_ref[:, l:l + LANES]
        else:
            out_ref[...] = value


def back_call(rows, turned, back, start, count, acc=None, q=None, came=None):
    members, R, D = back.shape
    last = None if q is None else "other" if came is None else "own"
    more = [v for v in (acc, q, *(came or ())) if v is not None]
    specs = [VMEM] * len(more)
    if last == "own":
        specs[-1] = SMEM
    return pl.pallas_call(
        functools.partial(back_kernel, start=start, first=acc is None, last=last),
        out_shape=(shape((R, D)), shape((1, R))) if last == "own" else shape((R, D)),
        in_specs=[VMEM, VMEM, ANY] + specs,
        out_specs=(VMEM, VMEM) if last == "own" else VMEM,
        scratch_shapes=[pltpu.VMEM((count, R, D), BF16), pltpu.SemaphoreType.DMA((count,))],
        compiler_params=pltpu.CompilerParams(vmem_limit_bytes=LIMIT),
        cost_estimate=pl.CostEstimate(flops=2 * count * R * D * D, bytes_accessed=count * R * D * 2, transcendentals=0),
        name="input_grads",
    )(rows, turned, back, *more)


def direction(weight, first_old, second_old, gradient):
    first_new = beta_one * first_old + (1.0 - beta_one) * gradient
    second_new = beta_two * second_old + (1.0 - beta_two) * gradient * gradient
    fix_one = 1.0 - beta_one**STEP
    fix_two = 1.0 - beta_two**STEP
    update = (
        first_new / fix_one / (jnp.sqrt(second_new / fix_two) + epsilon) + weight_decay * weight
    )
    return (first_new, second_new, update)


def lane_sums(value):
    total = jnp.sum(value, axis=0, keepdims=True)
    width = total.shape[1]
    if width < LANES:
        return jnp.concatenate([total, jnp.zeros((1, LANES - width), F32)], axis=1)
    return sum(total[:, l:l + LANES] for l in range(0, width, LANES))


def direction_kernel(low, size, *refs):
    wide_ref = refs[0]
    count = size - 1
    came = refs[1:1 + count]
    (m_ref, m1_ref, m2_ref, a_ref, a1_ref, a2_ref, h_ref, h1_ref, h2_ref,
     m1_out, m2_out, mu_out, a1_out, a2_out, au_out, h1_out, h2_out, hu_out, sums_out) = refs[1 + count:]
    own, D = m_ref.shape
    K = a_ref.shape[2]
    n_heads = h_ref.shape[0]
    place = lax.rem(lax.axis_index("dp") // low, size)
    grad = wide_ref[:own, :]
    for v in range(1, size):
        grad = jnp.where(place == v, wide_ref[v * own:(v + 1) * own, :], grad)
    heads = wide_ref[size * own:size * own + n_heads, :D]
    for c in came:
        grad = grad + c[:own, :].astype(F32)
        heads = heads + c[own:own + n_heads, :D].astype(F32)
    weight_rows, update_rows = [], []
    first, second, update = direction(m_ref[...], m1_ref[...], m2_ref[...], grad[:, :D])
    m1_out[...], m2_out[...], mu_out[...] = first, second, update
    weight_rows.append(lane_sums(m_ref[...] * m_ref[...]))
    update_rows.append(lane_sums(update * update))
    for k in range(3):
        first, second, update = direction(a_ref[k], a1_ref[k], a2_ref[k], grad[:, D + k * K:D + (k + 1) * K])
        a1_out[k], a2_out[k], au_out[k] = first, second, update
        weight_rows.append(lane_sums(a_ref[k] * a_ref[k]))
        update_rows.append(lane_sums(update * update))
    first, second, update = direction(h_ref[...], h1_ref[...], h2_ref[...], heads)
    h1_out[...], h2_out[...], hu_out[...] = first, second, update
    share = 1.0 / lax.axis_size("dp")
    weight_rows.append(lane_sums(h_ref[...] * h_ref[...]) * share)
    update_rows.append(lane_sums(update * update) * share)
    sums_out[...] = jnp.concatenate(weight_rows + update_rows + [jnp.zeros((6, LANES), F32)], axis=0)


def direction_call(wide, came, low, states):
    m, a, h = states[0], states[3], states[6]
    outs = [shape(v.shape) for v in (m, m, m, a, a, a, h, h, h)] + [shape((16, LANES))]
    return pl.pallas_call(
        functools.partial(direction_kernel, low, len(came) + 1),
        out_shape=tuple(outs),
        in_specs=[VMEM] * (1 + len(came) + 9),
        out_specs=tuple([VMEM] * 10),
        compiler_params=SMALL,
        name="directions",
    )(wide, *came, *states)


def update_kernel(count, *refs):
    sums_refs = refs[:count]
    m_ref, a_ref, h_ref, mu_ref, au_ref, hu_ref, m_out, a_out, h_out, norms_out = refs[count:]
    total = sums_refs[0][...]
    for ref in sums_refs[1:]:
        total = total + ref[...]
    norms = jnp.sqrt(jnp.sum(total, axis=1, keepdims=True))
    weight_norm, update_norm = norms[0:5], norms[5:10]
    rate = learn_rate * (weight_norm / update_norm)
    m_out[...] = m_ref[...] - rate[0:1] * mu_ref[...]
    for k in range(3):
        a_out[k] = a_ref[k] - rate[1 + k:2 + k] * au_ref[k]
    h_out[...] = h_ref[...] - rate[4:5] * hu_ref[...]
    row = jnp.sqrt(jnp.sum(total.T, axis=0, keepdims=True))
    norms_out[...] = jnp.concatenate([row[:, 0:5], row[:, 5:10]], axis=0)


def update_call(sums, m, a, h, mu, au, hu):
    return pl.pallas_call(
        functools.partial(update_kernel, len(sums)),
        out_shape=(shape(m.shape), shape(a.shape), shape(h.shape), shape((2, 5))),
        in_specs=[VMEM] * (len(sums) + 6),
        out_specs=(VMEM,) * 4,
        compiler_params=SMALL,
        name="updates",
    )(*sums, m, a, h, mu, au, hu)


def bit_groups(n_dp, n_member):
    def split(low, count):
        bits = count.bit_length() - 1
        groups = []
        while bits > 0:
            take = 2 if bits >= 2 else 1
            bits -= take
            groups.append((low << bits, 1 << take))
        return groups

    return split(n_member, n_dp), split(2, n_member // 2) + [(1, 2)]


def swap(value, total, mask):
    return lax.ppermute(value, AXES, [(i, i ^ mask) for i in range(total)])


def gather_groups(value, groups, total, index, objects, counts, cot, members):
    value, objects, cot = lax.optimization_barrier((value, objects, cot))
    for axis, (low, size) in enumerate(groups):
        place = (index // low) % size
        held = [value] + [swap(value, total, low * m) for m in reversed(range(1, size))][::-1]
        if axis == 0:
            x_other = swap(objects, total, 1)
            held, x_other, objects = lax.optimization_barrier((held, x_other, objects))
        elif axis == 1:
            lane = lax.broadcasted_iota(jnp.int32, cot.shape, 1)
            q = jnp.where(lane < counts[0], cot, 0.0) * (1.0 / members)
            x = jnp.concatenate([objects, x_other], axis=0)
            held, x, q = lax.optimization_barrier((held, x, q))
        elif axis == len(groups) - 1:
            q_other = swap(q, total, 1)
            held, q_other = lax.optimization_barrier((held, q_other))
            q = jnp.concatenate([q, q_other], axis=1)
        value = jnp.stack([lax.select_n(place ^ p, *held) for p in range(size)], axis=axis)
    return value, x, q


def beside(sends, work, *inputs):
    values, inputs = lax.optimization_barrier(([v for v, _, _ in sends], inputs))
    came = [swap(v, total, mask) for v, (_, total, mask) in reversed(list(zip(values, sends)))][::-1]
    done = work(*inputs)
    return lax.optimization_barrier((came, done))


def shards(n_dp, n_member, objects, counts, cotangent, matrix, matrix_first, matrix_second,
           adapters, adapter_first, adapter_second, head_weights, head_first, head_second):
    R, D = objects.shape
    K = adapters.shape[1]
    own, own_heads = matrix.shape[0], head_weights.shape[0]
    total = n_dp * n_member
    index = lax.axis_index("dp") * n_member + lax.axis_index("member")
    dp_groups, member_groups = bit_groups(n_dp, n_member)
    chip_groups = member_groups[:-1]
    turned = [v.transpose(0, 2, 1) for v in (adapters, adapter_first, adapter_second)]

    packed = pack_call(matrix, turned[0], head_weights)
    full, x_both, q_both = gather_groups(
        packed, dp_groups + member_groups, total, index, objects, counts, cotangent.reshape(1, R), K)
    full = full.reshape(D, -1)
    q_own, q_other = q_both[:, :R], q_both[:, R:]
    keep, sent, head_grads, preds, rows, wide_turned, back_own, back_other = grad_call(x_both, q_both, full, K, own)

    chips = [size for _, size in chip_groups]
    head_grads = head_grads.reshape(chips + [2, own_heads, D])
    core = index % 2
    axis = len(chips)
    members = K // 2

    def arrange(main, heads):
        main = main.reshape([n_dp] + chips + [own, D + LANES])
        main = jnp.moveaxis(main, 0, len(chips)).reshape(chips + [n_dp * own, D + LANES])
        return jnp.concatenate([main, jnp.pad(heads, [(0, 0)] * (len(chips) + 1) + [(0, LANES)])], axis=len(chips))

    def backward(start, count, **more):
        def work(rows, wide_turned, back, *acc):
            return back_call(rows, wide_turned, back, start, count, *acc, **more)
        return work

    weights = (rows, wide_turned, back_other)
    other_heads = lax.dynamic_index_in_dim(head_grads, 1 - core, axis, keepdims=False)
    own_heads_grad = lax.dynamic_index_in_dim(head_grads, core, axis, keepdims=False)
    (came, pred_came), acc = beside(
        [(arrange(sent, other_heads.astype(BF16)), total, 1), (preds[1:2], total, 1)], backward(0, 2), *weights)
    wide = arrange(keep, own_heads_grad) + came.astype(F32)
    for axis in reversed(range(len(chips))):
        low, size = chip_groups[axis]
        place = (index // low) % size
        part = [lax.dynamic_index_in_dim(wide, place ^ m, axis, keepdims=False) for m in range(size)]
        sends = [(part[m].astype(BF16), total, low * m) for m in range(1, size)]
        if axis == len(chips) - 1:
            came, acc = beside(sends, backward(2, 8), *weights, acc)
        else:
            came = [swap(*send) for send in sends]
        wide = part[0]
        for c in came:
            wide = wide + c.astype(F32)
    for axis in reversed(range(len(dp_groups))):
        low, size = dp_groups[axis]
        place = (index // low) % size
        outer_count = (wide.shape[0] - own_heads) // (own * size)
        main = wide[:-own_heads].reshape(outer_count, size * own, D + LANES)
        heads = wide[-own_heads:]

        def chunk(v):
            at = lax.dynamic_slice_in_dim(main, v * own, own, 1)
            return jnp.concatenate([at.reshape(-1, D + LANES), heads], axis=0)

        sends = [(chunk(place ^ m).astype(BF16), total, low * m) for m in range(1, size)]
        if axis == len(dp_groups) - 1:
            last, acc = beside(sends, backward(10, 6, q=q_other), *weights, acc)
        else:
            last = [swap(*send) for send in sends]
        if axis:
            wide = chunk(place)
            for c in last:
                wide = wide + c.astype(F32)
    ig_came = swap(acc, total, 1)

    states = [matrix, matrix_first, matrix_second, *turned, head_weights, head_first, head_second]
    (m_first, m_second, m_update, a_first, a_second, a_update, h_first, h_second, h_update, sums) = direction_call(
        wide, last, dp_groups[0][0] // n_member, states)

    rounds = [(1, 2)] + chip_groups[::-1] + dp_groups[::-1]
    plan = {0: backward(0, 2), 1: backward(2, 6), len(rounds) - 1: backward(8, 8, q=q_own, came=(ig_came, preds, pred_came, counts))}
    pending, acc = [sums], ()
    for step, (low, size) in enumerate(rounds):
        sums = pending[0]
        for p in pending[1:]:
            sums = sums + p
        sends = [(sums, total, low * m) for m in range(1, size)]
        if step in plan:
            came, acc = beside(sends, plan[step], rows, wide_turned, back_own, *acc)
            acc = (acc,)
        else:
            came = [swap(*send) for send in sends]
        pending = [sums] + list(came)
    input_grad, predictions = acc[0]
    new_matrix, new_adapters, new_heads, norm_pairs = update_call(
        pending, matrix, turned[0], head_weights, m_update, a_update, h_update)

    def back_turn(v):
        return v.transpose(0, 2, 1)

    return (predictions.reshape(R), input_grad, new_matrix, m_first, m_second, back_turn(new_adapters),
            back_turn(a_first), back_turn(a_second), new_heads, h_first, h_second, norm_pairs.T)


def solution(mesh):
    n_dp, n_member = mesh.shape["dp"], mesh.shape["member"]
    rows, cols = P(AXES, None), P(None, None, AXES)
    heads = P("member", None)
    return jax.shard_map(
        functools.partial(shards, n_dp, n_member),
        mesh=mesh,
        in_specs=(rows, P(AXES), P(AXES), rows, rows, rows, cols, cols, cols, heads, heads, heads),
        out_specs=(P(AXES), rows, rows, rows, rows, cols, cols, cols, heads, heads, heads, P()),
        check_vma=False,
    )
```

```python
import functools

import jax
import jax.numpy as jnp
from jax import lax
from jax.experimental import pallas as pl
from jax.experimental.pallas import tpu as pltpu
from jax.sharding import PartitionSpec as P

LANES = 128
F32, BF16 = jnp.float32, jnp.bfloat16
STEP = 10
beta_one = 0.5
beta_two = 0.5
epsilon = 1e-06
weight_decay = 0.01
learn_rate = 0.25
AXES = ("dp", "member")
VMEM = pl.BlockSpec(memory_space=pltpu.VMEM)
SMEM = pl.BlockSpec(memory_space=pltpu.SMEM)
ANY = pl.BlockSpec(memory_space=pl.ANY)
LIMIT = 48 * 1024 * 1024
SMALL = pltpu.CompilerParams(vmem_limit_bytes=8 * 1024 * 1024)


def shape(dims, dtype=F32):
    return jax.ShapeDtypeStruct(dims, dtype)


def this_core():
    return lax.rem(lax.axis_index("member"), 2)


def pack_kernel(matrix_ref, adapters_ref, heads_ref, packed_ref):
    own, D = matrix_ref.shape
    K = adapters_ref.shape[2]
    packed_ref[:, :D] = matrix_ref[...].astype(BF16)
    parts = [adapters_ref[k] for k in range(3)] + [jnp.zeros((own, LANES - 3 * K), F32)]
    packed_ref[:, D:D + LANES] = jnp.concatenate(parts, axis=1).astype(BF16)
    L = packed_ref.shape[1] - D - LANES
    rows = []
    for t in range(own):
        h, c = divmod(t * L, D)
        rows.append(heads_ref[h:h + 1, c:c + L])
    packed_ref[:, D + LANES:] = jnp.concatenate(rows, axis=0).astype(BF16)


def pack_call(matrix, adapters_t, heads):
    own, D = matrix.shape
    L = heads.shape[0] * D // own
    return pl.pallas_call(
        pack_kernel,
        out_shape=shape((own, D + LANES + L), BF16),
        in_specs=[VMEM] * 3,
        out_specs=VMEM,
        name="pack_weights",
    )(matrix, adapters_t, heads)


def grad_kernel(
    x_ref, rows_q_ref, packed_ref,
    keep_ref, sent_ref, heads_grad_ref, pred_ref, rows_ref, turned_ref, back0_ref, back1_ref,
    cols_ref, heads_ref, weight_ref, xq_ref, q_ref, z0_ref, z1_ref, gp0_ref, gp1_ref,
    post_ref, pred_acc, sums_ref, gr_ref, grads_ref, *, own,
):
    R, D = x_ref.shape
    half = R // 2
    K = heads_grad_ref.shape[0]
    members = K // 2
    n = back0_ref.shape[0]
    step_id, steps = pl.program_id(0), pl.num_programs(0)
    core = this_core()
    base = core * members
    z_refs, gp_refs = (z0_ref, z1_ref), (gp0_ref, gp1_ref)

    def set_up():
        weight_ref[...] = packed_ref[:, :D].astype(F32)
        cols = packed_ref[:, D:D + LANES].astype(F32)
        cols_ref[...] = cols
        rows_ref[...] = cols.T
        turned_ref[...] = packed_ref[:, :D].T
        L = packed_ref.shape[1] - D - LANES
        per_head = D // L
        for c in range(0, L, LANES):
            gr_ref[:K * per_head, :] = packed_ref[:K * per_head, D + LANES + c:D + 2 * LANES + c].astype(F32)
            for k in range(per_head):
                heads_ref[:, k * L + c:k * L + c + LANES] = gr_ref[pl.ds(k, K, stride=per_head), :]
        for ref in (pred_acc, gr_ref, sums_ref, grads_ref, gp1_ref, heads_grad_ref):
            ref[...] = jnp.zeros_like(ref)
        q_row = rows_q_ref[...]
        q_ref[...] = jnp.broadcast_to(q_row, (LANES, R)).T
        half_q = 0.5 * q_row
        q_hi = half_q.astype(BF16)
        q_lo = (half_q - q_hi.astype(F32)).astype(BF16)
        xq_ref[:D, :] = (x_ref[...].T.astype(F32) * half_q).astype(BF16)
        sub = lax.broadcasted_iota(jnp.int32, (16, R), 0)
        extra = jnp.where(sub == 0, q_hi.astype(F32), jnp.where(sub == 1, q_lo.astype(F32), 0.0))
        xq_ref[D:, :] = extra.astype(BF16)

    def forward(i, z_ref):
        r = rows_ref[pl.ds(base + i, 1), :].astype(BF16)
        z_ref[...] = jnp.dot(x_ref[...] * r, packed_ref[:, :D], preferred_element_type=F32)

    def middle(i, k, z_ref, gp_ref, lo, hi, total):
        s = 0.5 * rows_ref[pl.ds(K + base + i, 1), :]
        b = 0.5 * rows_ref[pl.ds(2 * K + base + i, 1), :]
        hb = heads_ref[pl.ds(base + i, 1), :]
        step = 16
        for c in range(lo, hi, step):
            y = z_ref[c:c + step, :] * s + b
            t = jnp.tanh(y)
            a = 1.0 + t
            h = y * a
            d = a + h * (1.0 - t)
            gp = (hb * d).astype(BF16)
            gp_ref[c:c + step, :] = gp
            back_ref, at = (back0_ref, c) if c < half else (back1_ref, c - half)
            back_ref[k, at:at + step, :] = gp
            hh = h * hb
            pred_acc[c:c + step, :] += sum(hh[:, l:l + LANES] for l in range(0, D, LANES))
            q = q_ref[c:c + step, :]
            qh = jnp.concatenate([h[:, l:l + LANES] * q for l in range(0, D, LANES)], axis=1)
            part = sum(qh[j:j + 8] for j in range(0, step, 8))
            total = part if total is None else total + part
        return total

    def outer(gp_ref):
        post_ref[...] = jnp.dot(xq_ref[...], gp_ref[...], preferred_element_type=F32)

    def spread(i, lo, hi, total):
        s_row = rows_ref[pl.ds(K + base + i, 1), :]
        step, width = 16, 2 * LANES
        lane = lax.broadcasted_iota(jnp.int32, (step, LANES), 1)
        totals = []
        for w in range(0, D, width):
            s, total = s_row[:, w:w + width], None
            for c in range(lo, hi, step):
                g = post_ref[c:c + step, w:w + width]
                r = jnp.sum(jnp.where(lane == base + i, cols_ref[c:c + step, :], 0.0), axis=1, keepdims=True)
                t = g * weight_ref[c:c + step, w:w + width]
                rt = t * r
                part = sum(rt[j:j + 8] for j in range(0, step, 8))
                total = part if total is None else total + part
                st = t * s
                fold = sum(st[:, l:l + LANES] for l in range(0, width, LANES))
                gr_ref[c:c + step, :] += jnp.where(lane == base + i, jnp.sum(fold, axis=1, keepdims=True), 0.0)
                grads_ref[c:c + step, w:w + width] += (g * s) * r
            totals.append(total)
        return jnp.concatenate(totals, axis=1)

    def finish(i, total):
        sums_ref[pl.ds(K + base + i, 1), :] = jnp.sum(total, axis=0, keepdims=True)
        sums_ref[pl.ds(2 * K + base + i, 1), :] = post_ref[D:D + 1, :] + post_ref[D + 1:D + 2, :]

    def member(i, k, now, other, nxt):
        total = middle(i, k, z_refs[now], gp_refs[now], 0, R, None)
        forward(nxt, z_refs[other])
        outer(gp_refs[other])
        heads_grad_ref[pl.ds(base + i, 1), :] = jnp.sum(total, axis=0, keepdims=True)
        finish(i - 1, spread(i - 1, 0, D, None))

    @pl.when(step_id == 0)
    def _():
        set_up()
        forward(0, z_refs[0])

    for k in range(n):
        i, now, other = step_id * n + k, k % 2, (k + 1) % 2
        member(i, k, now, other, jnp.minimum(i + 1, members - 1))

    @pl.when(step_id == steps - 1)
    def _():
        outer(gp_refs[1])
        finish(members - 1, spread(members - 1, 0, D, None))
        for side in range(2):
            at = slice(side * half, (side + 1) * half)
            pred_ref[side:side + 1, :] = jnp.sum(pred_acc[at, :].T, axis=0, keepdims=True)
        grads_ref[:, D:] = sums_ref[...].T + gr_ref[...]
        for j in range(D // (2 * own)):
            low = grads_ref[2 * j * own:(2 * j + 1) * own, :]
            high = grads_ref[(2 * j + 1) * own:(2 * j + 2) * own, :]
            keep_ref[j * own:(j + 1) * own, :] = jnp.where(core == 0, low, high)
            sent_ref[j * own:(j + 1) * own, :] = jnp.where(core == 0, high, low).astype(BF16)


def grad_call(x, q, packed, K, own, n=2):
    R, D = x.shape
    half = R // 2
    members = K // 2
    flops = 4 * members * R * D * D
    return pl.pallas_call(
        functools.partial(grad_kernel, own=own),
        grid=(members // n,),
        out_shape=(
            shape((D // 2, D + LANES)), shape((D // 2, D + LANES), BF16), shape((K, D)), shape((2, half)),
            shape((LANES, D)), shape((D, D), BF16), shape((members, half, D), BF16), shape((members, half, D), BF16),
        ),
        in_specs=[VMEM] * 3,
        out_specs=(VMEM,) * 6 + (pl.BlockSpec((n, half, D), lambda i: (i, 0, 0)),) * 2,
        scratch_shapes=[
            pltpu.VMEM((D, LANES), F32), pltpu.VMEM((K, D), F32), pltpu.VMEM((D, D), F32),
            pltpu.VMEM((D + 16, R), BF16), pltpu.VMEM((R, LANES), F32),
            pltpu.VMEM((R, D), F32), pltpu.VMEM((R, D), F32), pltpu.VMEM((R, D), BF16), pltpu.VMEM((R, D), BF16),
            pltpu.VMEM((D + 16, D), F32), pltpu.VMEM((R, LANES), F32), pltpu.VMEM((LANES, D), F32),
            pltpu.VMEM((D, LANES), F32), pltpu.VMEM((D, D + LANES), F32),
        ],
        compiler_params=pltpu.CompilerParams(vmem_limit_bytes=LIMIT),
        cost_estimate=pl.CostEstimate(flops=2 * flops, bytes_accessed=members * R * D * 2, transcendentals=members * R * D),
        name="member_grads",
    )(x, q, packed)


def back_kernel(*refs, start, first, last):
    rows_ref, turned_ref, gp_hbm = refs[:3]
    rest = list(refs[3:])
    acc_in = None if first else rest.pop(0)
    q_ref = rest.pop(0) if last else None
    if last == "own":
        came_ref, pred_ref, pred_came_ref, count_ref = [rest.pop(0) for _ in range(4)]
        out_ref, pred_out_ref, gp_ref, sems = rest
    else:
        came_ref = None
        out_ref, gp_ref, sems = rest
    n, R, D = gp_ref.shape
    K = 2 * gp_hbm.shape[0]
    base = this_core() * gp_hbm.shape[0] + start
    copies = [
        pltpu.make_async_copy(gp_hbm.at[start + k], gp_ref.at[k], sems.at[k]) for k in range(n)]
    for copy in copies:
        copy.start()
    if q_ref is not None:
        q_wide = jnp.broadcast_to(0.5 * q_ref[...], (LANES, R)).T
    if last == "own":
        lane = lax.broadcasted_iota(jnp.int32, (1, R), 1)
        total = pred_ref[0:1, :] + pred_came_ref[...]
        pred_out_ref[...] = jnp.where(lane < count_ref[0], total, 0.0) * (1.0 / K)
    for k in range(0, n, 2):
        left, right = [], []
        for j in (k, k + 1):
            r = rows_ref[pl.ds(base + j, 1), :].astype(BF16)
            s = rows_ref[pl.ds(K + base + j, 1), :].astype(BF16)
            right.append(turned_ref[...] * r)
            copies[j].wait()
            left.append(gp_ref[j] * s)
        value = jnp.dot(jnp.concatenate(left, axis=1), jnp.concatenate(right, axis=0), preferred_element_type=F32)
        if k or not first:
            value = value + (out_ref if k else acc_in)[...]
        if last and k + 2 == n:
            for l in range(0, D, LANES):
                part = value[:, l:l + LANES] * q_wide
                out_ref[:, l:l + LANES] = part if came_ref is None else part + came_ref[:, l:l + LANES]
        else:
            out_ref[...] = value


def back_call(rows, turned, back, start, count, acc=None, q=None, came=None):
    members, R, D = back.shape
    last = None if q is None else "other" if came is None else "own"
    more = [v for v in (acc, q, *(came or ())) if v is not None]
    specs = [VMEM] * len(more)
    if last == "own":
        specs[-1] = SMEM
    return pl.pallas_call(
        functools.partial(back_kernel, start=start, first=acc is None, last=last),
        out_shape=(shape((R, D)), shape((1, R))) if last == "own" else shape((R, D)),
        in_specs=[VMEM, VMEM, ANY] + specs,
        out_specs=(VMEM, VMEM) if last == "own" else VMEM,
        scratch_shapes=[pltpu.VMEM((count, R, D), BF16), pltpu.SemaphoreType.DMA((count,))],
        compiler_params=pltpu.CompilerParams(vmem_limit_bytes=LIMIT),
        cost_estimate=pl.CostEstimate(flops=2 * count * R * D * D, bytes_accessed=count * R * D * 2, transcendentals=0),
        name="input_grads",
    )(rows, turned, back, *more)


def direction(weight, first_old, second_old, gradient):
    first_new = beta_one * first_old + (1.0 - beta_one) * gradient
    second_new = beta_two * second_old + (1.0 - beta_two) * gradient * gradient
    fix_one = 1.0 - beta_one**STEP
    fix_two = 1.0 - beta_two**STEP
    update = (
        first_new / fix_one / (jnp.sqrt(second_new / fix_two) + epsilon) + weight_decay * weight
    )
    return (first_new, second_new, update)


def lane_sums(value):
    total = jnp.sum(value, axis=0, keepdims=True)
    width = total.shape[1]
    if width < LANES:
        return jnp.concatenate([total, jnp.zeros((1, LANES - width), F32)], axis=1)
    return sum(total[:, l:l + LANES] for l in range(0, width, LANES))


def direction_kernel(low, size, *refs):
    wide_ref = refs[0]
    count = size - 1
    came = refs[1:1 + count]
    (m_ref, m1_ref, m2_ref, a_ref, a1_ref, a2_ref, h_ref, h1_ref, h2_ref,
     m1_out, m2_out, mu_out, a1_out, a2_out, au_out, h1_out, h2_out, hu_out, sums_out) = refs[1 + count:]
    own, D = m_ref.shape
    K = a_ref.shape[2]
    n_heads = h_ref.shape[0]
    place = lax.rem(lax.axis_index("dp") // low, size)
    grad = wide_ref[:own, :]
    for v in range(1, size):
        grad = jnp.where(place == v, wide_ref[v * own:(v + 1) * own, :], grad)
    heads = wide_ref[size * own:size * own + n_heads, :D]
    for c in came:
        grad = grad + c[:own, :].astype(F32)
        heads = heads + c[own:own + n_heads, :D].astype(F32)
    weight_rows, update_rows = [], []
    first, second, update = direction(m_ref[...], m1_ref[...], m2_ref[...], grad[:, :D])
    m1_out[...], m2_out[...], mu_out[...] = first, second, update
    weight_rows.append(lane_sums(m_ref[...] * m_ref[...]))
    update_rows.append(lane_sums(update * update))
    for k in range(3):
        first, second, update = direction(a_ref[k], a1_ref[k], a2_ref[k], grad[:, D + k * K:D + (k + 1) * K])
        a1_out[k], a2_out[k], au_out[k] = first, second, update
        weight_rows.append(lane_sums(a_ref[k] * a_ref[k]))
        update_rows.append(lane_sums(update * update))
    first, second, update = direction(h_ref[...], h1_ref[...], h2_ref[...], heads)
    h1_out[...], h2_out[...], hu_out[...] = first, second, update
    share = 1.0 / lax.axis_size("dp")
    weight_rows.append(lane_sums(h_ref[...] * h_ref[...]) * share)
    update_rows.append(lane_sums(update * update) * share)
    sums_out[...] = jnp.concatenate(weight_rows + update_rows + [jnp.zeros((6, LANES), F32)], axis=0)


def direction_call(wide, came, low, states):
    m, a, h = states[0], states[3], states[6]
    outs = [shape(v.shape) for v in (m, m, m, a, a, a, h, h, h)] + [shape((16, LANES))]
    return pl.pallas_call(
        functools.partial(direction_kernel, low, len(came) + 1),
        out_shape=tuple(outs),
        in_specs=[VMEM] * (1 + len(came) + 9),
        out_specs=tuple([VMEM] * 10),
        compiler_params=SMALL,
        name="directions",
    )(wide, *came, *states)


def update_kernel(count, *refs):
    sums_refs = refs[:count]
    m_ref, a_ref, h_ref, mu_ref, au_ref, hu_ref, m_out, a_out, h_out, norms_out = refs[count:]
    total = sums_refs[0][...]
    for ref in sums_refs[1:]:
        total = total + ref[...]
    norms = jnp.sqrt(jnp.sum(total, axis=1, keepdims=True))
    weight_norm, update_norm = norms[0:5], norms[5:10]
    rate = learn_rate * (weight_norm / update_norm)
    m_out[...] = m_ref[...] - rate[0:1] * mu_ref[...]
    for k in range(3):
        a_out[k] = a_ref[k] - rate[1 + k:2 + k] * au_ref[k]
    h_out[...] = h_ref[...] - rate[4:5] * hu_ref[...]
    row = jnp.sqrt(jnp.sum(total.T, axis=0, keepdims=True))
    norms_out[...] = jnp.concatenate([row[:, 0:5], row[:, 5:10]], axis=0)


def update_call(sums, m, a, h, mu, au, hu):
    return pl.pallas_call(
        functools.partial(update_kernel, len(sums)),
        out_shape=(shape(m.shape), shape(a.shape), shape(h.shape), shape((2, 5))),
        in_specs=[VMEM] * (len(sums) + 6),
        out_specs=(VMEM,) * 4,
        compiler_params=SMALL,
        name="updates",
    )(*sums, m, a, h, mu, au, hu)


def bit_groups(n_dp, n_member):
    def split(low, count):
        bits = count.bit_length() - 1
        groups = []
        while bits > 0:
            take = 2 if bits >= 2 else 1
            bits -= take
            groups.append((low << bits, 1 << take))
        return groups

    return split(n_member, n_dp), split(2, n_member // 2) + [(1, 2)]


def swap(value, total, mask):
    return lax.ppermute(value, AXES, [(i, i ^ mask) for i in range(total)])


def gather_groups(value, groups, total, index, objects, counts, cot, members):
    value, objects, cot = lax.optimization_barrier((value, objects, cot))
    for axis, (low, size) in enumerate(groups):
        place = (index // low) % size
        held = [value] + [swap(value, total, low * m) for m in reversed(range(1, size))][::-1]
        if axis == 0:
            x_other = swap(objects, total, 1)
            held, x_other, objects = lax.optimization_barrier((held, x_other, objects))
        elif axis == 1:
            lane = lax.broadcasted_iota(jnp.int32, cot.shape, 1)
            q = jnp.where(lane < counts[0], cot, 0.0) * (1.0 / members)
            x = jnp.concatenate([objects, x_other], axis=0)
            held, x, q = lax.optimization_barrier((held, x, q))
        elif axis == len(groups) - 1:
            q_other = swap(q, total, 1)
            held, q_other = lax.optimization_barrier((held, q_other))
            q = jnp.concatenate([q, q_other], axis=1)
        value = jnp.stack([lax.select_n(place ^ p, *held) for p in range(size)], axis=axis)
    return value, x, q


def beside(sends, work, *inputs):
    values, inputs = lax.optimization_barrier(([v for v, _, _ in sends], inputs))
    came = [swap(v, total, mask) for v, (_, total, mask) in reversed(list(zip(values, sends)))][::-1]
    done = work(*inputs)
    return lax.optimization_barrier((came, done))


def shards(n_dp, n_member, objects, counts, cotangent, matrix, matrix_first, matrix_second,
           adapters, adapter_first, adapter_second, head_weights, head_first, head_second):
    R, D = objects.shape
    K = adapters.shape[1]
    own, own_heads = matrix.shape[0], head_weights.shape[0]
    total = n_dp * n_member
    index = lax.axis_index("dp") * n_member + lax.axis_index("member")
    dp_groups, member_groups = bit_groups(n_dp, n_member)
    chip_groups = member_groups[:-1]
    turned = [v.transpose(0, 2, 1) for v in (adapters, adapter_first, adapter_second)]

    packed = pack_call(matrix, turned[0], head_weights)
    full, x_both, q_both = gather_groups(
        packed, dp_groups + member_groups, total, index, objects, counts, cotangent.reshape(1, R), K)
    full = full.reshape(D, -1)
    q_own, q_other = q_both[:, :R], q_both[:, R:]
    keep, sent, head_grads, preds, rows, wide_turned, back_own, back_other = grad_call(x_both, q_both, full, K, own)

    chips = [size for _, size in chip_groups]
    head_grads = head_grads.reshape(chips + [2, own_heads, D])
    core = index % 2
    axis = len(chips)
    members = K // 2

    def arrange(main, heads):
        main = main.reshape([n_dp] + chips + [own, D + LANES])
        main = jnp.moveaxis(main, 0, len(chips)).reshape(chips + [n_dp * own, D + LANES])
        return jnp.concatenate([main, jnp.pad(heads, [(0, 0)] * (len(chips) + 1) + [(0, LANES)])], axis=len(chips))

    def backward(start, count, **more):
        def work(rows, wide_turned, back, *acc):
            return back_call(rows, wide_turned, back, start, count, *acc, **more)
        return work

    weights = (rows, wide_turned, back_other)
    other_heads = lax.dynamic_index_in_dim(head_grads, 1 - core, axis, keepdims=False)
    own_heads_grad = lax.dynamic_index_in_dim(head_grads, core, axis, keepdims=False)
    (came, pred_came), acc = beside(
        [(arrange(sent, other_heads.astype(BF16)), total, 1), (preds[1:2], total, 1)], backward(0, 2), *weights)
    wide = arrange(keep, own_heads_grad) + came.astype(F32)
    for axis in reversed(range(len(chips))):
        low, size = chip_groups[axis]
        place = (index // low) % size
        part = [lax.dynamic_index_in_dim(wide, place ^ m, axis, keepdims=False) for m in range(size)]
        sends = [(part[m].astype(BF16), total, low * m) for m in range(1, size)]
        if axis == len(chips) - 1:
            came, acc = beside(sends, backward(2, 8), *weights, acc)
        else:
            came = [swap(*send) for send in sends]
        wide = part[0]
        for c in came:
            wide = wide + c.astype(F32)
    for axis in reversed(range(len(dp_groups))):
        low, size = dp_groups[axis]
        place = (index // low) % size
        outer_count = (wide.shape[0] - own_heads) // (own * size)
        main = wide[:-own_heads].reshape(outer_count, size * own, D + LANES)
        heads = wide[-own_heads:]

        def chunk(v):
            at = lax.dynamic_slice_in_dim(main, v * own, own, 1)
            return jnp.concatenate([at.reshape(-1, D + LANES), heads], axis=0)

        sends = [(chunk(place ^ m).astype(BF16), total, low * m) for m in range(1, size)]
        if axis == len(dp_groups) - 1:
            last, acc = beside(sends, backward(10, 6, q=q_other), *weights, acc)
        else:
            last = [swap(*send) for send in sends]
        if axis:
            wide = chunk(place)
            for c in last:
                wide = wide + c.astype(F32)
    ig_came = swap(acc, total, 1)

    states = [matrix, matrix_first, matrix_second, *turned, head_weights, head_first, head_second]
    (m_first, m_second, m_update, a_first, a_second, a_update, h_first, h_second, h_update, sums) = direction_call(
        wide, last, dp_groups[0][0] // n_member, states)

    rounds = [(1, 2)] + chip_groups[::-1] + dp_groups[::-1]
    plan = {0: backward(0, 2), 1: backward(2, 6), len(rounds) - 1: backward(8, 8, q=q_own, came=(ig_came, preds, pred_came, counts))}
    pending, acc = [sums], ()
    for step, (low, size) in enumerate(rounds):
        sums = pending[0]
        for p in pending[1:]:
            sums = sums + p
        sends = [(sums, total, low * m) for m in range(1, size)]
        if step in plan:
            came, acc = beside(sends, plan[step], rows, wide_turned, back_own, *acc)
            acc = (acc,)
        else:
            came = [swap(*send) for send in sends]
        pending = [sums] + list(came)
    input_grad, predictions = acc[0]
    new_matrix, new_adapters, new_heads, norm_pairs = update_call(
        pending, matrix, turned[0], head_weights, m_update, a_update, h_update)

    def back_turn(v):
        return v.transpose(0, 2, 1)

    return (predictions.reshape(R), input_grad, new_matrix, m_first, m_second, back_turn(new_adapters),
            back_turn(a_first), back_turn(a_second), new_heads, h_first, h_second, norm_pairs.T)


def solution(mesh):
    n_dp, n_member = mesh.shape["dp"], mesh.shape["member"]
    rows, cols = P(AXES, None), P(None, None, AXES)
    heads = P("member", None)
    return jax.shard_map(
        functools.partial(shards, n_dp, n_member),
        mesh=mesh,
        in_specs=(rows, P(AXES), P(AXES), rows, rows, rows, cols, cols, cols, heads, heads, heads),
        out_specs=(P(AXES), rows, rows, rows, rows, cols, cols, cols, heads, heads, heads, P()),
        check_vma=False,
    )
```

```python
import functools

import jax
import jax.numpy as jnp
from jax import lax
from jax.experimental import pallas as pl
from jax.experimental.pallas import tpu as pltpu
from jax.sharding import PartitionSpec as P

LANES = 128
F32, BF16 = jnp.float32, jnp.bfloat16
STEP = 10
beta_one = 0.5
beta_two = 0.5
epsilon = 1e-06
weight_decay = 0.01
learn_rate = 0.25
AXES = ("dp", "member")
VMEM = pl.BlockSpec(memory_space=pltpu.VMEM)
SMEM = pl.BlockSpec(memory_space=pltpu.SMEM)
ANY = pl.BlockSpec(memory_space=pl.ANY)
LIMIT = 48 * 1024 * 1024
SMALL = pltpu.CompilerParams(vmem_limit_bytes=8 * 1024 * 1024)


def shape(dims, dtype=F32):
    return jax.ShapeDtypeStruct(dims, dtype)


def this_core():
    return lax.rem(lax.axis_index("member"), 2)


def pack_kernel(matrix_ref, adapters_ref, heads_ref, packed_ref):
    own, D = matrix_ref.shape
    K = adapters_ref.shape[2]
    packed_ref[:, :D] = matrix_ref[...].astype(BF16)
    parts = [adapters_ref[k] for k in range(3)] + [jnp.zeros((own, LANES - 3 * K), F32)]
    packed_ref[:, D:D + LANES] = jnp.concatenate(parts, axis=1).astype(BF16)
    L = packed_ref.shape[1] - D - LANES
    rows = []
    for t in range(own):
        h, c = divmod(t * L, D)
        rows.append(heads_ref[h:h + 1, c:c + L])
    packed_ref[:, D + LANES:] = jnp.concatenate(rows, axis=0).astype(BF16)


def pack_call(matrix, adapters_t, heads):
    own, D = matrix.shape
    L = heads.shape[0] * D // own
    return pl.pallas_call(
        pack_kernel,
        out_shape=shape((own, D + LANES + L), BF16),
        in_specs=[VMEM] * 3,
        out_specs=VMEM,
        name="pack_weights",
    )(matrix, adapters_t, heads)


def grad_kernel(
    x_ref, rows_q_ref, packed_ref,
    keep_ref, sent_ref, heads_grad_ref, pred_ref, rows_ref, turned_ref, back0_ref, back1_ref,
    cols_ref, heads_ref, weight_ref, xq_ref, q_ref, z0_ref, z1_ref, gp0_ref, gp1_ref,
    post_ref, pred_acc, sums_ref, gr_ref, grads_ref, *, own,
):
    R, D = x_ref.shape
    half = R // 2
    K = heads_grad_ref.shape[0]
    members = K // 2
    n = back0_ref.shape[0]
    step_id, steps = pl.program_id(0), pl.num_programs(0)
    core = this_core()
    base = core * members
    z_refs, gp_refs = (z0_ref, z1_ref), (gp0_ref, gp1_ref)

    def set_up():
        weight_ref[...] = packed_ref[:, :D].astype(F32)
        cols = packed_ref[:, D:D + LANES].astype(F32)
        cols_ref[...] = cols
        rows_ref[...] = cols.T
        turned_ref[...] = packed_ref[:, :D].T
        L = packed_ref.shape[1] - D - LANES
        per_head = D // L
        for c in range(0, L, LANES):
            gr_ref[:K * per_head, :] = packed_ref[:K * per_head, D + LANES + c:D + 2 * LANES + c].astype(F32)
            for k in range(per_head):
                heads_ref[:, k * L + c:k * L + c + LANES] = gr_ref[pl.ds(k, K, stride=per_head), :]
        for ref in (pred_acc, gr_ref, sums_ref, grads_ref, gp1_ref, heads_grad_ref):
            ref[...] = jnp.zeros_like(ref)
        q_row = rows_q_ref[...]
        q_ref[...] = jnp.broadcast_to(q_row, (LANES, R)).T
        half_q = 0.5 * q_row
        q_hi = half_q.astype(BF16)
        q_lo = (half_q - q_hi.astype(F32)).astype(BF16)
        xq_ref[:D, :] = (x_ref[...].T.astype(F32) * half_q).astype(BF16)
        sub = lax.broadcasted_iota(jnp.int32, (16, R), 0)
        extra = jnp.where(sub == 0, q_hi.astype(F32), jnp.where(sub == 1, q_lo.astype(F32), 0.0))
        xq_ref[D:, :] = extra.astype(BF16)

    def forward(i, z_ref):
        r = rows_ref[pl.ds(base + i, 1), :].astype(BF16)
        z_ref[...] = jnp.dot(x_ref[...] * r, packed_ref[:, :D], preferred_element_type=F32)

    def middle(i, k, z_ref, gp_ref, lo, hi, total):
        s = 0.5 * rows_ref[pl.ds(K + base + i, 1), :]
        b = 0.5 * rows_ref[pl.ds(2 * K + base + i, 1), :]
        hb = heads_ref[pl.ds(base + i, 1), :]
        step = 16
        for c in range(lo, hi, step):
            y = z_ref[c:c + step, :] * s + b
            t = jnp.tanh(y)
            a = 1.0 + t
            h = y * a
            d = a + h * (1.0 - t)
            gp = (hb * d).astype(BF16)
            gp_ref[c:c + step, :] = gp
            back_ref, at = (back0_ref, c) if c < half else (back1_ref, c - half)
            back_ref[k, at:at + step, :] = gp
            hh = h * hb
            pred_acc[c:c + step, :] += sum(hh[:, l:l + LANES] for l in range(0, D, LANES))
            q = q_ref[c:c + step, :]
            qh = jnp.concatenate([h[:, l:l + LANES] * q for l in range(0, D, LANES)], axis=1)
            part = sum(qh[j:j + 8] for j in range(0, step, 8))
            total = part if total is None else total + part
        return total

    def outer(gp_ref):
        post_ref[...] = jnp.dot(xq_ref[...], gp_ref[...], preferred_element_type=F32)

    def spread(i, lo, hi, total):
        s_row = rows_ref[pl.ds(K + base + i, 1), :]
        step, width = 16, 2 * LANES
        lane = lax.broadcasted_iota(jnp.int32, (step, LANES), 1)
        totals = []
        for w in range(0, D, width):
            s, total = s_row[:, w:w + width], None
            for c in range(lo, hi, step):
                g = post_ref[c:c + step, w:w + width]
                r = jnp.sum(jnp.where(lane == base + i, cols_ref[c:c + step, :], 0.0), axis=1, keepdims=True)
                t = g * weight_ref[c:c + step, w:w + width]
                rt = t * r
                part = sum(rt[j:j + 8] for j in range(0, step, 8))
                total = part if total is None else total + part
                st = t * s
                fold = sum(st[:, l:l + LANES] for l in range(0, width, LANES))
                gr_ref[c:c + step, :] += jnp.where(lane == base + i, jnp.sum(fold, axis=1, keepdims=True), 0.0)
                grads_ref[c:c + step, w:w + width] += (g * s) * r
            totals.append(total)
        return jnp.concatenate(totals, axis=1)

    def finish(i, total):
        sums_ref[pl.ds(K + base + i, 1), :] = jnp.sum(total, axis=0, keepdims=True)
        sums_ref[pl.ds(2 * K + base + i, 1), :] = post_ref[D:D + 1, :] + post_ref[D + 1:D + 2, :]

    def member(i, k, now, other, nxt):
        total = middle(i, k, z_refs[now], gp_refs[now], 0, R, None)
        forward(nxt, z_refs[other])
        outer(gp_refs[other])
        heads_grad_ref[pl.ds(base + i, 1), :] = jnp.sum(total, axis=0, keepdims=True)
        finish(i - 1, spread(i - 1, 0, D, None))

    @pl.when(step_id == 0)
    def _():
        set_up()
        forward(0, z_refs[0])

    for k in range(n):
        i, now, other = step_id * n + k, k % 2, (k + 1) % 2
        member(i, k, now, other, jnp.minimum(i + 1, members - 1))

    @pl.when(step_id == steps - 1)
    def _():
        mid = D // 2
        for lo, hi in ((0, mid), (mid, D + 16)):
            post_ref[lo:hi, :] = jnp.dot(xq_ref[lo:hi, :], gp_refs[1][...], preferred_element_type=F32)
        last = [spread(members - 1, lo, lo + mid, None) for lo in (0, mid)]
        finish(members - 1, last[0] + last[1])
        for side in range(2):
            at = slice(side * half, (side + 1) * half)
            pred_ref[side:side + 1, :] = jnp.sum(pred_acc[at, :].T, axis=0, keepdims=True)
        grads_ref[:, D:] = sums_ref[...].T + gr_ref[...]
        for j in range(D // (2 * own)):
            low = grads_ref[2 * j * own:(2 * j + 1) * own, :]
            high = grads_ref[(2 * j + 1) * own:(2 * j + 2) * own, :]
            keep_ref[j * own:(j + 1) * own, :] = jnp.where(core == 0, low, high)
            sent_ref[j * own:(j + 1) * own, :] = jnp.where(core == 0, high, low).astype(BF16)


def grad_call(x, q, packed, K, own, n=2):
    R, D = x.shape
    half = R // 2
    members = K // 2
    flops = 4 * members * R * D * D
    return pl.pallas_call(
        functools.partial(grad_kernel, own=own),
        grid=(members // n,),
        out_shape=(
            shape((D // 2, D + LANES)), shape((D // 2, D + LANES), BF16), shape((K, D)), shape((2, half)),
            shape((LANES, D)), shape((D, D), BF16), shape((members, half, D), BF16), shape((members, half, D), BF16),
        ),
        in_specs=[VMEM] * 3,
        out_specs=(VMEM,) * 6 + (pl.BlockSpec((n, half, D), lambda i: (i, 0, 0)),) * 2,
        scratch_shapes=[
            pltpu.VMEM((D, LANES), F32), pltpu.VMEM((K, D), F32), pltpu.VMEM((D, D), F32),
            pltpu.VMEM((D + 16, R), BF16), pltpu.VMEM((R, LANES), F32),
            pltpu.VMEM((R, D), F32), pltpu.VMEM((R, D), F32), pltpu.VMEM((R, D), BF16), pltpu.VMEM((R, D), BF16),
            pltpu.VMEM((D + 16, D), F32), pltpu.VMEM((R, LANES), F32), pltpu.VMEM((LANES, D), F32),
            pltpu.VMEM((D, LANES), F32), pltpu.VMEM((D, D + LANES), F32),
        ],
        compiler_params=pltpu.CompilerParams(vmem_limit_bytes=LIMIT),
        cost_estimate=pl.CostEstimate(flops=2 * flops, bytes_accessed=members * R * D * 2, transcendentals=members * R * D),
        name="member_grads",
    )(x, q, packed)


def back_kernel(*refs, start, first, last):
    rows_ref, turned_ref, gp_hbm = refs[:3]
    rest = list(refs[3:])
    acc_in = None if first else rest.pop(0)
    q_ref = rest.pop(0) if last else None
    if last == "own":
        came_ref, pred_ref, pred_came_ref, count_ref = [rest.pop(0) for _ in range(4)]
        out_ref, pred_out_ref, gp_ref, sems = rest
    else:
        came_ref = None
        out_ref, gp_ref, sems = rest
    n, R, D = gp_ref.shape
    K = 2 * gp_hbm.shape[0]
    base = this_core() * gp_hbm.shape[0] + start
    copies = [
        pltpu.make_async_copy(gp_hbm.at[start + k], gp_ref.at[k], sems.at[k]) for k in range(n)]
    for copy in copies:
        copy.start()
    if q_ref is not None:
        q_wide = jnp.broadcast_to(0.5 * q_ref[...], (LANES, R)).T
    if last == "own":
        lane = lax.broadcasted_iota(jnp.int32, (1, R), 1)
        total = pred_ref[0:1, :] + pred_came_ref[...]
        pred_out_ref[...] = jnp.where(lane < count_ref[0], total, 0.0) * (1.0 / K)
    for k in range(0, n, 2):
        left, right = [], []
        for j in (k, k + 1):
            r = rows_ref[pl.ds(base + j, 1), :].astype(BF16)
            s = rows_ref[pl.ds(K + base + j, 1), :].astype(BF16)
            right.append(turned_ref[...] * r)
            copies[j].wait()
            left.append(gp_ref[j] * s)
        value = jnp.dot(jnp.concatenate(left, axis=1), jnp.concatenate(right, axis=0), preferred_element_type=F32)
        if k or not first:
            value = value + (out_ref if k else acc_in)[...]
        if last and k + 2 == n:
            for l in range(0, D, LANES):
                part = value[:, l:l + LANES] * q_wide
                out_ref[:, l:l + LANES] = part if came_ref is None else part + came_ref[:, l:l + LANES]
        else:
            out_ref[...] = value


def back_call(rows, turned, back, start, count, acc=None, q=None, came=None):
    members, R, D = back.shape
    last = None if q is None else "other" if came is None else "own"
    more = [v for v in (acc, q, *(came or ())) if v is not None]
    specs = [VMEM] * len(more)
    if last == "own":
        specs[-1] = SMEM
    return pl.pallas_call(
        functools.partial(back_kernel, start=start, first=acc is None, last=last),
        out_shape=(shape((R, D)), shape((1, R))) if last == "own" else shape((R, D)),
        in_specs=[VMEM, VMEM, ANY] + specs,
        out_specs=(VMEM, VMEM) if last == "own" else VMEM,
        scratch_shapes=[pltpu.VMEM((count, R, D), BF16), pltpu.SemaphoreType.DMA((count,))],
        compiler_params=pltpu.CompilerParams(vmem_limit_bytes=LIMIT),
        cost_estimate=pl.CostEstimate(flops=2 * count * R * D * D, bytes_accessed=count * R * D * 2, transcendentals=0),
        name="input_grads",
    )(rows, turned, back, *more)


def direction(weight, first_old, second_old, gradient):
    first_new = beta_one * first_old + (1.0 - beta_one) * gradient
    second_new = beta_two * second_old + (1.0 - beta_two) * gradient * gradient
    fix_one = 1.0 - beta_one**STEP
    fix_two = 1.0 - beta_two**STEP
    update = (
        first_new / fix_one / (jnp.sqrt(second_new / fix_two) + epsilon) + weight_decay * weight
    )
    return (first_new, second_new, update)


def lane_sums(value):
    total = jnp.sum(value, axis=0, keepdims=True)
    width = total.shape[1]
    if width < LANES:
        return jnp.concatenate([total, jnp.zeros((1, LANES - width), F32)], axis=1)
    return sum(total[:, l:l + LANES] for l in range(0, width, LANES))


def direction_kernel(low, size, *refs):
    wide_ref = refs[0]
    count = size - 1
    came = refs[1:1 + count]
    (m_ref, m1_ref, m2_ref, a_ref, a1_ref, a2_ref, h_ref, h1_ref, h2_ref,
     m1_out, m2_out, mu_out, a1_out, a2_out, au_out, h1_out, h2_out, hu_out, sums_out) = refs[1 + count:]
    own, D = m_ref.shape
    K = a_ref.shape[2]
    n_heads = h_ref.shape[0]
    place = lax.rem(lax.axis_index("dp") // low, size)
    grad = wide_ref[:own, :]
    for v in range(1, size):
        grad = jnp.where(place == v, wide_ref[v * own:(v + 1) * own, :], grad)
    heads = wide_ref[size * own:size * own + n_heads, :D]
    for c in came:
        grad = grad + c[:own, :].astype(F32)
        heads = heads + c[own:own + n_heads, :D].astype(F32)
    weight_rows, update_rows = [], []
    first, second, update = direction(m_ref[...], m1_ref[...], m2_ref[...], grad[:, :D])
    m1_out[...], m2_out[...], mu_out[...] = first, second, update
    weight_rows.append(lane_sums(m_ref[...] * m_ref[...]))
    update_rows.append(lane_sums(update * update))
    for k in range(3):
        first, second, update = direction(a_ref[k], a1_ref[k], a2_ref[k], grad[:, D + k * K:D + (k + 1) * K])
        a1_out[k], a2_out[k], au_out[k] = first, second, update
        weight_rows.append(lane_sums(a_ref[k] * a_ref[k]))
        update_rows.append(lane_sums(update * update))
    first, second, update = direction(h_ref[...], h1_ref[...], h2_ref[...], heads)
    h1_out[...], h2_out[...], hu_out[...] = first, second, update
    share = 1.0 / lax.axis_size("dp")
    weight_rows.append(lane_sums(h_ref[...] * h_ref[...]) * share)
    update_rows.append(lane_sums(update * update) * share)
    sums_out[...] = jnp.concatenate(weight_rows + update_rows + [jnp.zeros((6, LANES), F32)], axis=0)


def direction_call(wide, came, low, states):
    m, a, h = states[0], states[3], states[6]
    outs = [shape(v.shape) for v in (m, m, m, a, a, a, h, h, h)] + [shape((16, LANES))]
    return pl.pallas_call(
        functools.partial(direction_kernel, low, len(came) + 1),
        out_shape=tuple(outs),
        in_specs=[VMEM] * (1 + len(came) + 9),
        out_specs=tuple([VMEM] * 10),
        compiler_params=SMALL,
        name="directions",
    )(wide, *came, *states)


def update_kernel(count, *refs):
    sums_refs = refs[:count]
    m_ref, a_ref, h_ref, mu_ref, au_ref, hu_ref, m_out, a_out, h_out, norms_out = refs[count:]
    total = sums_refs[0][...]
    for ref in sums_refs[1:]:
        total = total + ref[...]
    norms = jnp.sqrt(jnp.sum(total, axis=1, keepdims=True))
    weight_norm, update_norm = norms[0:5], norms[5:10]
    rate = learn_rate * (weight_norm / update_norm)
    m_out[...] = m_ref[...] - rate[0:1] * mu_ref[...]
    for k in range(3):
        a_out[k] = a_ref[k] - rate[1 + k:2 + k] * au_ref[k]
    h_out[...] = h_ref[...] - rate[4:5] * hu_ref[...]
    row = jnp.sqrt(jnp.sum(total.T, axis=0, keepdims=True))
    norms_out[...] = jnp.concatenate([row[:, 0:5], row[:, 5:10]], axis=0)


def update_call(sums, m, a, h, mu, au, hu):
    return pl.pallas_call(
        functools.partial(update_kernel, len(sums)),
        out_shape=(shape(m.shape), shape(a.shape), shape(h.shape), shape((2, 5))),
        in_specs=[VMEM] * (len(sums) + 6),
        out_specs=(VMEM,) * 4,
        compiler_params=SMALL,
        name="updates",
    )(*sums, m, a, h, mu, au, hu)


def bit_groups(n_dp, n_member):
    def split(low, count):
        bits = count.bit_length() - 1
        groups = []
        while bits > 0:
            take = 2 if bits >= 2 else 1
            bits -= take
            groups.append((low << bits, 1 << take))
        return groups

    return split(n_member, n_dp), split(2, n_member // 2) + [(1, 2)]


def swap(value, total, mask):
    return lax.ppermute(value, AXES, [(i, i ^ mask) for i in range(total)])


def gather_groups(value, groups, total, index, objects, counts, cot, members):
    value, objects, cot = lax.optimization_barrier((value, objects, cot))
    for axis, (low, size) in enumerate(groups):
        place = (index // low) % size
        held = [value] + [swap(value, total, low * m) for m in reversed(range(1, size))][::-1]
        if axis == 0:
            x_other = swap(objects, total, 1)
            held, x_other, objects = lax.optimization_barrier((held, x_other, objects))
        elif axis == 1:
            lane = lax.broadcasted_iota(jnp.int32, cot.shape, 1)
            q = jnp.where(lane < counts[0], cot, 0.0) * (1.0 / members)
            x = jnp.concatenate([objects, x_other], axis=0)
            held, x, q = lax.optimization_barrier((held, x, q))
        elif axis == len(groups) - 1:
            q_other = swap(q, total, 1)
            held, q_other = lax.optimization_barrier((held, q_other))
            q = jnp.concatenate([q, q_other], axis=1)
        value = jnp.stack([lax.select_n(place ^ p, *held) for p in range(size)], axis=axis)
    return value, x, q


def beside(sends, work, *inputs):
    values, inputs = lax.optimization_barrier(([v for v, _, _ in sends], inputs))
    came = [swap(v, total, mask) for v, (_, total, mask) in reversed(list(zip(values, sends)))][::-1]
    done = work(*inputs)
    return lax.optimization_barrier((came, done))


def shards(n_dp, n_member, objects, counts, cotangent, matrix, matrix_first, matrix_second,
           adapters, adapter_first, adapter_second, head_weights, head_first, head_second):
    R, D = objects.shape
    K = adapters.shape[1]
    own, own_heads = matrix.shape[0], head_weights.shape[0]
    total = n_dp * n_member
    index = lax.axis_index("dp") * n_member + lax.axis_index("member")
    dp_groups, member_groups = bit_groups(n_dp, n_member)
    chip_groups = member_groups[:-1]
    turned = [v.transpose(0, 2, 1) for v in (adapters, adapter_first, adapter_second)]

    packed = pack_call(matrix, turned[0], head_weights)
    full, x_both, q_both = gather_groups(
        packed, dp_groups + member_groups, total, index, objects, counts, cotangent.reshape(1, R), K)
    full = full.reshape(D, -1)
    q_own, q_other = q_both[:, :R], q_both[:, R:]
    keep, sent, head_grads, preds, rows, wide_turned, back_own, back_other = grad_call(x_both, q_both, full, K, own)

    chips = [size for _, size in chip_groups]
    head_grads = head_grads.reshape(chips + [2, own_heads, D])
    core = index % 2
    axis = len(chips)
    members = K // 2

    def arrange(main, heads):
        main = main.reshape([n_dp] + chips + [own, D + LANES])
        main = jnp.moveaxis(main, 0, len(chips)).reshape(chips + [n_dp * own, D + LANES])
        return jnp.concatenate([main, jnp.pad(heads, [(0, 0)] * (len(chips) + 1) + [(0, LANES)])], axis=len(chips))

    def backward(start, count, **more):
        def work(rows, wide_turned, back, *acc):
            return back_call(rows, wide_turned, back, start, count, *acc, **more)
        return work

    weights = (rows, wide_turned, back_other)
    other_heads = lax.dynamic_index_in_dim(head_grads, 1 - core, axis, keepdims=False)
    own_heads_grad = lax.dynamic_index_in_dim(head_grads, core, axis, keepdims=False)
    (came, pred_came), acc = beside(
        [(arrange(sent, other_heads.astype(BF16)), total, 1), (preds[1:2], total, 1)], backward(0, 2), *weights)
    wide = arrange(keep, own_heads_grad) + came.astype(F32)
    for axis in reversed(range(len(chips))):
        low, size = chip_groups[axis]
        place = (index // low) % size
        part = [lax.dynamic_index_in_dim(wide, place ^ m, axis, keepdims=False) for m in range(size)]
        sends = [(part[m].astype(BF16), total, low * m) for m in range(1, size)]
        if axis == len(chips) - 1:
            came, acc = beside(sends, backward(2, 8), *weights, acc)
        else:
            came = [swap(*send) for send in sends]
        wide = part[0]
        for c in came:
            wide = wide + c.astype(F32)
    for axis in reversed(range(len(dp_groups))):
        low, size = dp_groups[axis]
        place = (index // low) % size
        outer_count = (wide.shape[0] - own_heads) // (own * size)
        main = wide[:-own_heads].reshape(outer_count, size * own, D + LANES)
        heads = wide[-own_heads:]

        def chunk(v):
            at = lax.dynamic_slice_in_dim(main, v * own, own, 1)
            return jnp.concatenate([at.reshape(-1, D + LANES), heads], axis=0)

        sends = [(chunk(place ^ m).astype(BF16), total, low * m) for m in range(1, size)]
        if axis == len(dp_groups) - 1:
            last, acc = beside(sends, backward(10, 6, q=q_other), *weights, acc)
        else:
            last = [swap(*send) for send in sends]
        if axis:
            wide = chunk(place)
            for c in last:
                wide = wide + c.astype(F32)
    ig_came = swap(acc, total, 1)

    states = [matrix, matrix_first, matrix_second, *turned, head_weights, head_first, head_second]
    (m_first, m_second, m_update, a_first, a_second, a_update, h_first, h_second, h_update, sums) = direction_call(
        wide, last, dp_groups[0][0] // n_member, states)

    rounds = [(1, 2)] + chip_groups[::-1] + dp_groups[::-1]
    plan = {0: backward(0, 2), 1: backward(2, 6), len(rounds) - 1: backward(8, 8, q=q_own, came=(ig_came, preds, pred_came, counts))}
    pending, acc = [sums], ()
    for step, (low, size) in enumerate(rounds):
        sums = pending[0]
        for p in pending[1:]:
            sums = sums + p
        sends = [(sums, total, low * m) for m in range(1, size)]
        if step in plan:
            came, acc = beside(sends, plan[step], rows, wide_turned, back_own, *acc)
            acc = (acc,)
        else:
            came = [swap(*send) for send in sends]
        pending = [sums] + list(came)
    input_grad, predictions = acc[0]
    new_matrix, new_adapters, new_heads, norm_pairs = update_call(
        pending, matrix, turned[0], head_weights, m_update, a_update, h_update)

    def back_turn(v):
        return v.transpose(0, 2, 1)

    return (predictions.reshape(R), input_grad, new_matrix, m_first, m_second, back_turn(new_adapters),
            back_turn(a_first), back_turn(a_second), new_heads, h_first, h_second, norm_pairs.T)


def solution(mesh):
    n_dp, n_member = mesh.shape["dp"], mesh.shape["member"]
    rows, cols = P(AXES, None), P(None, None, AXES)
    heads = P("member", None)
    return jax.shard_map(
        functools.partial(shards, n_dp, n_member),
        mesh=mesh,
        in_specs=(rows, P(AXES), P(AXES), rows, rows, rows, cols, cols, cols, heads, heads, heads),
        out_specs=(P(AXES), rows, rows, rows, rows, cols, cols, cols, heads, heads, heads, P()),
        check_vma=False,
    )
```

```python
import functools

import jax
import jax.numpy as jnp
from jax import lax
from jax.experimental import pallas as pl
from jax.experimental.pallas import tpu as pltpu
from jax.sharding import PartitionSpec as P

LANES = 128
F32, BF16 = jnp.float32, jnp.bfloat16
STEP = 10
beta_one = 0.5
beta_two = 0.5
epsilon = 1e-06
weight_decay = 0.01
learn_rate = 0.25
AXES = ("dp", "member")
VMEM = pl.BlockSpec(memory_space=pltpu.VMEM)
SMEM = pl.BlockSpec(memory_space=pltpu.SMEM)
ANY = pl.BlockSpec(memory_space=pl.ANY)
LIMIT = 48 * 1024 * 1024
SMALL = pltpu.CompilerParams(vmem_limit_bytes=8 * 1024 * 1024)


def shape(dims, dtype=F32):
    return jax.ShapeDtypeStruct(dims, dtype)


def this_core():
    return lax.rem(lax.axis_index("member"), 2)


def pack_kernel(matrix_ref, adapters_ref, heads_ref, packed_ref):
    own, D = matrix_ref.shape
    K = adapters_ref.shape[2]
    packed_ref[:, :D] = matrix_ref[...].astype(BF16)
    parts = [adapters_ref[k] for k in range(3)] + [jnp.zeros((own, LANES - 3 * K), F32)]
    packed_ref[:, D:D + LANES] = jnp.concatenate(parts, axis=1).astype(BF16)
    L = packed_ref.shape[1] - D - LANES
    rows = []
    for t in range(own):
        h, c = divmod(t * L, D)
        rows.append(heads_ref[h:h + 1, c:c + L])
    packed_ref[:, D + LANES:] = jnp.concatenate(rows, axis=0).astype(BF16)


def pack_call(matrix, adapters_t, heads):
    own, D = matrix.shape
    L = heads.shape[0] * D // own
    return pl.pallas_call(
        pack_kernel,
        out_shape=shape((own, D + LANES + L), BF16),
        in_specs=[VMEM] * 3,
        out_specs=VMEM,
        name="pack_weights",
    )(matrix, adapters_t, heads)


def grad_kernel(
    x_ref, rows_q_ref, packed_ref,
    keep_ref, sent_ref, heads_grad_ref, pred_ref, rows_ref, turned_ref, back0_ref, back1_ref,
    cols_ref, heads_ref, weight_ref, xq_ref, q_ref, z0_ref, z1_ref, gp0_ref, gp1_ref,
    post_ref, pred_acc, sums_ref, gr_ref, grads_ref, *, own,
):
    R, D = x_ref.shape
    half = R // 2
    K = heads_grad_ref.shape[0]
    members = K // 2
    n = back0_ref.shape[0]
    step_id, steps = pl.program_id(0), pl.num_programs(0)
    core = this_core()
    base = core * members
    z_refs, gp_refs = (z0_ref, z1_ref), (gp0_ref, gp1_ref)

    def set_up():
        weight_ref[...] = packed_ref[:, :D].astype(F32)
        cols = packed_ref[:, D:D + LANES].astype(F32)
        cols_ref[...] = cols
        rows_ref[...] = cols.T
        turned_ref[...] = packed_ref[:, :D].T
        L = packed_ref.shape[1] - D - LANES
        per_head = D // L
        for c in range(0, L, LANES):
            gr_ref[:K * per_head, :] = packed_ref[:K * per_head, D + LANES + c:D + 2 * LANES + c].astype(F32)
            for k in range(per_head):
                heads_ref[:, k * L + c:k * L + c + LANES] = gr_ref[pl.ds(k, K, stride=per_head), :]
        for ref in (pred_acc, gr_ref, sums_ref, grads_ref, gp1_ref, heads_grad_ref):
            ref[...] = jnp.zeros_like(ref)
        q_row = rows_q_ref[...]
        q_ref[...] = jnp.broadcast_to(q_row, (LANES, R)).T
        half_q = 0.5 * q_row
        q_hi = half_q.astype(BF16)
        q_lo = (half_q - q_hi.astype(F32)).astype(BF16)
        xq_ref[:D, :] = (x_ref[...].T.astype(F32) * half_q).astype(BF16)
        sub = lax.broadcasted_iota(jnp.int32, (16, R), 0)
        extra = jnp.where(sub == 0, q_hi.astype(F32), jnp.where(sub == 1, q_lo.astype(F32), 0.0))
        xq_ref[D:, :] = extra.astype(BF16)

    def forward(i, z_ref):
        r = rows_ref[pl.ds(base + i, 1), :].astype(BF16)
        z_ref[...] = jnp.dot(x_ref[...] * r, packed_ref[:, :D], preferred_element_type=F32)

    def middle(i, k, z_ref, gp_ref, lo, hi, total):
        s = 0.5 * rows_ref[pl.ds(K + base + i, 1), :]
        b = 0.5 * rows_ref[pl.ds(2 * K + base + i, 1), :]
        hb = heads_ref[pl.ds(base + i, 1), :]
        step = 16
        for c in range(lo, hi, step):
            y = z_ref[c:c + step, :] * s + b
            t = jnp.tanh(y)
            a = 1.0 + t
            h = y * a
            d = a + h * (1.0 - t)
            gp = (hb * d).astype(BF16)
            gp_ref[c:c + step, :] = gp
            back_ref, at = (back0_ref, c) if c < half else (back1_ref, c - half)
            back_ref[k, at:at + step, :] = gp
            hh = h * hb
            pred_acc[c:c + step, :] += sum(hh[:, l:l + LANES] for l in range(0, D, LANES))
            q = q_ref[c:c + step, :]
            qh = jnp.concatenate([h[:, l:l + LANES] * q for l in range(0, D, LANES)], axis=1)
            part = sum(qh[j:j + 8] for j in range(0, step, 8))
            total = part if total is None else total + part
        return total

    def outer(gp_ref):
        post_ref[...] = jnp.dot(xq_ref[...], gp_ref[...], preferred_element_type=F32)

    def spread(i, lo, hi, total):
        s_row = rows_ref[pl.ds(K + base + i, 1), :]
        step, width = 16, 2 * LANES
        lane = lax.broadcasted_iota(jnp.int32, (step, LANES), 1)
        totals = []
        for w in range(0, D, width):
            s, total = s_row[:, w:w + width], None
            for c in range(lo, hi, step):
                g = post_ref[c:c + step, w:w + width]
                r = jnp.sum(jnp.where(lane == base + i, cols_ref[c:c + step, :], 0.0), axis=1, keepdims=True)
                t = g * weight_ref[c:c + step, w:w + width]
                rt = t * r
                part = sum(rt[j:j + 8] for j in range(0, step, 8))
                total = part if total is None else total + part
                st = t * s
                fold = sum(st[:, l:l + LANES] for l in range(0, width, LANES))
                gr_ref[c:c + step, :] += jnp.where(lane == base + i, jnp.sum(fold, axis=1, keepdims=True), 0.0)
                grads_ref[c:c + step, w:w + width] += (g * s) * r
            totals.append(total)
        return jnp.concatenate(totals, axis=1)

    def finish(i, total):
        sums_ref[pl.ds(K + base + i, 1), :] = jnp.sum(total, axis=0, keepdims=True)
        sums_ref[pl.ds(2 * K + base + i, 1), :] = post_ref[D:D + 1, :] + post_ref[D + 1:D + 2, :]

    def member(i, k, now, other, nxt):
        total = middle(i, k, z_refs[now], gp_refs[now], 0, R, None)
        forward(nxt, z_refs[other])
        outer(gp_refs[other])
        heads_grad_ref[pl.ds(base + i, 1), :] = jnp.sum(total, axis=0, keepdims=True)
        finish(i - 1, spread(i - 1, 0, D, None))

    @pl.when(step_id == 0)
    def _():
        set_up()
        forward(0, z_refs[0])

    for k in range(n):
        i, now, other = step_id * n + k, k % 2, (k + 1) % 2
        member(i, k, now, other, jnp.minimum(i + 1, members - 1))

    @pl.when(step_id == steps - 1)
    def _():
        outer(gp_refs[1])
        finish(members - 1, spread(members - 1, 0, D, None))
        for side in range(2):
            at = slice(side * half, (side + 1) * half)
            pred_ref[side:side + 1, :] = jnp.sum(pred_acc[at, :].T, axis=0, keepdims=True)
        grads_ref[:, D:] = sums_ref[...].T + gr_ref[...]
        for j in range(D // (2 * own)):
            low = grads_ref[2 * j * own:(2 * j + 1) * own, :]
            high = grads_ref[(2 * j + 1) * own:(2 * j + 2) * own, :]
            keep_ref[j * own:(j + 1) * own, :] = jnp.where(core == 0, low, high)
            sent_ref[j * own:(j + 1) * own, :] = jnp.where(core == 0, high, low).astype(BF16)


def grad_call(x, q, packed, K, own, n=2):
    R, D = x.shape
    half = R // 2
    members = K // 2
    flops = 4 * members * R * D * D
    return pl.pallas_call(
        functools.partial(grad_kernel, own=own),
        grid=(members // n,),
        out_shape=(
            shape((D // 2, D + LANES)), shape((D // 2, D + LANES), BF16), shape((K, D)), shape((2, half)),
            shape((LANES, D)), shape((D, D), BF16), shape((members, half, D), BF16), shape((members, half, D), BF16),
        ),
        in_specs=[VMEM] * 3,
        out_specs=(VMEM,) * 6 + (pl.BlockSpec((n, half, D), lambda i: (i, 0, 0)),) * 2,
        scratch_shapes=[
            pltpu.VMEM((D, LANES), F32), pltpu.VMEM((K, D), F32), pltpu.VMEM((D, D), F32),
            pltpu.VMEM((D + 16, R), BF16), pltpu.VMEM((R, LANES), F32),
            pltpu.VMEM((R, D), F32), pltpu.VMEM((R, D), F32), pltpu.VMEM((R, D), BF16), pltpu.VMEM((R, D), BF16),
            pltpu.VMEM((D + 16, D), F32), pltpu.VMEM((R, LANES), F32), pltpu.VMEM((LANES, D), F32),
            pltpu.VMEM((D, LANES), F32), pltpu.VMEM((D, D + LANES), F32),
        ],
        compiler_params=pltpu.CompilerParams(vmem_limit_bytes=LIMIT),
        cost_estimate=pl.CostEstimate(flops=2 * flops, bytes_accessed=members * R * D * 2, transcendentals=members * R * D),
        name="member_grads",
    )(x, q, packed)


def back_kernel(*refs, start, first, last):
    rows_ref, turned_ref, gp_hbm = refs[:3]
    rest = list(refs[3:])
    acc_in = None if first else rest.pop(0)
    q_ref = rest.pop(0) if last else None
    if last == "own":
        came_ref, pred_ref, pred_came_ref, count_ref = [rest.pop(0) for _ in range(4)]
        out_ref, pred_out_ref, gp_ref, sems = rest
    else:
        came_ref = None
        out_ref, gp_ref, sems = rest
    n, R, D = gp_ref.shape
    K = 2 * gp_hbm.shape[0]
    base = this_core() * gp_hbm.shape[0] + start
    copies = [
        pltpu.make_async_copy(gp_hbm.at[start + k], gp_ref.at[k], sems.at[k]) for k in range(n)]
    for copy in copies:
        copy.start()
    if q_ref is not None:
        q_wide = jnp.broadcast_to(0.5 * q_ref[...], (LANES, R)).T
    if last == "own":
        lane = lax.broadcasted_iota(jnp.int32, (1, R), 1)
        total = pred_ref[0:1, :] + pred_came_ref[...]
        pred_out_ref[...] = jnp.where(lane < count_ref[0], total, 0.0) * (1.0 / K)
    for k in range(0, n, 2):
        left, right = [], []
        for j in (k, k + 1):
            r = rows_ref[pl.ds(base + j, 1), :].astype(BF16)
            s = rows_ref[pl.ds(K + base + j, 1), :].astype(BF16)
            right.append(turned_ref[...] * r)
            copies[j].wait()
            left.append(gp_ref[j] * s)
        value = jnp.dot(jnp.concatenate(left, axis=1), jnp.concatenate(right, axis=0), preferred_element_type=F32)
        if k or not first:
            value = value + (out_ref if k else acc_in)[...]
        if last and k + 2 == n:
            for l in range(0, D, LANES):
                part = value[:, l:l + LANES] * q_wide
                out_ref[:, l:l + LANES] = part if came_ref is None else part + came_ref[:, l:l + LANES]
        else:
            out_ref[...] = value


def back_call(rows, turned, back, start, count, acc=None, q=None, came=None):
    members, R, D = back.shape
    last = None if q is None else "other" if came is None else "own"
    more = [v for v in (acc, q, *(came or ())) if v is not None]
    specs = [VMEM] * len(more)
    if last == "own":
        specs[-1] = SMEM
    return pl.pallas_call(
        functools.partial(back_kernel, start=start, first=acc is None, last=last),
        out_shape=(shape((R, D)), shape((1, R))) if last == "own" else shape((R, D)),
        in_specs=[VMEM, VMEM, ANY] + specs,
        out_specs=(VMEM, VMEM) if last == "own" else VMEM,
        scratch_shapes=[pltpu.VMEM((count, R, D), BF16), pltpu.SemaphoreType.DMA((count,))],
        compiler_params=pltpu.CompilerParams(vmem_limit_bytes=LIMIT),
        cost_estimate=pl.CostEstimate(flops=2 * count * R * D * D, bytes_accessed=count * R * D * 2, transcendentals=0),
        name="input_grads",
    )(rows, turned, back, *more)


def direction(weight, first_old, second_old, gradient):
    first_new = beta_one * first_old + (1.0 - beta_one) * gradient
    second_new = beta_two * second_old + (1.0 - beta_two) * gradient * gradient
    fix_one = 1.0 - beta_one**STEP
    fix_two = 1.0 - beta_two**STEP
    update = (
        first_new / fix_one / (jnp.sqrt(second_new / fix_two) + epsilon) + weight_decay * weight
    )
    return (first_new, second_new, update)


def lane_sums(value):
    total = jnp.sum(value, axis=0, keepdims=True)
    width = total.shape[1]
    if width < LANES:
        return jnp.concatenate([total, jnp.zeros((1, LANES - width), F32)], axis=1)
    return sum(total[:, l:l + LANES] for l in range(0, width, LANES))


def direction_kernel(low, size, *refs):
    wide_ref = refs[0]
    count = size - 1
    came = refs[1:1 + count]
    (m_ref, m1_ref, m2_ref, a_ref, a1_ref, a2_ref, h_ref, h1_ref, h2_ref,
     m1_out, m2_out, mu_out, a1_out, a2_out, au_out, h1_out, h2_out, hu_out, sums_out) = refs[1 + count:]
    own, D = m_ref.shape
    K = a_ref.shape[2]
    n_heads = h_ref.shape[0]
    place = lax.rem(lax.axis_index("dp") // low, size)
    grad = wide_ref[:own, :]
    for v in range(1, size):
        grad = jnp.where(place == v, wide_ref[v * own:(v + 1) * own, :], grad)
    heads = wide_ref[size * own:size * own + n_heads, :D]
    for c in came:
        grad = grad + c[:own, :].astype(F32)
        heads = heads + c[own:own + n_heads, :D].astype(F32)
    weight_rows, update_rows = [], []
    first, second, update = direction(m_ref[...], m1_ref[...], m2_ref[...], grad[:, :D])
    m1_out[...], m2_out[...], mu_out[...] = first, second, update
    weight_rows.append(lane_sums(m_ref[...] * m_ref[...]))
    update_rows.append(lane_sums(update * update))
    for k in range(3):
        first, second, update = direction(a_ref[k], a1_ref[k], a2_ref[k], grad[:, D + k * K:D + (k + 1) * K])
        a1_out[k], a2_out[k], au_out[k] = first, second, update
        weight_rows.append(lane_sums(a_ref[k] * a_ref[k]))
        update_rows.append(lane_sums(update * update))
    first, second, update = direction(h_ref[...], h1_ref[...], h2_ref[...], heads)
    h1_out[...], h2_out[...], hu_out[...] = first, second, update
    share = 1.0 / lax.axis_size("dp")
    weight_rows.append(lane_sums(h_ref[...] * h_ref[...]) * share)
    update_rows.append(lane_sums(update * update) * share)
    sums_out[...] = jnp.concatenate(weight_rows + update_rows + [jnp.zeros((6, LANES), F32)], axis=0)


def direction_call(wide, came, low, states):
    m, a, h = states[0], states[3], states[6]
    outs = [shape(v.shape) for v in (m, m, m, a, a, a, h, h, h)] + [shape((16, LANES))]
    return pl.pallas_call(
        functools.partial(direction_kernel, low, len(came) + 1),
        out_shape=tuple(outs),
        in_specs=[VMEM] * (1 + len(came) + 9),
        out_specs=tuple([VMEM] * 10),
        compiler_params=SMALL,
        name="directions",
    )(wide, *came, *states)


def update_kernel(count, *refs):
    sums_refs = refs[:count]
    m_ref, a_ref, h_ref, mu_ref, au_ref, hu_ref, m_out, a_out, h_out, norms_out = refs[count:]
    total = sums_refs[0][...]
    for ref in sums_refs[1:]:
        total = total + ref[...]
    norms = jnp.sqrt(jnp.sum(total, axis=1, keepdims=True))
    weight_norm, update_norm = norms[0:5], norms[5:10]
    rate = learn_rate * (weight_norm / update_norm)
    m_out[...] = m_ref[...] - rate[0:1] * mu_ref[...]
    for k in range(3):
        a_out[k] = a_ref[k] - rate[1 + k:2 + k] * au_ref[k]
    h_out[...] = h_ref[...] - rate[4:5] * hu_ref[...]
    row = jnp.sqrt(jnp.sum(total.T, axis=0, keepdims=True))
    norms_out[...] = jnp.concatenate([row[:, 0:5], row[:, 5:10]], axis=0)


def update_call(sums, m, a, h, mu, au, hu):
    return pl.pallas_call(
        functools.partial(update_kernel, len(sums)),
        out_shape=(shape(m.shape), shape(a.shape), shape(h.shape), shape((2, 5))),
        in_specs=[VMEM] * (len(sums) + 6),
        out_specs=(VMEM,) * 4,
        compiler_params=SMALL,
        name="updates",
    )(*sums, m, a, h, mu, au, hu)


def bit_groups(n_dp, n_member):
    def split(low, count):
        bits = count.bit_length() - 1
        groups = []
        while bits > 0:
            take = 2 if bits >= 2 else 1
            bits -= take
            groups.append((low << bits, 1 << take))
        return groups

    return split(n_member, n_dp), split(2, n_member // 2) + [(1, 2)]


def swap(value, total, mask):
    return lax.ppermute(value, AXES, [(i, i ^ mask) for i in range(total)])


def gather_groups(value, groups, total, index, objects, counts, cot, members):
    value, objects, cot = lax.optimization_barrier((value, objects, cot))
    for axis, (low, size) in enumerate(groups):
        place = (index // low) % size
        held = [value] + [swap(value, total, low * m) for m in reversed(range(1, size))][::-1]
        if axis == 0:
            x_other = swap(objects, total, 1)
            held, x_other, objects = lax.optimization_barrier((held, x_other, objects))
        elif axis == 1:
            lane = lax.broadcasted_iota(jnp.int32, cot.shape, 1)
            q = jnp.where(lane < counts[0], cot, 0.0) * (1.0 / members)
            x = jnp.concatenate([objects, x_other], axis=0)
            held, x, q = lax.optimization_barrier((held, x, q))
        elif axis == len(groups) - 1:
            q_other = swap(q, total, 1)
            held, q_other = lax.optimization_barrier((held, q_other))
            q = jnp.concatenate([q, q_other], axis=1)
        value = jnp.stack([lax.select_n(place ^ p, *held) for p in range(size)], axis=axis)
    return value, x, q


def beside(sends, work, *inputs):
    values, inputs = lax.optimization_barrier(([v for v, _, _ in sends], inputs))
    came = [swap(v, total, mask) for v, (_, total, mask) in reversed(list(zip(values, sends)))][::-1]
    done = work(*inputs)
    return lax.optimization_barrier((came, done))


def shards(n_dp, n_member, objects, counts, cotangent, matrix, matrix_first, matrix_second,
           adapters, adapter_first, adapter_second, head_weights, head_first, head_second):
    R, D = objects.shape
    K = adapters.shape[1]
    own, own_heads = matrix.shape[0], head_weights.shape[0]
    total = n_dp * n_member
    index = lax.axis_index("dp") * n_member + lax.axis_index("member")
    dp_groups, member_groups = bit_groups(n_dp, n_member)
    chip_groups = member_groups[:-1]
    turned = [v.transpose(0, 2, 1) for v in (adapters, adapter_first, adapter_second)]

    packed = pack_call(matrix, turned[0], head_weights)
    full, x_both, q_both = gather_groups(
        packed, dp_groups + member_groups, total, index, objects, counts, cotangent.reshape(1, R), K)
    full = full.reshape(D, -1)
    q_own, q_other = q_both[:, :R], q_both[:, R:]
    keep, sent, head_grads, preds, rows, wide_turned, back_own, back_other = grad_call(x_both, q_both, full, K, own)

    chips = [size for _, size in chip_groups]
    head_grads = head_grads.reshape(chips + [2, own_heads, D])
    core = index % 2
    axis = len(chips)
    members = K // 2

    def arrange(main, heads):
        main = main.reshape([n_dp] + chips + [own, D + LANES])
        main = jnp.moveaxis(main, 0, len(chips)).reshape(chips + [n_dp * own, D + LANES])
        return jnp.concatenate([main, jnp.pad(heads, [(0, 0)] * (len(chips) + 1) + [(0, LANES)])], axis=len(chips))

    def backward(start, count, **more):
        def work(rows, wide_turned, back, *acc):
            return back_call(rows, wide_turned, back, start, count, *acc, **more)
        return work

    weights = (rows, wide_turned, back_other)
    other_heads = lax.dynamic_index_in_dim(head_grads, 1 - core, axis, keepdims=False)
    own_heads_grad = lax.dynamic_index_in_dim(head_grads, core, axis, keepdims=False)
    (came,), acc = beside([(arrange(sent, other_heads.astype(BF16)), total, 1)], backward(0, 2), *weights)
    wide = arrange(keep, own_heads_grad) + came.astype(F32)
    for axis in reversed(range(len(chips))):
        low, size = chip_groups[axis]
        place = (index // low) % size
        part = [lax.dynamic_index_in_dim(wide, place ^ m, axis, keepdims=False) for m in range(size)]
        sends = [(part[m].astype(BF16), total, low * m) for m in range(1, size)]
        if axis == len(chips) - 1:
            came, acc = beside(sends + [(preds[1:2], total, 1)], backward(2, 8), *weights, acc)
            *came, pred_came = came
        else:
            came = [swap(*send) for send in sends]
        wide = part[0]
        for c in came:
            wide = wide + c.astype(F32)
    for axis in reversed(range(len(dp_groups))):
        low, size = dp_groups[axis]
        place = (index // low) % size
        outer_count = (wide.shape[0] - own_heads) // (own * size)
        main = wide[:-own_heads].reshape(outer_count, size * own, D + LANES)
        heads = wide[-own_heads:]

        def chunk(v):
            at = lax.dynamic_slice_in_dim(main, v * own, own, 1)
            return jnp.concatenate([at.reshape(-1, D + LANES), heads], axis=0)

        sends = [(chunk(place ^ m).astype(BF16), total, low * m) for m in range(1, size)]
        if axis == len(dp_groups) - 1:
            last, acc = beside(sends, backward(10, 6, q=q_other), *weights, acc)
        else:
            last = [swap(*send) for send in sends]
        if axis:
            wide = chunk(place)
            for c in last:
                wide = wide + c.astype(F32)
    ig_came = swap(acc, total, 1)

    states = [matrix, matrix_first, matrix_second, *turned, head_weights, head_first, head_second]
    (m_first, m_second, m_update, a_first, a_second, a_update, h_first, h_second, h_update, sums) = direction_call(
        wide, last, dp_groups[0][0] // n_member, states)

    rounds = [(1, 2)] + chip_groups[::-1] + dp_groups[::-1]
    plan = {0: backward(0, 2), 1: backward(2, 6), len(rounds) - 1: backward(8, 8, q=q_own, came=(ig_came, preds, pred_came, counts))}
    pending, acc = [sums], ()
    for step, (low, size) in enumerate(rounds):
        sums = pending[0]
        for p in pending[1:]:
            sums = sums + p
        sends = [(sums, total, low * m) for m in range(1, size)]
        if step in plan:
            came, acc = beside(sends, plan[step], rows, wide_turned, back_own, *acc)
            acc = (acc,)
        else:
            came = [swap(*send) for send in sends]
        pending = [sums] + list(came)
    input_grad, predictions = acc[0]
    new_matrix, new_adapters, new_heads, norm_pairs = update_call(
        pending, matrix, turned[0], head_weights, m_update, a_update, h_update)

    def back_turn(v):
        return v.transpose(0, 2, 1)

    return (predictions.reshape(R), input_grad, new_matrix, m_first, m_second, back_turn(new_adapters),
            back_turn(a_first), back_turn(a_second), new_heads, h_first, h_second, norm_pairs.T)


def solution(mesh):
    n_dp, n_member = mesh.shape["dp"], mesh.shape["member"]
    rows, cols = P(AXES, None), P(None, None, AXES)
    heads = P("member", None)
    return jax.shard_map(
        functools.partial(shards, n_dp, n_member),
        mesh=mesh,
        in_specs=(rows, P(AXES), P(AXES), rows, rows, rows, cols, cols, cols, heads, heads, heads),
        out_specs=(P(AXES), rows, rows, rows, rows, cols, cols, cols, heads, heads, heads, P()),
        check_vma=False,
    )
```
